32 devices in a mesh: section: 2 (over core), rep: 4 (over y, x), fsdp: 4 (over z).
Axes of the slice: x: 2, y: 2, z: 4, core: 2. Of those that a mesh axis runs over, the one named last changes fastest.
Arguments:
- layer_input: bfloat16 [2, 2, 1024, 8192], P('section', None, ('rep', 'fsdp')), may hold values from -600 to 600
- value_grad: bfloat16 [2, 2, 1024, 1024], P('section', None, ('rep', 'fsdp')), may hold values from -7 to 7
- value_weight: bfloat16 [2, 8192, 1024], P('section', 'fsdp'), may hold values from -2 to 2
- norm_gain: bfloat16 [2, 8192], P('section', 'fsdp'), may hold values from 0.25 to 1.75
- top_grad: bfloat16 [2, 1024, 8192], P(None, ('rep', 'fsdp')), may hold values from -6 to 6
Outputs:
- input_grad: bfloat16 [2, 2, 1024, 8192], P('section', None, ('rep', 'fsdp'))
- weight_grad: float32 [2, 8192, 1024], P('section', 'fsdp')
- gain_grad: float32 [2, 8192], P('section', 'fsdp')
The draws below stay inside these ranges and needn't reach their ends.
All inputs are finite; a program needn't handle non-finite values.
Results may differ from the reference program's by a relative error of at most 0.0041.
Values may be sent and summed in bfloat16 or wider, within the bound.
No kernel may reach another device: no remote copies, remote signals or barrier semaphores. Data moves between devices by JAX's collectives and lax.ppermute only.
A program may use at most 128 MiB of HBM per device.

```python
import math
import jax
import jax.numpy as jnp
from jax import lax

MODEL_WIDTH = 8192
MICRO = 2
TOK_DEV = 64
VW = 1024
TOKENS = 1024
N_SECTION = 2


def shared_terms(key):
    grad_key = jax.random.fold_in(key, 101)
    sign_key = jax.random.fold_in(key, 102)
    grad_base = jnp.clip(jax.random.normal(grad_key, (N_SECTION, MICRO, TOKENS, VW), jnp.float32), -3.0, 3.0)
    feature_sign = 2.0 * jax.random.randint(sign_key, (N_SECTION, MODEL_WIDTH), 0, 2).astype(jnp.float32) - 1.0
    return (grad_base, feature_sign)


def draw_layer_input(key, part):
    grad_base, feature_sign = shared_terms(key)
    key = jax.random.fold_in(key, 1)
    jitter_key, token_key, row_key, column_key, pair_key = jax.random.split(key, 5)
    array_shape = (N_SECTION, MICRO, TOKENS, MODEL_WIDTH)
    jitter = jnp.clip(jax.random.normal(jitter_key, array_shape, jnp.float32), -3.0, 3.0)
    ramp_slope = 0.6
    token_sign = 2.0 * jax.random.randint(token_key, (N_SECTION, MICRO, TOKENS, 1), 0, 2).astype(jnp.float32) - 1.0
    row_scale = jnp.exp(jax.random.uniform(row_key, (N_SECTION, MICRO, TOKENS, 1), jnp.float32, 0.0, math.log(10.0)))
    feature = jnp.arange(MODEL_WIDTH)
    ramp_term = ramp_slope * (2.0 * feature.astype(jnp.float32) / (MODEL_WIDTH - 1) - 1.0)
    column_scale = jnp.exp(jax.random.uniform(column_key, (N_SECTION, 1, 1, MODEL_WIDTH), jnp.float32, -math.log(2.0), math.log(2.0)) + ramp_term)
    blocks = TOKENS // TOK_DEV
    pairing = jax.random.permutation(pair_key, blocks)
    token_block = jnp.arange(TOKENS) // TOK_DEV
    feature_block = feature * blocks // MODEL_WIDTH
    spike_gain = jnp.where(pairing[token_block][:, None] == feature_block[None, :], 2.0, 1.0)
    tiled_grad = jnp.take(grad_base, feature % VW, axis=3)
    value_entries = row_scale * column_scale * spike_gain * (jitter + token_sign * feature_sign[:, None, None, :] * tiled_grad)
    return value_entries.astype(jnp.bfloat16)


def draw_value_grad(key, part):
    grad_base, feature_sign = shared_terms(key)
    value_entries = 1.5 * grad_base
    return value_entries.astype(jnp.bfloat16)


def draw_value_weight(key, part):
    grad_base, feature_sign = shared_terms(key)
    key = jax.random.fold_in(key, 3)
    weight_shape = (N_SECTION, MODEL_WIDTH, VW)
    random_part = jnp.clip(jax.random.normal(key, weight_shape, jnp.float32), -3.0, 3.0)
    matched = (jnp.arange(MODEL_WIDTH)[:, None] % VW == jnp.arange(VW)[None, :]).astype(jnp.float32)
    value_entries = random_part * MODEL_WIDTH ** (-0.5) + feature_sign[:, :, None] * matched * math.sqrt(VW / MODEL_WIDTH)
    return value_entries.astype(jnp.bfloat16)


def block_levels(own_key, dims, cuts, least, high):
    level, own = 1.0, jax.random.fold_in(own_key, 6)
    for position, blocks in cuts:
        steps = jnp.exp(jax.random.uniform(jax.random.fold_in(own, position), (blocks,), jnp.float32, least / len(cuts), high / len(cuts)))
        level = level * jnp.repeat(steps, dims[position] // blocks).reshape([-1 if axis == position else 1 for axis in range(len(dims))])
    return level


def normal_values(rng, shape, deviation, bound, pieces=(), dtype=jnp.bfloat16):
    result = jax.random.normal(rng, shape, jnp.float32) * deviation
    if len(pieces) > 0:
        result = block_levels(rng, shape, pieces, -0.22, 0.18) * result
    return jnp.clip(result, min=-bound, max=bound).astype(dtype)


def setup_inputs(seed: int = 0) -> dict:
    splits = jax.random.split(jax.random.key(seed), 6)
    return {
        "layer_input": draw_layer_input(jax.random.fold_in(splits[5], 71), 0),
        "value_grad": draw_value_grad(jax.random.fold_in(splits[5], 71), 0),
        "value_weight": draw_value_weight(jax.random.fold_in(splits[5], 71), 0),
        "norm_gain": jnp.clip(1.0 + 0.15 * jax.random.normal(splits[3], (N_SECTION, MODEL_WIDTH), jnp.float32), 0.25, 1.75).astype(jnp.bfloat16),
        "top_grad": normal_values(splits[4], (MICRO, TOKENS, MODEL_WIDTH), 1.0, 6.0, ((1, 16),)),
    }


norm_eps = 1e-05

def section_terms(inputs, grads, weight, gain):
    value_entries = inputs.astype(jnp.float32)
    inverse_scale = jax.lax.rsqrt(lax.optimization_barrier(jnp.mean(value_entries * value_entries, axis=1)) + norm_eps)
    centered_input = value_entries * inverse_scale[:, None]
    gain_float_full = gain.astype(jnp.float32)
    normalized_input = (centered_input * gain_float_full).astype(jnp.bfloat16)
    weight_part = jnp.dot(normalized_input.T, grads, preferred_element_type=jnp.float32)
    normalized_gradient = jnp.dot(grads, weight.T, preferred_element_type=jnp.float32)
    gain_portion = lax.optimization_barrier(jnp.sum(normalized_gradient * centered_input, axis=0))
    centered_gradient = normalized_gradient * gain_float_full
    average_product = lax.optimization_barrier(jnp.sum(centered_gradient * centered_input, axis=1)) / MODEL_WIDTH
    local_piece = (inverse_scale[:, None] * (centered_gradient - centered_input * average_product[:, None])).astype(jnp.bfloat16)
    return (weight_part, gain_portion, local_piece)

def reference(layer_input, value_grad, value_weight, norm_gain, top_grad):
    norm_scale = float(MICRO * TOKENS) ** (-0.5)
    upper_list = []
    lower_list = []
    weight_grads = [None, None]
    gain_grads = [None, None]
    for section_id in (1, 0):
        weight_total = jnp.zeros((MODEL_WIDTH, VW), jnp.float32)
        gain_total = jnp.zeros((MODEL_WIDTH,), jnp.float32)
        for batch_index in range(MICRO):
            weight_part, gain_portion, local_piece = section_terms(layer_input[section_id, batch_index], value_grad[section_id, batch_index], value_weight[section_id], norm_gain[section_id])
            weight_total = weight_total + weight_part
            gain_total = gain_total + gain_portion
            if section_id == 1:
                upper_list.append((top_grad[batch_index].astype(jnp.float32) + local_piece.astype(jnp.float32)).astype(jnp.bfloat16))
            else:
                lower_list.append((upper_list[batch_index].astype(jnp.float32) + local_piece.astype(jnp.float32)).astype(jnp.bfloat16))
        weight_grads[section_id] = weight_total * norm_scale
        gain_grads[section_id] = gain_total * norm_scale
    input_grad = jnp.stack([jnp.stack(lower_list), jnp.stack(upper_list)])
    return (input_grad, jnp.stack(weight_grads), jnp.stack(gain_grads))
```

```python
import jax
import jax.numpy as jnp
from jax import lax
from jax.sharding import PartitionSpec as P

norm_eps = 1e-05
bf16 = jnp.bfloat16
f32 = jnp.float32


def cyclic(value, axis, steps):
    count = lax.axis_size(axis)
    return lax.ppermute(value, axis, [(i, (i + steps) % count) for i in range(count)])


def flipped(value, axis, bit):
    count = lax.axis_size(axis)
    return lax.ppermute(value, axis, [(i, i ^ (1 << bit)) for i in range(count)])


def line_gather(value, axis):
    count = lax.axis_size(axis)
    me = lax.axis_index(axis)
    right, left = [value], [value]
    for k in range(1, count):
        right.append(lax.ppermute(right[-1], axis, [(i, i + 1) for i in range(k - 1, count - 1)]))
        left.append(lax.ppermute(left[-1], axis, [(i, i - 1) for i in range(1, count - k + 1)]))
    return [value] + [jnp.where(me >= j, right[j], left[count - j]) for j in range(1, count)]


def summed_over_rep(part, order):
    me = lax.axis_index("rep")
    for bit in order:
        half = part.shape[0] // 2
        mine = (me >> bit) & 1
        keep = lax.dynamic_slice_in_dim(part, mine * half, half, 0)
        send = lax.dynamic_slice_in_dim(part, (1 - mine) * half, half, 0)
        part = keep + flipped(send.astype(bf16), "rep", bit).astype(f32)
    part = part.astype(bf16)
    for bit in reversed(order):
        mine = ((me >> bit) & 1) == 1
        other = flipped(part, "rep", bit)
        part = jnp.concatenate([jnp.where(mine, other, part), jnp.where(mine, part, other)], axis=0)
    return part


def local(layer_input, value_grad, value_weight, norm_gain, top_grad):
    groups = lax.axis_size("fsdp")
    reps = lax.axis_size("rep")
    bits = reps.bit_length() - 1
    me = lax.axis_index("fsdp")
    _, micro, rows, width = layer_input.shape
    tokens = micro * rows
    shard = width // groups
    total_rows = tokens * reps * groups
    norm_scale = float(total_rows) ** (-0.5)
    chunks = 2
    chunk = shard // chunks

    weight = value_weight[0]
    gain = norm_gain[0].astype(f32)
    x = layer_input[0].reshape(tokens, width).astype(f32)
    grads = value_grad[0].reshape(tokens, -1)

    grad_slots = line_gather(grads, "fsdp")
    grads_all = jnp.concatenate(grad_slots, axis=0)

    scale = lax.rsqrt(jnp.mean(x * x, axis=1, keepdims=True) + norm_eps)
    hat = (x * scale).astype(bf16)

    sums = []
    for c in range(chunks):
        blocks = []
        for j in range(groups):
            start = ((me + j) % groups) * shard + c * chunk
            block = lax.dynamic_slice_in_dim(hat, start, chunk, 1)
            blocks.append(cyclic(block, "fsdp", j) if j else block)
        columns = jnp.concatenate(blocks, axis=0)
        product = lax.dot_general(columns, grads_all, (((0,), (0,)), ((), ())), preferred_element_type=f32)
        orders = [tuple(range(bits)), tuple(reversed(range(bits)))] if bits > 1 else [tuple(range(bits))]
        piece = chunk // len(orders)
        for p, order in enumerate(orders):
            sums.append(summed_over_rep(product[p * piece : (p + 1) * piece], order))
    raw = jnp.concatenate(sums, axis=0).astype(f32)
    weight_grad = raw * (gain * norm_scale)[:, None]
    gain_grad = jnp.sum(raw * weight.astype(f32), axis=1) * norm_scale

    back = lax.dot_general(grads_all, weight, (((1,), (1,)), ((), ())), preferred_element_type=f32)
    back = (back * gain).astype(bf16).reshape(groups, micro, rows, shard)
    results = []
    for m in range(micro):
        dhat = jnp.zeros((rows, width), bf16)
        for j in range(groups):
            block = back[j, m]
            block = cyclic(block, "fsdp", -j) if j else block
            dhat = lax.dynamic_update_slice(dhat, block, (0, ((me + j) % groups) * shard))
        dhat = dhat.astype(f32)
        own = x[m * rows : (m + 1) * rows] * scale[m * rows : (m + 1) * rows]
        mean = jnp.sum(dhat * own, axis=1, keepdims=True) / width
        piece = (scale[m * rows : (m + 1) * rows] * (dhat - own * mean)).astype(bf16).astype(f32)
        upper = (top_grad[m].astype(f32) + piece).astype(bf16)
        passed = lax.ppermute(upper, "section", [(1, 0)])
        lower = (passed.astype(f32) + piece).astype(bf16)
        results.append(jnp.where(lax.axis_index("section") == 1, upper, lower))
    return (jnp.stack(results)[None], weight_grad[None], gain_grad[None])


def solution(mesh):
    return jax.shard_map(
        local,
        mesh=mesh,
        in_specs=(
            P("section", None, ("rep", "fsdp"), None),
            P("section", None, ("rep", "fsdp"), None),
            P("section", "fsdp", None),
            P("section", "fsdp"),
            P(None, ("rep", "fsdp"), None),
        ),
        out_specs=(
            P("section", None, ("rep", "fsdp"), None),
            P("section", "fsdp", None),
            P("section", "fsdp"),
        ),
        check_vma=False,
    )
```

```python
import jax
import jax.numpy as jnp
from jax import lax
from jax.experimental import pallas as pl
from jax.experimental.pallas import tpu as pltpu
from jax.sharding import PartitionSpec as P

norm_eps = 1e-05
bf16 = jnp.bfloat16
f32 = jnp.float32
MIB = 1 << 20
SMEM_ARG = pl.BlockSpec(memory_space=pltpu.SMEM)
VMEM_ARG = pl.BlockSpec(memory_space=pltpu.VMEM)


def cyclic(value, axis, steps):
    count = lax.axis_size(axis)
    return lax.ppermute(value, axis, [(i, (i + steps) % count) for i in range(count)])


def flipped(value, axis, bit):
    count = lax.axis_size(axis)
    return lax.ppermute(value, axis, [(i, i ^ (1 << bit)) for i in range(count)])


def after(value, *others):
    return lax.optimization_barrier((value, *others))[0]


def params(mib):
    return pltpu.CompilerParams(vmem_limit_bytes=mib * MIB)


def cost(flops, bytes_accessed):
    return pl.CostEstimate(flops=int(flops), bytes_accessed=int(bytes_accessed), transcendentals=0)


def line_gather(value, axis):
    count = lax.axis_size(axis)
    me = lax.axis_index(axis)
    right, left = [value], [value]
    for k in range(1, count):
        right.append(lax.ppermute(right[-1], axis, [(i, i + 1) for i in range(k - 1, count - 1)]))
        left.append(lax.ppermute(left[-1], axis, [(i, i - 1) for i in range(1, count - k + 1)]))
    return [value] + [jnp.where(me >= j, right[j], left[count - j]) for j in range(1, count)]


def mask_of(pos, order):
    bits = len(order)
    return sum(((pos >> (bits - 1 - i)) & 1) << order[i] for i in range(bits))


def scaled_blocks(x, me, groups, chunks):
    tokens, width = x.shape
    chunk = width // groups // chunks
    step = 16

    def kernel(me_ref, x_ref, *out_refs):
        start = me_ref[0]

        @pl.loop(0, tokens, step=step)
        def _(row):
            rows = pl.ds(pl.multiple_of(row, step), step)
            total = jnp.zeros((step, 128), f32)
            span = 1024 if width % 1024 == 0 else 128
            for c in range(0, width, span):
                v = x_ref[rows, c : c + span].astype(f32)
                v = v * v
                for k in range(0, span, 128):
                    total = total + v[:, k : k + 128]
            scale = lax.rsqrt(jnp.sum(total, axis=1, keepdims=True) / width + norm_eps)
            for c in range(chunks):
                for j in range(groups):
                    at = lax.rem(start + j, groups) * (chunk * chunks) + c * chunk
                    v = x_ref[rows, pl.ds(pl.multiple_of(at, chunk), chunk)].astype(f32)
                    out_refs[c * groups + j][rows, :] = (v * scale).astype(bf16)

    outs = pl.pallas_call(
        kernel,
        out_shape=[jax.ShapeDtypeStruct((tokens, chunk), bf16)] * (chunks * groups),
        in_specs=[SMEM_ARG, VMEM_ARG],
        out_specs=[VMEM_ARG] * (chunks * groups),
        compiler_params=params(24),
        cost_estimate=cost(6 * x.size, 4 * x.size),
        name="scaled_blocks",
    )(me, x)
    return [list(outs[c * groups : (c + 1) * groups]) for c in range(chunks)]


def weight_product(blocks, slots, rep, reps, orders):
    groups = len(blocks)
    tokens, chunk = blocks[0].shape
    features = slots[0].shape[1]
    part = chunk // len(orders)
    piece = part // reps
    half = part // 2
    tile = min(part, 256)

    def kernel(rep_ref, *refs):
        block_refs, slot_refs = refs[:groups], refs[groups : 2 * groups]
        out_refs, total = refs[2 * groups : -1], refs[-1]
        values = jnp.concatenate([s[...] for s in slot_refs], axis=0)
        for p, order in enumerate(orders):
            for t in range(0, part, tile):
                at = p * part + t
                columns = jnp.concatenate([b[:, at : at + tile] for b in block_refs], axis=0)
                total[t : t + tile, :] = lax.dot_general(
                    columns, values, (((0,), (0,)), ((), ())), preferred_element_type=f32
                )
            for pos in range(reps):
                owner = rep_ref[0] ^ mask_of(pos, order)
                rows = total[pl.ds(pl.multiple_of(owner * piece, piece), piece), :]
                if pos < reps // 2:
                    out_refs[2 * p][pos * piece : (pos + 1) * piece, :] = rows
                else:
                    at = (pos - reps // 2) * piece
                    out_refs[2 * p + 1][at : at + piece, :] = rows.astype(bf16)

    shapes = []
    for _ in orders:
        shapes += [jax.ShapeDtypeStruct((half, features), f32), jax.ShapeDtypeStruct((half, features), bf16)]
    return pl.pallas_call(
        kernel,
        out_shape=shapes,
        in_specs=[SMEM_ARG] + [VMEM_ARG] * (2 * groups),
        out_specs=[VMEM_ARG] * len(shapes),
        scratch_shapes=[pltpu.VMEM((part, features), f32)],
        compiler_params=params(32),
        cost_estimate=cost(2 * groups * tokens * chunk * features, 2 * groups * tokens * (chunk + features) + 3 * chunk * features),
        name="weight_product",
    )(rep, *blocks, *slots)


def returned_blocks(slots, weight, gain, micro):
    groups = len(slots)
    tokens, features = slots[0].shape
    rows = tokens // micro
    shard = weight.shape[0]
    tile = min(shard, 512)

    def kernel(*refs):
        slot_refs, weight_ref, gain_ref = refs[:groups], refs[groups], refs[groups + 1]
        out_refs = refs[groups + 2 :]
        factor = gain_ref[...].astype(f32)
        pair = 2 if groups % 2 == 0 else 1
        for j in range(0, groups, pair):
            values = jnp.concatenate([slot_refs[j + i][...] for i in range(pair)], axis=0)
            back = lax.dot_general(values, weight_ref[...], (((1,), (1,)), ((), ())), preferred_element_type=f32)
            back = (back * factor).astype(bf16)
            for i in range(pair):
                for m in range(micro):
                    at = i * tokens + m * rows
                    out_refs[(j + i) * micro + m][...] = back[at : at + rows, :]

    outs = pl.pallas_call(
        kernel,
        grid=(shard // tile,),
        out_shape=[jax.ShapeDtypeStruct((rows, shard), bf16)] * (groups * micro),
        in_specs=[pl.BlockSpec((tokens, features), lambda i: (0, 0))] * groups
        + [pl.BlockSpec((tile, features), lambda i: (i, 0)), pl.BlockSpec((1, tile), lambda i: (0, i))],
        out_specs=[pl.BlockSpec((rows, tile), lambda i: (0, i))] * (groups * micro),
        compiler_params=params(32),
        cost_estimate=cost(2 * groups * tokens * shard * features, 2 * groups * tokens * (shard + features) + 2 * shard * features),
        name="returned_blocks",
    )(*slots, weight, gain)
    return [list(outs[j * micro : (j + 1) * micro]) for j in range(groups)]


def row_gradient(x, top, blocks, me, m):
    groups = len(blocks)
    rows, shard = blocks[0].shape
    width = shard * groups
    step = 16

    def kernel(me_ref, x_ref, top_ref, *refs):
        block_refs, upper_ref, piece_ref = refs[:groups], refs[groups], refs[groups + 1]
        squares = jnp.zeros((step, 128), f32)
        dots = jnp.zeros((step, 128), f32)
        starts = [pl.multiple_of(lax.rem(me_ref[0] + j, groups) * shard, shard) for j in range(groups)]
        span = min(shard, 512)
        for j in range(groups):
            for c in range(0, shard, span):
                v = x_ref[0, 0, :, pl.ds(pl.multiple_of(starts[j] + c, span), span)].astype(f32)
                d = block_refs[j][:, c : c + span].astype(f32) * v
                v = v * v
                for k in range(0, span, 128):
                    squares = squares + v[:, k : k + 128]
                    dots = dots + d[:, k : k + 128]
        scale = lax.rsqrt(jnp.sum(squares, axis=1, keepdims=True) / width + norm_eps)
        mean = jnp.sum(dots, axis=1, keepdims=True) * scale / width
        slope = scale * mean
        for j in range(groups):
            for c in range(0, shard, span):
                at = pl.ds(pl.multiple_of(starts[j] + c, span), span)
                v = x_ref[0, 0, :, at].astype(f32)
                piece = (scale * (block_refs[j][:, c : c + span].astype(f32) - v * slope)).astype(bf16)
                piece_ref[:, at] = piece
                upper_ref[:, at] = (top_ref[0, :, at].astype(f32) + piece.astype(f32)).astype(bf16)

    return pl.pallas_call(
        kernel,
        grid=(rows // step,),
        out_shape=[jax.ShapeDtypeStruct((rows, width), bf16)] * 2,
        in_specs=[
            SMEM_ARG,
            pl.BlockSpec((1, 1, step, width), lambda i: (0, m, i, 0)),
            pl.BlockSpec((1, step, width), lambda i: (m, i, 0)),
        ]
        + [pl.BlockSpec((step, shard), lambda i: (i, 0))] * groups,
        out_specs=[pl.BlockSpec((step, width), lambda i: (i, 0))] * 2,
        compiler_params=params(24),
        cost_estimate=cost(12 * rows * width, 10 * rows * width),
        name="row_gradient",
    )(me, x, top, *blocks)


def finished_chunk(parts, orders, rep, reps, weight, factor, c, earlier):
    shard, features = weight.shape
    half_rows = parts[0][0].shape[0]
    piece = half_rows * 2 // reps
    count = len(parts)
    base = c * count * reps
    half = reps // 2
    steps = count * reps

    def owner(i, rep_ref):
        at = i * 0 + base
        for p, order in enumerate(orders):
            bits = len(order)
            pos = i - p * reps
            mask = sum(((pos >> (bits - 1 - b)) & 1) << order[b] for b in range(bits))
            inside = (i >= p * reps) & (i < (p + 1) * reps)
            at = at + jnp.where(inside, p * reps + (rep_ref[0] ^ mask), 0)
        return (at, 0)

    def kernel(rep_ref, *refs):
        part_refs = refs[: 2 * count]
        weight_ref, factor_ref = refs[2 * count], refs[2 * count + 1]
        grad_ref, gain_ref = refs[-2], refs[-1]
        i = pl.program_id(0)
        for k in range(2 * count):

            @pl.when((i >= k * half) & (i < (k + 1) * half))
            def _():
                raw = part_refs[k][...].astype(f32)
                grad_ref[...] = raw * factor_ref[:, 0:1]
                gain_ref[...] = jnp.sum(raw * weight_ref[...].astype(f32), axis=1, keepdims=True) * factor_ref[:, 1:2]

    def held(k):
        return lambda i, rep_ref: (jnp.clip(i - k * half, 0, half - 1), 0)

    operands = [a for pair in parts for a in pair]
    in_specs = [pl.BlockSpec((piece, features), held(k)) for k in range(2 * count)]
    in_specs += [pl.BlockSpec((piece, features), owner), pl.BlockSpec((piece, 2), owner)]
    aliases = {}
    extra = []
    if earlier is not None:
        extra = list(earlier)
        in_specs += [pl.BlockSpec(memory_space=pl.ANY)] * 2
        aliases = {1 + len(operands) + 2: 0, 1 + len(operands) + 3: 1}
    return pl.pallas_call(
        kernel,
        grid_spec=pltpu.PrefetchScalarGridSpec(
            num_scalar_prefetch=1,
            grid=(steps,),
            in_specs=in_specs,
            out_specs=[pl.BlockSpec((piece, features), owner), pl.BlockSpec((piece, 1), owner)],
        ),
        out_shape=[jax.ShapeDtypeStruct((shard, features), f32), jax.ShapeDtypeStruct((shard, 1), f32)],
        input_output_aliases=aliases,
        compiler_params=params(24),
        cost_estimate=cost(4 * piece * steps * features, 8 * piece * steps * features),
        name="finished_chunk",
    )(rep, *operands, weight, factor, *extra)


def local(layer_input, value_grad, value_weight, norm_gain, top_grad):
    groups = lax.axis_size("fsdp")
    reps = lax.axis_size("rep")
    bits = reps.bit_length() - 1
    me = lax.axis_index("fsdp").astype(jnp.int32)[None]
    rep = lax.axis_index("rep").astype(jnp.int32)[None]
    _, micro, rows, width = layer_input.shape
    tokens = micro * rows
    shard = width // groups
    norm_scale = float(tokens * reps * groups) ** (-0.5)
    chunks = 2
    orders = [tuple(range(bits)), tuple(reversed(range(bits)))]

    weight = value_weight[0]
    grads = value_grad[0].reshape(tokens, -1)
    gain = norm_gain[0].astype(f32) * norm_scale
    factor = jnp.stack([gain, jnp.full_like(gain, norm_scale)], axis=1)

    slots = line_gather(grads, "fsdp")
    hats = scaled_blocks(layer_input[0].reshape(tokens, width), me, groups, chunks)
    columns = []
    for c in range(chunks):
        sent = hats[c] if c == 0 else [after(h, *slots[1:]) for h in hats[c]]
        columns.append([sent[j] if j == 0 else cyclic(sent[j], "fsdp", j) for j in range(groups)])

    back = returned_blocks(slots, weight, norm_gain, micro)
    returned = []
    for m in range(micro):
        line = []
        for j in range(groups):
            block = back[j][m]
            if j:
                block = after(block, columns[-1][j] if m == 0 else returned[-1][1])
                block = cyclic(block, "fsdp", -j)
            line.append(block)
        returned.append(line)

    finished = None
    for c in range(chunks):
        product = weight_product(columns[c], slots, rep, reps, orders)
        kept = [product[2 * p] for p in range(len(orders))]
        sent = [product[2 * p + 1] for p in range(len(orders))]
        for b in range(bits):
            for p, order in enumerate(orders):
                other = flipped(sent[p], "rep", order[b])
                total = kept[p] + other.astype(f32)
                if b + 1 < bits:
                    half = total.shape[0] // 2
                    kept[p], sent[p] = total[:half], total[half:].astype(bf16)
                else:
                    kept[p] = total.astype(bf16)
        for b in reversed(range(bits)):
            for p, order in enumerate(orders):
                other = flipped(kept[p], "rep", order[b])
                kept[p] = jnp.concatenate([kept[p], other], axis=0) if b else (kept[p], other)
        finished = finished_chunk(kept, orders, rep, reps, weight, factor, c, finished)
    weight_grad, gain_grad = finished

    results = []
    is_upper = lax.axis_index("section") == 1
    for m in range(micro):
        upper, piece = row_gradient(layer_input, top_grad, returned[m], me, m)
        passed = lax.ppermute(upper, "section", [(1, 0)])
        lower = (passed.astype(f32) + piece.astype(f32)).astype(bf16)
        results.append(jnp.where(is_upper, upper, lower))
    return (jnp.stack(results)[None], weight_grad[None], gain_grad[:, 0][None])


def solution(mesh):
    return jax.shard_map(
        local,
        mesh=mesh,
        in_specs=(
            P("section", None, ("rep", "fsdp"), None),
            P("section", None, ("rep", "fsdp"), None),
            P("section", "fsdp", None),
            P("section", "fsdp"),
            P(None, ("rep", "fsdp"), None),
        ),
        out_specs=(
            P("section", None, ("rep", "fsdp"), None),
            P("section", "fsdp", None),
            P("section", "fsdp"),
        ),
        check_vma=False,
    )
```

```python
import jax
import jax.numpy as jnp
from jax import lax
from jax.experimental import pallas as pl
from jax.experimental.pallas import tpu as pltpu
from jax.sharding import PartitionSpec as P

norm_eps = 1e-05
bf16 = jnp.bfloat16
f32 = jnp.float32
MIB = 1 << 20
SMEM_ARG = pl.BlockSpec(memory_space=pltpu.SMEM)
VMEM_ARG = pl.BlockSpec(memory_space=pltpu.VMEM)


def cyclic(value, axis, steps):
    count = lax.axis_size(axis)
    return lax.ppermute(value, axis, [(i, (i + steps) % count) for i in range(count)])


def flipped(value, axis, mask):
    count = lax.axis_size(axis)
    return lax.ppermute(value, axis, [(i, i ^ mask) for i in range(count)])


def after(value, *others):
    return lax.optimization_barrier((value, *others))[0]


def params(mib):
    return pltpu.CompilerParams(vmem_limit_bytes=mib * MIB)


def cost(flops, bytes_accessed):
    return pl.CostEstimate(flops=int(flops), bytes_accessed=int(bytes_accessed), transcendentals=0)


def scaled_blocks(x, me, rep, groups, reps, chunks):
    tokens, width = x.shape
    shard = width // groups
    piece = shard // reps
    chunk = piece // chunks
    if chunk % 128:
        x = x.astype(f32)
        hat = (x * lax.rsqrt(jnp.mean(x * x, axis=1, keepdims=True) + norm_eps)).astype(bf16)
        hat = jnp.roll(hat.reshape(tokens, groups, reps, chunks, chunk), -me[0], axis=1)
        take = lambda e, c: lax.dynamic_index_in_dim(hat, rep[0] ^ e, 2, False)[:, :, c].reshape(tokens, groups * chunk)
        return [[take(e, c) for e in range(reps)] for c in range(chunks)]
    step = 16
    block = min(tokens, 32)

    def kernel(me_ref, rep_ref, x_ref, *out_refs):
        span = min(shard, 512)
        for row in range(0, block, step):
            rows = slice(row, row + step)
            total = jnp.zeros((step, 128), f32)
            for c in range(0, width, span):
                v = x_ref[rows, c : c + span].astype(f32)
                v = v * v
                for k in range(0, span, 128):
                    total = total + v[:, k : k + 128]
            scale = lax.rsqrt(jnp.sum(total, axis=1, keepdims=True) / width + norm_eps)
            for c in range(chunks):
                for e in range(reps):
                    for j in range(groups):
                        at = lax.rem(me_ref[0] + j, groups) * shard + (rep_ref[0] ^ e) * piece + c * chunk
                        v = x_ref[rows, pl.ds(pl.multiple_of(at, chunk), chunk)].astype(f32)
                        out_refs[c * reps + e][rows, j * chunk : (j + 1) * chunk] = (v * scale).astype(bf16)

    outs = pl.pallas_call(
        kernel,
        grid=(tokens // block,),
        out_shape=[jax.ShapeDtypeStruct((tokens, groups * chunk), bf16)] * (chunks * reps),
        in_specs=[SMEM_ARG, SMEM_ARG, pl.BlockSpec((block, width), lambda i: (i, 0))],
        out_specs=[pl.BlockSpec((block, groups * chunk), lambda i: (i, 0))] * (chunks * reps),
        compiler_params=params(8),
        cost_estimate=cost(6 * x.size, 4 * x.size),
        name="scaled_blocks",
    )(me, rep, x)
    return [list(outs[c * reps : (c + 1) * reps]) for c in range(chunks)]


def regrouped(blocks, groups):
    tokens, width = blocks[0].shape
    chunk = width // groups
    reps = len(blocks)
    if chunk % 128:
        return [jnp.concatenate([b[:, j * chunk : (j + 1) * chunk] for b in blocks], axis=0) for j in range(groups)]

    def kernel(*refs):
        for e in range(reps):
            for j in range(groups):
                refs[reps + j][e * tokens : (e + 1) * tokens, :] = refs[e][:, j * chunk : (j + 1) * chunk]

    return list(
        pl.pallas_call(
            kernel,
            out_shape=[jax.ShapeDtypeStruct((reps * tokens, chunk), bf16)] * groups,
            in_specs=[VMEM_ARG] * reps,
            out_specs=[VMEM_ARG] * groups,
            compiler_params=params(8),
            cost_estimate=cost(0, 4 * reps * tokens * width),
            name="regrouped",
        )(*blocks)
    )


def weight_product(chunks, grads, me, rep, groups, reps):
    rows, chunk = chunks[0][0].shape
    features = grads.shape[1]
    tokens = rows // reps
    count = len(chunks)

    def place(me, rep, j, e):
        return ((rep ^ e) * groups + lax.rem(me - j + groups, groups)) * tokens

    if chunk % 128:
        order = [lax.dynamic_slice_in_dim(grads, place(me[0], rep[0], j, e), tokens, 0) for j in range(groups) for e in range(reps)]
        values = jnp.concatenate(order, axis=0)
        contract = (((0,), (0,)), ((), ()))
        return [
            lax.dot_general(jnp.concatenate(c, axis=0), values, contract, preferred_element_type=f32).astype(bf16)
            for c in chunks
        ]

    def kernel(me_ref, rep_ref, *refs):
        block_refs, grads_ref = refs[: count * groups], refs[count * groups]
        out_refs, total = refs[count * groups + 1 : -1], refs[-1]
        for j in range(groups):
            values = []
            for e in range(reps):
                at = place(me_ref[0], rep_ref[0], j, e)
                values.append(grads_ref[pl.ds(pl.multiple_of(at, tokens), tokens), :])
            values = jnp.concatenate(values, axis=0)
            for c in range(count):
                product = lax.dot_general(
                    block_refs[c * groups + j][...], values, (((0,), (0,)), ((), ())), preferred_element_type=f32
                )
                if j == 0:
                    total[c] = product
                elif j + 1 < groups:
                    total[c] += product
                else:
                    out_refs[c][...] = (total[c] + product).astype(bf16)

    return pl.pallas_call(
        kernel,
        out_shape=[jax.ShapeDtypeStruct((chunk, features), bf16)] * count,
        in_specs=[SMEM_ARG] * 2 + [VMEM_ARG] * (count * groups + 1),
        out_specs=[VMEM_ARG] * count,
        scratch_shapes=[pltpu.VMEM((count, chunk, features), f32)],
        compiler_params=params(20),
        cost_estimate=cost(
            2 * groups * rows * chunk * count * features, 2 * groups * rows * (chunk * count + features) + 2 * chunk * count * features
        ),
        name="weight_product",
    )(me, rep, *[b for c in chunks for b in c], grads)


def returned_blocks(grads, weight, gain, me, groups, micro):
    features = grads.shape[1]
    tokens = grads.shape[0] // groups
    rows = tokens // micro
    shard = weight.shape[0]
    tile = min(shard, 512)

    def kernel(me_ref, grads_ref, weight_ref, gain_ref, *out_refs):
        factor = gain_ref[...].astype(f32)
        pair = 2 if groups % 2 == 0 else 1
        for j in range(0, groups, pair):
            values = []
            for i in range(pair):
                at = lax.rem(me_ref[0] - j - i + groups, groups) * tokens
                values.append(grads_ref[pl.ds(pl.multiple_of(at, tokens), tokens), :])
            values = jnp.concatenate(values, axis=0)
            back = lax.dot_general(values, weight_ref[...], (((1,), (1,)), ((), ())), preferred_element_type=f32)
            back = (back * factor).astype(bf16)
            for i in range(pair):
                for m in range(micro):
                    at = i * tokens + m * rows
                    out_refs[(j + i) * micro + m][...] = back[at : at + rows, :]

    outs = pl.pallas_call(
        kernel,
        grid=(shard // tile,),
        out_shape=[jax.ShapeDtypeStruct((rows, shard), bf16)] * (groups * micro),
        in_specs=[
            SMEM_ARG,
            pl.BlockSpec((groups * tokens, features), lambda i: (0, 0)),
            pl.BlockSpec((tile, features), lambda i: (i, 0)),
            pl.BlockSpec((1, tile), lambda i: (0, i)),
        ],
        out_specs=[pl.BlockSpec((rows, tile), lambda i: (0, i))] * (groups * micro),
        compiler_params=params(14),
        cost_estimate=cost(2 * groups * tokens * shard * features, 2 * groups * tokens * (shard + features) + 2 * shard * features),
        name="returned_blocks",
    )(me, grads, weight, gain)
    return [list(outs[j * micro : (j + 1) * micro]) for j in range(groups)]


def row_gradient(x, top, blocks, me, m):
    groups = len(blocks)
    rows, shard = blocks[0].shape
    width = shard * groups
    step = 16

    def kernel(me_ref, x_ref, top_ref, *refs):
        block_refs, upper_ref, piece_ref = refs[:groups], refs[groups], refs[groups + 1]
        squares = jnp.zeros((step, 128), f32)
        dots = jnp.zeros((step, 128), f32)
        starts = [pl.multiple_of(lax.rem(me_ref[0] + j, groups) * shard, shard) for j in range(groups)]
        span = min(shard, 512)
        for j in range(groups):
            for c in range(0, shard, span):
                v = x_ref[0, 0, :, pl.ds(pl.multiple_of(starts[j] + c, span), span)].astype(f32)
                d = block_refs[j][:, c : c + span].astype(f32) * v
                v = v * v
                for k in range(0, span, 128):
                    squares = squares + v[:, k : k + 128]
                    dots = dots + d[:, k : k + 128]
        scale = lax.rsqrt(jnp.sum(squares, axis=1, keepdims=True) / width + norm_eps)
        mean = jnp.sum(dots, axis=1, keepdims=True) * scale / width
        slope = scale * mean
        for j in range(groups):
            for c in range(0, shard, span):
                at = pl.ds(pl.multiple_of(starts[j] + c, span), span)
                v = x_ref[0, 0, :, at].astype(f32)
                piece = (scale * (block_refs[j][:, c : c + span].astype(f32) - v * slope)).astype(bf16)
                piece_ref[:, at] = piece
                upper_ref[:, at] = (top_ref[0, :, at].astype(f32) + piece.astype(f32)).astype(bf16)

    return pl.pallas_call(
        kernel,
        grid=(rows // step,),
        out_shape=[jax.ShapeDtypeStruct((rows, width), bf16)] * 2,
        in_specs=[
            SMEM_ARG,
            pl.BlockSpec((1, 1, step, width), lambda i: (0, m, i, 0)),
            pl.BlockSpec((1, step, width), lambda i: (m, i, 0)),
        ]
        + [pl.BlockSpec((step, shard), lambda i: (i, 0))] * groups,
        out_specs=[pl.BlockSpec((step, width), lambda i: (i, 0))] * 2,
        compiler_params=params(8),
        cost_estimate=cost(12 * rows * width, 10 * rows * width),
        name="row_gradient",
    )(me, x, top, *blocks)


def input_gradient(upper, piece, passed, is_upper, shape, m, earlier):
    rows, width = upper.shape
    step = min(rows, 32)

    def kernel(is_upper_ref, upper_ref, piece_ref, passed_ref, *refs):
        lower = (passed_ref[...].astype(f32) + piece_ref[...].astype(f32)).astype(bf16)
        refs[-1][0, 0] = jnp.where(is_upper_ref[0] == 1, upper_ref[...], lower)

    spec = pl.BlockSpec((step, width), lambda i: (i, 0))
    return pl.pallas_call(
        kernel,
        grid=(rows // step,),
        out_shape=jax.ShapeDtypeStruct(shape, bf16),
        in_specs=[SMEM_ARG, spec, spec, spec] + [pl.BlockSpec(memory_space=pl.ANY)] * len(earlier),
        out_specs=pl.BlockSpec((1, 1, step, width), lambda i: (0, m, i, 0)),
        input_output_aliases={4: 0} if earlier else {},
        compiler_params=params(8),
        cost_estimate=cost(4 * rows * width, 8 * rows * width),
        name="input_gradient",
    )(is_upper, upper, piece, passed, *earlier)


def finished_chunk(sums, weight, factor, c, chunks, earlier):
    reps, rows, features = sums.shape
    shard = weight.shape[0]

    def kernel(sum_ref, weight_ref, factor_ref, *refs):
        raw = sum_ref[0].astype(f32)
        refs[-2][...] = raw * factor_ref[:, 0:1]
        refs[-1][...] = jnp.sum(raw * weight_ref[...].astype(f32), axis=1, keepdims=True) * factor_ref[:, 1:2]

    place = lambda i: (i * chunks + c, 0)
    return pl.pallas_call(
        kernel,
        grid=(reps,),
        out_shape=[jax.ShapeDtypeStruct((shard, features), f32), jax.ShapeDtypeStruct((shard, 1), f32)],
        in_specs=[
            pl.BlockSpec((1, rows, features), lambda i: (i, 0, 0)),
            pl.BlockSpec((rows, features), place),
            pl.BlockSpec((rows, 2), place),
        ]
        + [pl.BlockSpec(memory_space=pl.ANY)] * len(earlier),
        out_specs=[pl.BlockSpec((rows, features), place), pl.BlockSpec((rows, 1), place)],
        input_output_aliases={3: 0, 4: 1} if earlier else {},
        compiler_params=params(8),
        cost_estimate=cost(4 * reps * rows * features, 8 * reps * rows * features),
        name="finished_chunk",
    )(sums, weight, factor, *earlier)


def local(layer_input, value_grad, value_weight, norm_gain, top_grad):
    groups = lax.axis_size("fsdp")
    reps = lax.axis_size("rep")
    me = lax.axis_index("fsdp").astype(jnp.int32)[None]
    rep = lax.axis_index("rep").astype(jnp.int32)[None]
    _, micro, rows, width = layer_input.shape
    tokens = micro * rows
    norm_scale = float(tokens * reps * groups) ** (-0.5)
    chunks = 2

    weight = value_weight[0]
    gain = norm_gain[0].astype(f32) * norm_scale
    factor = jnp.stack([gain, jnp.full_like(gain, norm_scale)], axis=1)

    grads = lax.all_gather(value_grad[0].reshape(tokens, -1), "fsdp", axis=0, tiled=True)
    grads_all = lax.all_gather(grads, "rep", axis=0, tiled=True)

    hats = scaled_blocks(layer_input[0].reshape(tokens, width), me, rep, groups, reps, chunks)
    columns = []
    for c in range(chunks):
        plane = [hats[c][e] if e == 0 else flipped(hats[c][e], "rep", e) for e in range(reps)]
        sent = regrouped(plane, groups)
        columns.append([sent[j] if j == 0 else cyclic(sent[j], "fsdp", j) for j in range(groups)])

    sums = weight_product(columns, grads_all, me, rep, groups, reps)
    finished = ()
    for c in range(chunks):
        gathered = lax.all_gather(sums[c], "rep", axis=0)
        finished = finished_chunk(gathered, weight, factor, c, chunks, finished)
    weight_grad, gain_grad = finished

    back = returned_blocks(grads, weight, norm_gain, me, groups, micro)
    ties = [columns[0][1:], columns[1][1:2]]
    result = ()
    is_upper = lax.axis_index("section").astype(jnp.int32)[None]
    for m in range(micro):
        line = [back[j][m] for j in range(groups)]
        for j in range(1, groups):
            line[j] = cyclic(after(line[j], *ties[min(j - 1, 1)]), "fsdp", -j)
        ties = [line[1:2], line[2:3]]
        upper, piece = row_gradient(layer_input, top_grad, line, me, m)
        passed = lax.ppermute(upper, "section", [(1, 0)])
        result = (input_gradient(upper, piece, passed, is_upper, layer_input.shape, m, result),)
    return (result[0], weight_grad[None], gain_grad[:, 0][None])


def solution(mesh):
    return jax.shard_map(
        local,
        mesh=mesh,
        in_specs=(
            P("section", None, ("rep", "fsdp"), None),
            P("section", None, ("rep", "fsdp"), None),
            P("section", "fsdp", None),
            P("section", "fsdp"),
            P(None, ("rep", "fsdp"), None),
        ),
        out_specs=(
            P("section", None, ("rep", "fsdp"), None),
            P("section", "fsdp", None),
            P("section", "fsdp"),
        ),
        check_vma=False,
    )
```

```python
import jax
import jax.numpy as jnp
from jax import lax
from jax.experimental import pallas as pl
from jax.experimental.pallas import tpu as pltpu
from jax.sharding import PartitionSpec as P

norm_eps = 1e-05
bf16 = jnp.bfloat16
f32 = jnp.float32
MIB = 1 << 20
SMEM_ARG = pl.BlockSpec(memory_space=pltpu.SMEM)
ANY_ARG = pl.BlockSpec(memory_space=pl.ANY)


def cyclic(value, axis, steps):
    count = lax.axis_size(axis)
    return lax.ppermute(value, axis, [(i, (i + steps) % count) for i in range(count)])


def flipped(value, axis, mask):
    count = lax.axis_size(axis)
    return lax.ppermute(value, axis, [(i, i ^ mask) for i in range(count)])


def after(value, *others):
    return lax.optimization_barrier((value, *others))[0]


def params(mib):
    return pltpu.CompilerParams(vmem_limit_bytes=mib * MIB)


def cost(flops, bytes_accessed):
    return pl.CostEstimate(flops=int(flops), bytes_accessed=int(bytes_accessed), transcendentals=0)


def scaled_blocks(x, me, rep, groups, reps, chunks):
    tokens, width = x.shape
    shard = width // groups
    piece = shard // reps
    chunk = piece // chunks
    if chunk % 128:
        x = x.astype(f32)
        hat = (x * lax.rsqrt(jnp.mean(x * x, axis=1, keepdims=True) + norm_eps)).astype(bf16)
        hat = jnp.roll(hat.reshape(tokens, groups, reps, chunks, chunk), -me[0], axis=1)
        take = lambda e, c: lax.dynamic_index_in_dim(hat, rep[0] ^ e, 2, False)[:, :, c].reshape(tokens, groups * chunk)
        return [[take(e, c) for e in range(reps)] for c in range(chunks)]
    step = 16
    block = min(tokens, 32)

    def kernel(me_ref, rep_ref, x_ref, *out_refs):
        span = min(shard, 512)
        for row in range(0, block, step):
            rows = slice(row, row + step)
            total = jnp.zeros((step, 128), f32)
            for c in range(0, width, span):
                v = x_ref[rows, c : c + span].astype(f32)
                v = v * v
                for k in range(0, span, 128):
                    total = total + v[:, k : k + 128]
            scale = lax.rsqrt(jnp.sum(total, axis=1, keepdims=True) / width + norm_eps)
            for c in range(chunks):
                for e in range(reps):
                    for j in range(groups):
                        at = lax.rem(me_ref[0] + j, groups) * shard + (rep_ref[0] ^ e) * piece + c * chunk
                        v = x_ref[rows, pl.ds(pl.multiple_of(at, chunk), chunk)].astype(f32)
                        out_refs[c * reps + e][rows, j * chunk : (j + 1) * chunk] = (v * scale).astype(bf16)

    outs = pl.pallas_call(
        kernel,
        grid=(tokens // block,),
        out_shape=[jax.ShapeDtypeStruct((tokens, groups * chunk), bf16)] * (chunks * reps),
        in_specs=[SMEM_ARG, SMEM_ARG, pl.BlockSpec((block, width), lambda i: (i, 0))],
        out_specs=[pl.BlockSpec((block, groups * chunk), lambda i: (i, 0))] * (chunks * reps),
        compiler_params=params(8),
        cost_estimate=cost(6 * x.size, 4 * x.size),
        name="scaled_blocks",
    )(me, rep, x)
    return [list(outs[c * reps : (c + 1) * reps]) for c in range(chunks)]


def doubled(value, order):
    for bit in order[:-1]:
        value = jnp.concatenate([value, flipped(value, "rep", 1 << bit)], axis=0)
    return value, flipped(value, "rep", 1 << order[-1])


def mask_of(pos, order):
    return sum(((pos >> i) & 1) << bit for i, bit in enumerate(order))


def regrouped(blocks, groups):
    tokens, width = blocks[0].shape
    chunk = width // groups
    reps = len(blocks)
    if chunk % 128:
        return [jnp.concatenate([b[:, j * chunk : (j + 1) * chunk] for b in blocks], axis=0) for j in range(groups)]

    def kernel(*refs):
        copies = []
        for e in range(reps):
            for j in range(groups):
                source = refs[e].at[:, j * chunk : (j + 1) * chunk]
                target = refs[reps + j].at[e * tokens : (e + 1) * tokens, :]
                copies.append(pltpu.make_async_copy(source, target, refs[-1].at[e * groups + j]))
                copies[-1].start()
        for copy in copies:
            copy.wait()

    return list(
        pl.pallas_call(
            kernel,
            out_shape=[jax.ShapeDtypeStruct((reps * tokens, chunk), bf16)] * groups,
            in_specs=[ANY_ARG] * reps,
            out_specs=[ANY_ARG] * groups,
            scratch_shapes=[pltpu.SemaphoreType.DMA((reps * groups,))],
            compiler_params=params(8),
            cost_estimate=cost(0, 4 * reps * tokens * width),
            name="regrouped",
        )(*blocks)
    )


def weight_product(columns, values, weight, gain, groups, count, norm_scale):
    rows, width = columns[0].shape
    reps = len(values)
    tokens = rows // reps
    features = values[0].shape[1]
    chunk = width // count
    contract = (((0,), (0,)), ((), ()))

    def thirds(row):
        first = row.astype(bf16)
        rest = row - first.astype(f32)
        second = rest.astype(bf16)
        return first, second, (rest - second.astype(f32)).astype(bf16)

    if chunk % 128:
        order = jnp.stack([v.reshape(groups, tokens, features) for v in values], axis=1)
        raw = lax.dot_general(
            jnp.concatenate(columns, axis=0), order.reshape(-1, features), contract, preferred_element_type=f32
        )
        dots = jnp.sum(raw * weight.astype(f32), axis=1) * norm_scale
        raw = (raw * gain).astype(bf16)
        outs = []
        for c in range(count):
            at = slice(c * chunk, (c + 1) * chunk)
            under = jnp.stack(thirds(dots[at]) + (jnp.zeros((chunk,), bf16),) * 13)
            outs.append(jnp.concatenate([raw[at], jnp.pad(under, ((0, 0), (0, features - chunk)))], axis=0))
        return outs

    def kernel(*refs):
        column_refs, value_refs = refs[:groups], refs[groups : groups + reps]
        weight_ref, gain_ref = refs[groups + reps], refs[groups + reps + 1]
        out_refs = refs[groups + reps + 2 : -5]
        left, right, own, total, sems = refs[-5:]
        copies = []
        for j in range(groups):
            line = [pltpu.make_async_copy(column_refs[j], left.at[j], sems.at[j, reps])]
            for e in range(reps):
                source = value_refs[e].at[j * tokens : (j + 1) * tokens, :]
                target = right.at[j, e * tokens : (e + 1) * tokens, :]
                line.append(pltpu.make_async_copy(source, target, sems.at[j, e]))
            for copy in line:
                copy.start()
            copies.append(line)
        copy = pltpu.make_async_copy(weight_ref, own, sems.at[groups, 0])
        copy.start()
        for j in range(groups):
            for c in copies[j]:
                c.wait()
            for c in range(count):
                block = left[j, :, c * chunk : (c + 1) * chunk]
                product = lax.dot_general(block, right[j], contract, preferred_element_type=f32)
                if j == 0:
                    total[c] = product
                else:
                    total[c] += product
        copy.wait()
        for c in range(count):
            at = slice(c * chunk, (c + 1) * chunk)
            raw = total[c]
            out_refs[c][:chunk, :] = (raw * gain_ref[at, :]).astype(bf16)
            dots = lax.dot_general(
                jnp.full((8, features), norm_scale, f32),
                raw * own[at, :].astype(f32),
                (((1,), (1,)), ((), ())),
                precision=lax.Precision.HIGHEST,
                preferred_element_type=f32,
            )
            under = jnp.concatenate([row[0:1, :].astype(f32) for row in thirds(dots)] + [jnp.zeros((13, chunk), f32)], axis=0)
            out_refs[c][chunk:, :chunk] = under.astype(bf16)
            out_refs[c][chunk:, chunk:] = jnp.zeros((16, features - chunk), bf16)

    return pl.pallas_call(
        kernel,
        out_shape=[jax.ShapeDtypeStruct((chunk + 16, features), bf16)] * count,
        in_specs=[ANY_ARG] * (groups + reps + 1) + [pl.BlockSpec(memory_space=pltpu.VMEM)],
        scratch_shapes=[
            pltpu.VMEM((groups, rows, width), bf16),
            pltpu.VMEM((groups, rows, features), bf16),
            pltpu.VMEM((width, features), bf16),
            pltpu.VMEM((count, chunk, features), f32),
            pltpu.SemaphoreType.DMA((groups + 1, reps + 1)),
        ],
        compiler_params=params(24),
        cost_estimate=cost(2 * groups * rows * width * features, 2 * groups * rows * (width + features) + 4 * width * features),
        name="weight_product",
    )(*columns, *values, weight, gain)


def returned_blocks(slots, weight, gain, micro):
    groups = len(slots)
    tokens, features = slots[0].shape
    rows = tokens // micro
    shard = weight.shape[0]
    tile = min(shard, 512)

    def kernel(*refs):
        slot_refs, weight_ref, gain_ref = refs[:groups], refs[groups], refs[groups + 1]
        out_refs = refs[groups + 2 :]
        factor = gain_ref[...].astype(f32)
        pair = 2 if groups % 2 == 0 else 1
        for j in range(0, groups, pair):
            values = jnp.concatenate([slot_refs[j + i][...] for i in range(pair)], axis=0)
            back = lax.dot_general(values, weight_ref[...], (((1,), (1,)), ((), ())), preferred_element_type=f32)
            back = (back * factor).astype(bf16)
            for i in range(pair):
                for m in range(micro):
                    at = i * tokens + m * rows
                    out_refs[(j + i) * micro + m][...] = back[at : at + rows, :]

    outs = pl.pallas_call(
        kernel,
        grid=(shard // tile,),
        out_shape=[jax.ShapeDtypeStruct((rows, shard), bf16)] * (groups * micro),
        in_specs=[pl.BlockSpec((tokens, features), lambda i: (0, 0))] * groups
        + [pl.BlockSpec((tile, features), lambda i: (i, 0)), pl.BlockSpec((1, tile), lambda i: (0, i))],
        out_specs=[pl.BlockSpec((rows, tile), lambda i: (0, i))] * (groups * micro),
        compiler_params=params(8),
        cost_estimate=cost(2 * groups * tokens * shard * features, 2 * groups * tokens * (shard + features) + 2 * shard * features),
        name="returned_blocks",
    )(*slots, weight, gain)
    return [list(outs[j * micro : (j + 1) * micro]) for j in range(groups)]


def row_gradient(x, top, blocks, me, m):
    groups = len(blocks)
    rows, shard = blocks[0].shape
    width = shard * groups
    step = 16

    def kernel(me_ref, x_ref, top_ref, *refs):
        block_refs, upper_ref, piece_ref = refs[:groups], refs[groups], refs[groups + 1]
        squares = jnp.zeros((step, 128), f32)
        dots = jnp.zeros((step, 128), f32)
        starts = [pl.multiple_of(lax.rem(me_ref[0] + j, groups) * shard, shard) for j in range(groups)]
        span = min(shard, 512)
        for j in range(groups):
            for c in range(0, shard, span):
                v = x_ref[0, 0, :, pl.ds(pl.multiple_of(starts[j] + c, span), span)].astype(f32)
                d = block_refs[j][:, c : c + span].astype(f32) * v
                v = v * v
                for k in range(0, span, 128):
                    squares = squares + v[:, k : k + 128]
                    dots = dots + d[:, k : k + 128]
        scale = lax.rsqrt(jnp.sum(squares, axis=1, keepdims=True) / width + norm_eps)
        mean = jnp.sum(dots, axis=1, keepdims=True) * scale / width
        slope = scale * mean
        for j in range(groups):
            for c in range(0, shard, span):
                at = pl.ds(pl.multiple_of(starts[j] + c, span), span)
                v = x_ref[0, 0, :, at].astype(f32)
                piece = (scale * (block_refs[j][:, c : c + span].astype(f32) - v * slope)).astype(bf16)
                piece_ref[:, at] = piece
                upper_ref[:, at] = (top_ref[0, :, at].astype(f32) + piece.astype(f32)).astype(bf16)

    return pl.pallas_call(
        kernel,
        grid=(rows // step,),
        out_shape=[jax.ShapeDtypeStruct((rows, width), bf16)] * 2,
        in_specs=[
            SMEM_ARG,
            pl.BlockSpec((1, 1, step, width), lambda i: (0, m, i, 0)),
            pl.BlockSpec((1, step, width), lambda i: (m, i, 0)),
        ]
        + [pl.BlockSpec((step, shard), lambda i: (i, 0))] * groups,
        out_specs=[pl.BlockSpec((step, width), lambda i: (i, 0))] * 2,
        compiler_params=params(8),
        cost_estimate=cost(12 * rows * width, 10 * rows * width),
        name="row_gradient",
    )(me, x, top, *blocks)


def input_gradient(upper, piece, passed, is_upper, shape, m, earlier):
    rows, width = upper.shape
    step = min(rows, 32)

    def kernel(is_upper_ref, upper_ref, piece_ref, passed_ref, *refs):
        lower = (passed_ref[...].astype(f32) + piece_ref[...].astype(f32)).astype(bf16)
        refs[-1][0, 0] = jnp.where(is_upper_ref[0] == 1, upper_ref[...], lower)

    spec = pl.BlockSpec((step, width), lambda i: (i, 0))
    return pl.pallas_call(
        kernel,
        grid=(rows // step,),
        out_shape=jax.ShapeDtypeStruct(shape, bf16),
        in_specs=[SMEM_ARG, spec, spec, spec] + [ANY_ARG] * len(earlier),
        out_specs=pl.BlockSpec((1, 1, step, width), lambda i: (0, m, i, 0)),
        input_output_aliases={4: 0} if earlier else {},
        compiler_params=params(8),
        cost_estimate=cost(4 * rows * width, 8 * rows * width),
        name="input_gradient",
    )(is_upper, upper, piece, passed, *earlier)


def finished_half(sums, rep, order, half, c, chunks, earlier):
    pieces = (1 << len(order)) // 2
    rows = sums.shape[0] // pieces - 16
    features = sums.shape[1]
    shard = rows * chunks * pieces * 2

    def place(i, rep_ref):
        return (rep_ref[0] ^ mask_of(i + half * pieces, order)) * chunks + c

    def total(under):
        return under[0:1, :rows] + under[1:2, :rows] + under[2:3, :rows]

    if rows % 128:
        earlier = earlier or (jnp.zeros((shard, features), f32), jnp.zeros((1, shard), f32))
        for i in range(pieces):
            piece = sums[i * (rows + 16) : (i + 1) * (rows + 16)].astype(f32)
            at = place(i, rep) * rows
            earlier = (
                lax.dynamic_update_slice(earlier[0], piece[:rows], (at, 0)),
                lax.dynamic_update_slice(earlier[1], total(piece[rows:]), (0, at)),
            )
        return earlier

    def kernel(rep_ref, sum_ref, *refs):
        refs[-2][...] = sum_ref[:rows, :].astype(f32)
        refs[-1][...] = total(sum_ref[rows:, :].astype(f32))

    return pl.pallas_call(
        kernel,
        grid_spec=pltpu.PrefetchScalarGridSpec(
            num_scalar_prefetch=1,
            grid=(pieces,),
            in_specs=[pl.BlockSpec((rows + 16, features), lambda i, rep_ref: (i, 0))] + [ANY_ARG] * len(earlier),
            out_specs=[
                pl.BlockSpec((rows, features), lambda i, rep_ref: (place(i, rep_ref), 0)),
                pl.BlockSpec((1, rows), lambda i, rep_ref: (0, place(i, rep_ref))),
            ],
        ),
        out_shape=[jax.ShapeDtypeStruct((shard, features), f32), jax.ShapeDtypeStruct((1, shard), f32)],
        input_output_aliases={2: 0, 3: 1} if earlier else {},
        compiler_params=params(8),
        cost_estimate=cost(sums.size, 6 * sums.size),
        name="finished_half",
    )(rep, sums, *earlier)


def local(layer_input, value_grad, value_weight, norm_gain, top_grad):
    groups = lax.axis_size("fsdp")
    reps = lax.axis_size("rep")
    bits = reps.bit_length() - 1
    me = lax.axis_index("fsdp").astype(jnp.int32)[None]
    rep = lax.axis_index("rep").astype(jnp.int32)[None]
    _, micro, rows, width = layer_input.shape
    tokens = micro * rows
    norm_scale = float(tokens * reps * groups) ** (-0.5)
    chunks = 2
    orders = [tuple(range(bits)), tuple(reversed(range(bits)))]

    weight = value_weight[0]
    piece = weight.shape[0] // reps
    own_weight = lax.dynamic_slice_in_dim(weight, rep[0] * piece, piece, 0)
    own_gain = lax.dynamic_slice_in_dim(norm_gain[0], rep[0] * piece, piece, 0).astype(f32)[:, None] * norm_scale

    hats = scaled_blocks(layer_input[0].reshape(tokens, width), me, rep, groups, reps, 1)[0]
    plane = list(hats)
    for e in range(1, reps):
        plane[e] = flipped(hats[e], "rep", e)
    grads = after(value_grad[0].reshape(tokens, -1), hats[0])
    slots = [grads] + [cyclic(grads, "fsdp", j) for j in range(1, groups)]

    sent = regrouped(plane, groups)
    back = returned_blocks(slots, weight, norm_gain, micro)
    columns = list(sent)
    for j in range(1, groups):
        columns[j] = cyclic(after(sent[j], back[0][0]) if j == groups - 1 else sent[j], "fsdp", j)
    held = after(jnp.concatenate(slots, axis=0), sent[0])
    values = [held if e == 0 else flipped(held, "rep", e) for e in range(reps)]

    lines = []
    ties = [columns[1:2], columns[2:]]
    for m in range(micro):
        line = [back[j][m] for j in range(groups)]
        for j in range(1, groups):
            line[j] = cyclic(after(line[j], *ties[min(j - 1, 1)]), "fsdp", -j)
        ties = [line[1:2], line[2:3]]
        lines.append(line)
    own = (after(own_weight, back[0][0]), after(own_gain, back[0][0]))
    sums = weight_product(columns, values, *own, groups, chunks, norm_scale)
    gathered = [doubled(sums[c], orders[c]) for c in range(chunks)]
    finished = ()
    for half in (0, 1):
        for c in range(chunks):
            finished = finished_half(gathered[c][half], rep, orders[c], half, c, chunks, finished)
        if half == 0:
            early = finished
    weight_grad, gain_grad = finished

    result = ()
    is_upper = lax.axis_index("section").astype(jnp.int32)[None]
    for m in range(micro):
        lines[m][0] = after(lines[m][0], *([g[0] for g in gathered] if m == 0 else early))
        upper, piece = row_gradient(layer_input, top_grad, lines[m], me, m)
        passed = lax.ppermute(upper, "section", [(1, 0)])
        result = (input_gradient(upper, piece, passed, is_upper, layer_input.shape, m, result),)
    return (result[0], weight_grad[None], gain_grad)


def solution(mesh):
    return jax.shard_map(
        local,
        mesh=mesh,
        in_specs=(
            P("section", None, ("rep", "fsdp"), None),
            P("section", None, ("rep", "fsdp"), None),
            P("section", "fsdp", None),
            P("section", "fsdp"),
            P(None, ("rep", "fsdp"), None),
        ),
        out_specs=(
            P("section", None, ("rep", "fsdp"), None),
            P("section", "fsdp", None),
            P("section", "fsdp"),
        ),
        check_vma=False,
    )
```

```python
import jax
import jax.numpy as jnp
from jax import lax
from jax.experimental import pallas as pl
from jax.experimental.pallas import tpu as pltpu
from jax.sharding import PartitionSpec as P

norm_eps = 1e-05
bf16 = jnp.bfloat16
f32 = jnp.float32
MIB = 1 << 20
SMEM_ARG = pl.BlockSpec(memory_space=pltpu.SMEM)
ANY_ARG = pl.BlockSpec(memory_space=pl.ANY)


def cyclic(value, axis, steps):
    count = lax.axis_size(axis)
    return lax.ppermute(value, axis, [(i, (i + steps) % count) for i in range(count)])


def flipped(value, axis, mask):
    count = lax.axis_size(axis)
    return lax.ppermute(value, axis, [(i, i ^ mask) for i in range(count)])


def after(value, *others):
    return lax.optimization_barrier((value, *others))[0]


def params(mib):
    return pltpu.CompilerParams(vmem_limit_bytes=mib * MIB)


def cost(flops, bytes_accessed):
    return pl.CostEstimate(flops=int(flops), bytes_accessed=int(bytes_accessed), transcendentals=0)


def scaled_blocks(x, me, rep, groups, reps, chunks):
    tokens, width = x.shape
    shard = width // groups
    piece = shard // reps
    chunk = piece // chunks
    if chunk % 128:
        x = x.astype(f32)
        hat = (x * lax.rsqrt(jnp.mean(x * x, axis=1, keepdims=True) + norm_eps)).astype(bf16)
        hat = jnp.roll(hat.reshape(tokens, groups, reps, chunks, chunk), -me[0], axis=1)
        take = lambda e, c: lax.dynamic_index_in_dim(hat, rep[0] ^ e, 2, False)[:, :, c].reshape(tokens, groups * chunk)
        return [[take(e, c) for e in range(reps)] for c in range(chunks)]
    step = 16
    block = min(tokens, 32)

    def kernel(me_ref, rep_ref, x_ref, *out_refs):
        span = min(shard, 512)
        for row in range(0, block, step):
            rows = slice(row, row + step)
            total = jnp.zeros((step, 128), f32)
            for c in range(0, width, span):
                v = x_ref[rows, c : c + span].astype(f32)
                v = v * v
                for k in range(0, span, 128):
                    total = total + v[:, k : k + 128]
            scale = lax.rsqrt(jnp.sum(total, axis=1, keepdims=True) / width + norm_eps)
            for c in range(chunks):
                for e in range(reps):
                    for j in range(groups):
                        at = lax.rem(me_ref[0] + j, groups) * shard + (rep_ref[0] ^ e) * piece + c * chunk
                        v = x_ref[rows, pl.ds(pl.multiple_of(at, chunk), chunk)].astype(f32)
                        out_refs[c * reps + e][rows, j * chunk : (j + 1) * chunk] = (v * scale).astype(bf16)

    outs = pl.pallas_call(
        kernel,
        grid=(tokens // block,),
        out_shape=[jax.ShapeDtypeStruct((tokens, groups * chunk), bf16)] * (chunks * reps),
        in_specs=[SMEM_ARG, SMEM_ARG, pl.BlockSpec((block, width), lambda i: (i, 0))],
        out_specs=[pl.BlockSpec((block, groups * chunk), lambda i: (i, 0))] * (chunks * reps),
        compiler_params=params(8),
        cost_estimate=cost(6 * x.size, 4 * x.size),
        name="scaled_blocks",
    )(me, rep, x)
    return [list(outs[c * reps : (c + 1) * reps]) for c in range(chunks)]


def joined(arrays):
    rows, width = arrays[0].shape
    if rows % 16 or width % 128:
        return jnp.concatenate(arrays, axis=0)

    def kernel(*refs):
        copies = []
        for k in range(len(arrays)):
            target = refs[-2].at[k * rows : (k + 1) * rows, :]
            copies.append(pltpu.make_async_copy(refs[k], target, refs[-1].at[k]))
            copies[-1].start()
        for copy in copies:
            copy.wait()

    return pl.pallas_call(
        kernel,
        out_shape=jax.ShapeDtypeStruct((len(arrays) * rows, width), bf16),
        in_specs=[ANY_ARG] * len(arrays),
        out_specs=ANY_ARG,
        scratch_shapes=[pltpu.SemaphoreType.DMA((len(arrays),))],
        compiler_params=params(4),
        cost_estimate=cost(0, 4 * len(arrays) * rows * width),
        name="joined",
    )(*arrays)


def doubled(value, order):
    for bit in order[:-1]:
        value = joined([value, flipped(value, "rep", 1 << bit)])
    return value, flipped(value, "rep", 1 << order[-1])


def mask_of(pos, order):
    return sum(((pos >> i) & 1) << bit for i, bit in enumerate(order))


def regrouped(blocks, groups):
    tokens, width = blocks[0].shape
    chunk = width // groups
    reps = len(blocks)
    if chunk % 128:
        return [jnp.concatenate([b[:, j * chunk : (j + 1) * chunk] for b in blocks], axis=0) for j in range(groups)]

    def kernel(*refs):
        copies = []
        for e in range(reps):
            for j in range(groups):
                source = refs[e].at[:, j * chunk : (j + 1) * chunk]
                target = refs[reps + j].at[e * tokens : (e + 1) * tokens, :]
                copies.append(pltpu.make_async_copy(source, target, refs[-1].at[e * groups + j]))
                copies[-1].start()
        for copy in copies:
            copy.wait()

    return list(
        pl.pallas_call(
            kernel,
            out_shape=[jax.ShapeDtypeStruct((reps * tokens, chunk), bf16)] * groups,
            in_specs=[ANY_ARG] * reps,
            out_specs=[ANY_ARG] * groups,
            scratch_shapes=[pltpu.SemaphoreType.DMA((reps * groups,))],
            compiler_params=params(8),
            cost_estimate=cost(0, 4 * reps * tokens * width),
            name="regrouped",
        )(*blocks)
    )


def weight_product(columns, values, weight, gain, rep, groups, count, norm_scale):
    rows, width = columns[0].shape
    reps = len(values)
    tokens = rows // reps
    features = values[0].shape[1]
    chunk = width // count
    contract = (((0,), (0,)), ((), ()))

    def thirds(row):
        first = row.astype(bf16)
        rest = row - first.astype(f32)
        second = rest.astype(bf16)
        return first, second, (rest - second.astype(f32)).astype(bf16)

    if chunk % 128:
        order = jnp.stack([v.reshape(groups, tokens, features) for v in values], axis=1)
        raw = lax.dot_general(
            jnp.concatenate(columns, axis=0), order.reshape(-1, features), contract, preferred_element_type=f32
        )
        own = lax.dynamic_slice_in_dim(weight, rep[0] * width, width, 0).astype(f32)
        dots = jnp.sum(raw * own, axis=1) * norm_scale
        factor = lax.dynamic_slice_in_dim(gain[0], rep[0] * width, width, 0).astype(f32) * norm_scale
        raw = (raw * factor[:, None]).astype(bf16)
        outs = []
        for c in range(count):
            at = slice(c * chunk, (c + 1) * chunk)
            under = jnp.stack(thirds(dots[at]) + (jnp.zeros((chunk,), bf16),) * 13)
            outs.append(jnp.concatenate([raw[at], jnp.pad(under, ((0, 0), (0, features - chunk)))], axis=0))
        return outs

    def kernel(rep_ref, *refs):
        column_refs, value_refs = refs[:groups], refs[groups : groups + reps]
        weight_ref, gain_ref = refs[groups + reps], refs[groups + reps + 1]
        start = pl.multiple_of(rep_ref[0] * width, width)
        out_refs = refs[groups + reps + 2 : -5]
        left, right, own, total, sems = refs[-5:]
        copies = []
        for j in range(groups):
            line = [pltpu.make_async_copy(column_refs[j], left.at[j], sems.at[j, reps])]
            for e in range(reps):
                source = value_refs[e].at[j * tokens : (j + 1) * tokens, :]
                target = right.at[j, e * tokens : (e + 1) * tokens, :]
                line.append(pltpu.make_async_copy(source, target, sems.at[j, e]))
            for copy in line:
                copy.start()
            copies.append(line)
        copy = pltpu.make_async_copy(weight_ref.at[pl.ds(start, width), :], own, sems.at[groups, 0])
        copy.start()
        for j in range(groups):
            for c in copies[j]:
                c.wait()
            for c in range(count):
                block = left[j, :, c * chunk : (c + 1) * chunk]
                product = lax.dot_general(block, right[j], contract, preferred_element_type=f32)
                if j == 0:
                    total[c] = product
                else:
                    total[c] += product
        copy.wait()
        for c in range(count):
            at = slice(c * chunk, (c + 1) * chunk)
            raw = total[c]
            factor = gain_ref[:, pl.ds(pl.multiple_of(start + c * chunk, chunk), chunk)].astype(f32) * norm_scale
            factor = jnp.transpose(jnp.broadcast_to(factor, (128, chunk)))[:, 0:1]
            out_refs[c][:chunk, :] = (raw * factor).astype(bf16)
            dots = lax.dot_general(
                jnp.full((8, features), norm_scale, f32),
                raw * own[at, :].astype(f32),
                (((1,), (1,)), ((), ())),
                precision=lax.Precision.HIGHEST,
                preferred_element_type=f32,
            )
            under = jnp.concatenate([row[0:1, :].astype(f32) for row in thirds(dots)] + [jnp.zeros((13, chunk), f32)], axis=0)
            out_refs[c][chunk:, :chunk] = under.astype(bf16)
            out_refs[c][chunk:, chunk:] = jnp.zeros((16, features - chunk), bf16)

    return pl.pallas_call(
        kernel,
        out_shape=[jax.ShapeDtypeStruct((chunk + 16, features), bf16)] * count,
        in_specs=[SMEM_ARG] + [ANY_ARG] * (groups + reps + 1) + [pl.BlockSpec(memory_space=pltpu.VMEM)],
        scratch_shapes=[
            pltpu.VMEM((groups, rows, width), bf16),
            pltpu.VMEM((groups, rows, features), bf16),
            pltpu.VMEM((width, features), bf16),
            pltpu.VMEM((count, chunk, features), f32),
            pltpu.SemaphoreType.DMA((groups + 1, reps + 1)),
        ],
        compiler_params=params(16),
        cost_estimate=cost(2 * groups * rows * width * features, 2 * groups * rows * (width + features) + 4 * width * features),
        name="weight_product",
    )(rep, *columns, *values, weight, gain)


def returned_blocks(slots, weight, gain, micro):
    groups = len(slots)
    tokens, features = slots[0].shape
    rows = tokens // micro
    shard = weight.shape[0]
    tile = min(shard, 512)

    def kernel(*refs):
        slot_refs, weight_ref, gain_ref = refs[:groups], refs[groups], refs[groups + 1]
        out_refs = refs[groups + 2 :]
        factor = gain_ref[...].astype(f32)
        pair = 2 if groups % 2 == 0 else 1
        for j in range(0, groups, pair):
            values = jnp.concatenate([slot_refs[j + i][...] for i in range(pair)], axis=0)
            back = lax.dot_general(values, weight_ref[...], (((1,), (1,)), ((), ())), preferred_element_type=f32)
            back = (back * factor).astype(bf16)
            for i in range(pair):
                for m in range(micro):
                    at = i * tokens + m * rows
                    out_refs[(j + i) * micro + m][...] = back[at : at + rows, :]

    outs = pl.pallas_call(
        kernel,
        grid=(shard // tile,),
        out_shape=[jax.ShapeDtypeStruct((rows, shard), bf16)] * (groups * micro),
        in_specs=[pl.BlockSpec((tokens, features), lambda i: (0, 0))] * groups
        + [pl.BlockSpec((tile, features), lambda i: (i, 0)), pl.BlockSpec((1, tile), lambda i: (0, i))],
        out_specs=[pl.BlockSpec((rows, tile), lambda i: (0, i))] * (groups * micro),
        compiler_params=params(8),
        cost_estimate=cost(2 * groups * tokens * shard * features, 2 * groups * tokens * (shard + features) + 2 * shard * features),
        name="returned_blocks",
    )(*slots, weight, gain)
    return [list(outs[j * micro : (j + 1) * micro]) for j in range(groups)]


def row_gradient(x, top, blocks, me, m):
    groups = len(blocks)
    rows, shard = blocks[0].shape
    width = shard * groups
    step = 16

    def kernel(me_ref, x_ref, top_ref, *refs):
        block_refs, upper_ref, piece_ref = refs[:groups], refs[groups], refs[groups + 1]
        squares = jnp.zeros((step, 128), f32)
        dots = jnp.zeros((step, 128), f32)
        starts = [pl.multiple_of(lax.rem(me_ref[0] + j, groups) * shard, shard) for j in range(groups)]
        span = min(shard, 512)
        for j in range(groups):
            for c in range(0, shard, span):
                v = x_ref[0, 0, :, pl.ds(pl.multiple_of(starts[j] + c, span), span)].astype(f32)
                d = block_refs[j][:, c : c + span].astype(f32) * v
                v = v * v
                for k in range(0, span, 128):
                    squares = squares + v[:, k : k + 128]
                    dots = dots + d[:, k : k + 128]
        scale = lax.rsqrt(jnp.sum(squares, axis=1, keepdims=True) / width + norm_eps)
        mean = jnp.sum(dots, axis=1, keepdims=True) * scale / width
        slope = scale * mean
        for j in range(groups):
            for c in range(0, shard, span):
                at = pl.ds(pl.multiple_of(starts[j] + c, span), span)
                v = x_ref[0, 0, :, at].astype(f32)
                piece = (scale * (block_refs[j][:, c : c + span].astype(f32) - v * slope)).astype(bf16)
                piece_ref[:, at] = piece
                upper_ref[:, at] = (top_ref[0, :, at].astype(f32) + piece.astype(f32)).astype(bf16)

    return pl.pallas_call(
        kernel,
        grid=(rows // step,),
        out_shape=[jax.ShapeDtypeStruct((rows, width), bf16)] * 2,
        in_specs=[
            SMEM_ARG,
            pl.BlockSpec((1, 1, step, width), lambda i: (0, m, i, 0)),
            pl.BlockSpec((1, step, width), lambda i: (m, i, 0)),
        ]
        + [pl.BlockSpec((step, shard), lambda i: (i, 0))] * groups,
        out_specs=[pl.BlockSpec((step, width), lambda i: (i, 0))] * 2,
        compiler_params=params(8),
        cost_estimate=cost(12 * rows * width, 10 * rows * width),
        name="row_gradient",
    )(me, x, top, *blocks)


def input_gradient(upper, piece, passed, is_upper, shape, m, earlier):
    rows, width = upper.shape
    step = min(rows, 32)

    def kernel(is_upper_ref, upper_ref, piece_ref, passed_ref, *refs):
        lower = (passed_ref[...].astype(f32) + piece_ref[...].astype(f32)).astype(bf16)
        refs[-1][0, 0] = jnp.where(is_upper_ref[0] == 1, upper_ref[...], lower)

    spec = pl.BlockSpec((step, width), lambda i: (i, 0))
    return pl.pallas_call(
        kernel,
        grid=(rows // step,),
        out_shape=jax.ShapeDtypeStruct(shape, bf16),
        in_specs=[SMEM_ARG, spec, spec, spec] + [ANY_ARG] * len(earlier),
        out_specs=pl.BlockSpec((1, 1, step, width), lambda i: (0, m, i, 0)),
        input_output_aliases={4: 0} if earlier else {},
        compiler_params=params(8),
        cost_estimate=cost(4 * rows * width, 8 * rows * width),
        name="input_gradient",
    )(is_upper, upper, piece, passed, *earlier)


def finished_half(sums, rep, order, half, c, chunks, earlier):
    pieces = (1 << len(order)) // 2
    rows = sums.shape[0] // pieces - 16
    features = sums.shape[1]
    shard = rows * chunks * pieces * 2

    def place(i, rep_ref):
        return (rep_ref[0] ^ mask_of(i + half * pieces, order)) * chunks + c

    def total(under):
        return under[0:1, :rows] + under[1:2, :rows] + under[2:3, :rows]

    if rows % 128:
        earlier = earlier or (jnp.zeros((shard, features), f32), jnp.zeros((1, shard), f32))
        for i in range(pieces):
            piece = sums[i * (rows + 16) : (i + 1) * (rows + 16)].astype(f32)
            at = place(i, rep) * rows
            earlier = (
                lax.dynamic_update_slice(earlier[0], piece[:rows], (at, 0)),
                lax.dynamic_update_slice(earlier[1], total(piece[rows:]), (0, at)),
            )
        return earlier

    def kernel(rep_ref, sum_ref, *refs):
        refs[-2][...] = sum_ref[:rows, :].astype(f32)
        refs[-1][...] = total(sum_ref[rows:, :].astype(f32))

    return pl.pallas_call(
        kernel,
        grid_spec=pltpu.PrefetchScalarGridSpec(
            num_scalar_prefetch=1,
            grid=(pieces,),
            in_specs=[pl.BlockSpec((rows + 16, features), lambda i, rep_ref: (i, 0))] + [ANY_ARG] * len(earlier),
            out_specs=[
                pl.BlockSpec((rows, features), lambda i, rep_ref: (place(i, rep_ref), 0)),
                pl.BlockSpec((1, rows), lambda i, rep_ref: (0, place(i, rep_ref))),
            ],
        ),
        out_shape=[jax.ShapeDtypeStruct((shard, features), f32), jax.ShapeDtypeStruct((1, shard), f32)],
        input_output_aliases={2: 0, 3: 1} if earlier else {},
        compiler_params=params(8),
        cost_estimate=cost(sums.size, 6 * sums.size),
        name="finished_half",
    )(rep, sums, *earlier)


def local(layer_input, value_grad, value_weight, norm_gain, top_grad):
    groups = lax.axis_size("fsdp")
    reps = lax.axis_size("rep")
    bits = reps.bit_length() - 1
    me = lax.axis_index("fsdp").astype(jnp.int32)[None]
    rep = lax.axis_index("rep").astype(jnp.int32)[None]
    _, micro, rows, width = layer_input.shape
    tokens = micro * rows
    norm_scale = float(tokens * reps * groups) ** (-0.5)
    chunks = 2
    orders = [tuple(range(bits)), tuple(reversed(range(bits)))]

    weight = value_weight[0]
    is_upper = lax.axis_index("section").astype(jnp.int32)[None]
    inputs = after(layer_input[0].reshape(tokens, width), me, rep, is_upper)

    hats = scaled_blocks(inputs, me, rep, groups, reps, 1)[0]
    plane = list(hats)
    for e in range(1, reps):
        plane[e] = flipped(hats[e], "rep", e)
    grads = after(value_grad[0].reshape(tokens, -1), hats[0])
    slots = [grads] + [cyclic(grads, "fsdp", j) for j in range(1, groups)]

    plane[0] = after(plane[0], *slots[1:])
    sent = regrouped(plane, groups)
    back = returned_blocks(slots, weight, norm_gain, micro)
    columns = list(sent)
    for j in range(1, groups):
        columns[j] = cyclic(after(sent[j], back[0][0]) if j == groups - 1 else sent[j], "fsdp", j)
    held = after(joined(slots), sent[0])
    values = [held if e == 0 else flipped(held, "rep", e) for e in range(reps)]

    lines = [[back[j][m] for j in range(groups)] for m in range(micro)]
    far = groups // 2
    near = [(m, j) for m in range(micro) for j in range(1, groups) if j != far]
    for chain in (near, [(m, far) for m in range(micro)]):
        ties = [columns[1]]
        for m, j in chain:
            lines[m][j] = cyclic(after(lines[m][j], *ties), "fsdp", -j)
            ties = [lines[m][j]]
    columns[0] = after(columns[0], lines[0][1])
    sums = weight_product(columns, values, weight, norm_gain, rep, groups, chunks, norm_scale)
    gathered = [doubled(sums[c], orders[c]) for c in range(chunks)]
    finished = ()
    for half in (0, 1):
        for c in range(chunks):
            finished = finished_half(gathered[c][half], rep, orders[c], half, c, chunks, finished)
        if half == 0:
            early = finished
    weight_grad, gain_grad = finished

    result = ()
    for m in range(micro):
        ties = [lines[-1][1], *[g[0] for g in gathered]] if m == 0 else [*finished, *result]
        lines[m][0] = after(lines[m][0], *ties)
        upper, piece = row_gradient(layer_input, top_grad, lines[m], me, m)
        passed = lax.ppermute(upper, "section", [(1, 0)])
        result = (input_gradient(upper, piece, passed, is_upper, layer_input.shape, m, result),)
    return (result[0], weight_grad[None], gain_grad)


def solution(mesh):
    return jax.shard_map(
        local,
        mesh=mesh,
        in_specs=(
            P("section", None, ("rep", "fsdp"), None),
            P("section", None, ("rep", "fsdp"), None),
            P("section", "fsdp", None),
            P("section", "fsdp"),
            P(None, ("rep", "fsdp"), None),
        ),
        out_specs=(
            P("section", None, ("rep", "fsdp"), None),
            P("section", "fsdp", None),
            P("section", "fsdp"),
        ),
        check_vma=False,
    )
```

```python
import jax
import jax.numpy as jnp
from jax import lax
from jax.experimental import pallas as pl
from jax.experimental.pallas import tpu as pltpu
from jax.sharding import PartitionSpec as P

norm_eps = 1e-05
bf16 = jnp.bfloat16
f32 = jnp.float32
MIB = 1 << 20
SMEM_ARG = pl.BlockSpec(memory_space=pltpu.SMEM)
ANY_ARG = pl.BlockSpec(memory_space=pl.ANY)


def cyclic(value, axis, steps):
    count = lax.axis_size(axis)
    return lax.ppermute(value, axis, [(i, (i + steps) % count) for i in range(count)])


def flipped(value, axis, mask):
    count = lax.axis_size(axis)
    return lax.ppermute(value, axis, [(i, i ^ mask) for i in range(count)])


def after(value, *others):
    return lax.optimization_barrier((value, *others))[0]


def params(mib):
    return pltpu.CompilerParams(vmem_limit_bytes=mib * MIB)


def cost(flops, bytes_accessed):
    return pl.CostEstimate(flops=int(flops), bytes_accessed=int(bytes_accessed), transcendentals=0)


def scaled_blocks(x, me, rep, groups, reps, chunks):
    tokens, width = x.shape
    shard = width // groups
    piece = shard // reps
    chunk = piece // chunks
    if chunk % 128:
        x = x.astype(f32)
        hat = (x * lax.rsqrt(jnp.mean(x * x, axis=1, keepdims=True) + norm_eps)).astype(bf16)
        hat = jnp.roll(hat.reshape(tokens, groups, reps, chunks, chunk), -me[0], axis=1)
        take = lambda e, c: lax.dynamic_index_in_dim(hat, rep[0] ^ e, 2, False)[:, :, c].reshape(tokens, groups * chunk)
        return [[take(e, c) for e in range(reps)] for c in range(chunks)]
    step = 16
    block = min(tokens, 32)

    def kernel(me_ref, rep_ref, x_ref, *out_refs):
        span = min(shard, 512)
        for row in range(0, block, step):
            rows = slice(row, row + step)
            total = jnp.zeros((step, 128), f32)
            for c in range(0, width, span):
                v = x_ref[rows, c : c + span].astype(f32)
                v = v * v
                for k in range(0, span, 128):
                    total = total + v[:, k : k + 128]
            scale = lax.rsqrt(jnp.sum(total, axis=1, keepdims=True) / width + norm_eps)
            for c in range(chunks):
                for e in range(reps):
                    for j in range(groups):
                        at = lax.rem(me_ref[0] + j, groups) * shard + (rep_ref[0] ^ e) * piece + c * chunk
                        v = x_ref[rows, pl.ds(pl.multiple_of(at, chunk), chunk)].astype(f32)
                        out_refs[c * reps + e][rows, j * chunk : (j + 1) * chunk] = (v * scale).astype(bf16)

    outs = pl.pallas_call(
        kernel,
        grid=(tokens // block,),
        out_shape=[jax.ShapeDtypeStruct((tokens, groups * chunk), bf16)] * (chunks * reps),
        in_specs=[SMEM_ARG, SMEM_ARG, pl.BlockSpec((block, width), lambda i: (i, 0))],
        out_specs=[pl.BlockSpec((block, groups * chunk), lambda i: (i, 0))] * (chunks * reps),
        compiler_params=params(8),
        cost_estimate=cost(6 * x.size, 4 * x.size),
        name="scaled_blocks",
    )(me, rep, x)
    return [list(outs[c * reps : (c + 1) * reps]) for c in range(chunks)]


def joined(arrays):
    rows, width = arrays[0].shape
    if rows % 16 or width % 128:
        return jnp.concatenate(arrays, axis=0)

    def kernel(*refs):
        copies = []
        for k in range(len(arrays)):
            target = refs[-2].at[k * rows : (k + 1) * rows, :]
            copies.append(pltpu.make_async_copy(refs[k], target, refs[-1].at[k]))
            copies[-1].start()
        for copy in copies:
            copy.wait()

    return pl.pallas_call(
        kernel,
        out_shape=jax.ShapeDtypeStruct((len(arrays) * rows, width), bf16),
        in_specs=[ANY_ARG] * len(arrays),
        out_specs=ANY_ARG,
        scratch_shapes=[pltpu.SemaphoreType.DMA((len(arrays),))],
        compiler_params=params(4),
        cost_estimate=cost(0, 4 * len(arrays) * rows * width),
        name="joined",
    )(*arrays)


def doubled(value, order):
    for bit in order[:-1]:
        value = joined([value, flipped(value, "rep", 1 << bit)])
    return value, flipped(value, "rep", 1 << order[-1])


def mask_of(pos, order):
    return sum(((pos >> i) & 1) << bit for i, bit in enumerate(order))


def regrouped(blocks, groups):
    tokens, width = blocks[0].shape
    chunk = width // groups
    reps = len(blocks)
    if chunk % 128:
        return [jnp.concatenate([b[:, j * chunk : (j + 1) * chunk] for b in blocks], axis=0) for j in range(groups)]

    def kernel(*refs):
        copies = []
        for e in range(reps):
            for j in range(groups):
                source = refs[e].at[:, j * chunk : (j + 1) * chunk]
                target = refs[reps + j].at[e * tokens : (e + 1) * tokens, :]
                copies.append(pltpu.make_async_copy(source, target, refs[-1].at[e * groups + j]))
                copies[-1].start()
        for copy in copies:
            copy.wait()

    return list(
        pl.pallas_call(
            kernel,
            out_shape=[jax.ShapeDtypeStruct((reps * tokens, chunk), bf16)] * groups,
            in_specs=[ANY_ARG] * reps,
            out_specs=[ANY_ARG] * groups,
            scratch_shapes=[pltpu.SemaphoreType.DMA((reps * groups,))],
            compiler_params=params(8),
            cost_estimate=cost(0, 4 * reps * tokens * width),
            name="regrouped",
        )(*blocks)
    )


def weight_product(columns, values, weight, gain, rep, groups, count, norm_scale):
    rows, width = columns[0].shape
    reps = len(values)
    tokens = rows // reps
    features = values[0].shape[1]
    chunk = width // count
    contract = (((0,), (0,)), ((), ()))

    def thirds(row):
        first = row.astype(bf16)
        rest = row - first.astype(f32)
        second = rest.astype(bf16)
        return first, second, (rest - second.astype(f32)).astype(bf16)

    if chunk % 128:
        order = jnp.stack([v.reshape(groups, tokens, features) for v in values], axis=1)
        raw = lax.dot_general(
            jnp.concatenate(columns, axis=0), order.reshape(-1, features), contract, preferred_element_type=f32
        )
        own = lax.dynamic_slice_in_dim(weight, rep[0] * width, width, 0).astype(f32)
        dots = jnp.sum(raw * own, axis=1) * norm_scale
        factor = lax.dynamic_slice_in_dim(gain[0], rep[0] * width, width, 0).astype(f32) * norm_scale
        raw = (raw * factor[:, None]).astype(bf16)
        outs = []
        for c in range(count):
            at = slice(c * chunk, (c + 1) * chunk)
            under = jnp.stack(thirds(dots[at]) + (jnp.zeros((chunk,), bf16),) * 13)
            outs.append(jnp.concatenate([raw[at], jnp.pad(under, ((0, 0), (0, features - chunk)))], axis=0))
        return outs

    def kernel(rep_ref, *refs):
        column_refs, value_refs = refs[:groups], refs[groups : groups + reps]
        weight_ref, gain_ref = refs[groups + reps], refs[groups + reps + 1]
        out_refs, total = refs[groups + reps + 2 : -1], refs[-1]
        start = pl.multiple_of(rep_ref[0] * width, width)
        for j in range(groups):
            right = jnp.concatenate([v[j * tokens : (j + 1) * tokens, :] for v in value_refs], axis=0)
            for c in range(count):
                block = column_refs[j][:, c * chunk : (c + 1) * chunk]
                product = lax.dot_general(block, right, contract, preferred_element_type=f32)
                if j == 0:
                    total[c] = product
                else:
                    total[c] += product
        for c in range(count):
            at = pl.ds(pl.multiple_of(start + c * chunk, chunk), chunk)
            raw = total[c]
            factor = gain_ref[:, at].astype(f32) * norm_scale
            factor = jnp.transpose(jnp.broadcast_to(factor, (128, chunk)))[:, 0:1]
            out_refs[c][:chunk, :] = (raw * factor).astype(bf16)
            terms = raw * weight_ref[at, :].astype(f32)
            terms = sum(terms[:, k : k + 128] for k in range(0, features, 128))
            dots = lax.dot_general(
                jnp.full((8, 128), norm_scale, f32),
                terms,
                (((1,), (1,)), ((), ())),
                precision=lax.Precision.HIGHEST,
                preferred_element_type=f32,
            )
            under = jnp.concatenate([row[0:1, :].astype(f32) for row in thirds(dots)] + [jnp.zeros((13, chunk), f32)], axis=0)
            out_refs[c][chunk:, :chunk] = under.astype(bf16)
            out_refs[c][chunk:, chunk:] = jnp.zeros((16, features - chunk), bf16)

    vmem = pl.BlockSpec(memory_space=pltpu.VMEM)
    return pl.pallas_call(
        kernel,
        out_shape=[jax.ShapeDtypeStruct((chunk + 16, features), bf16)] * count,
        in_specs=[SMEM_ARG] + [vmem] * (groups + reps + 2),
        out_specs=[vmem] * count,
        scratch_shapes=[pltpu.VMEM((count, chunk, features), f32)],
        compiler_params=params(24),
        cost_estimate=cost(2 * groups * rows * width * features, 2 * groups * rows * (width + features) + 4 * width * features),
        name="weight_product",
    )(rep, *columns, *values, weight, gain)


def returned_blocks(slots, weight, gain, micro):
    groups = len(slots)
    tokens, features = slots[0].shape
    rows = tokens // micro
    shard = weight.shape[0]
    tile = min(shard, 512)

    def kernel(*refs):
        slot_refs, weight_ref, gain_ref = refs[:groups], refs[groups], refs[groups + 1]
        out_refs = refs[groups + 2 :]
        factor = gain_ref[...].astype(f32)
        pair = 2 if groups % 2 == 0 else 1
        for j in range(0, groups, pair):
            values = jnp.concatenate([slot_refs[j + i][...] for i in range(pair)], axis=0)
            back = lax.dot_general(values, weight_ref[...], (((1,), (1,)), ((), ())), preferred_element_type=f32)
            back = (back * factor).astype(bf16)
            for i in range(pair):
                for m in range(micro):
                    at = i * tokens + m * rows
                    out_refs[(j + i) * micro + m][...] = back[at : at + rows, :]

    outs = pl.pallas_call(
        kernel,
        grid=(shard // tile,),
        out_shape=[jax.ShapeDtypeStruct((rows, shard), bf16)] * (groups * micro),
        in_specs=[pl.BlockSpec((tokens, features), lambda i: (0, 0))] * groups
        + [pl.BlockSpec((tile, features), lambda i: (i, 0)), pl.BlockSpec((1, tile), lambda i: (0, i))],
        out_specs=[pl.BlockSpec((rows, tile), lambda i: (0, i))] * (groups * micro),
        compiler_params=params(8),
        cost_estimate=cost(2 * groups * tokens * shard * features, 2 * groups * tokens * (shard + features) + 2 * shard * features),
        name="returned_blocks",
    )(*slots, weight, gain)
    return [list(outs[j * micro : (j + 1) * micro]) for j in range(groups)]


def row_gradient(x, top, blocks, me, m):
    groups = len(blocks)
    rows, shard = blocks[0].shape
    width = shard * groups
    step = 16

    def kernel(me_ref, x_ref, top_ref, *refs):
        block_refs, upper_ref, piece_ref = refs[:groups], refs[groups], refs[groups + 1]
        squares = jnp.zeros((step, 128), f32)
        dots = jnp.zeros((step, 128), f32)
        starts = [pl.multiple_of(lax.rem(me_ref[0] + j, groups) * shard, shard) for j in range(groups)]
        span = min(shard, 512)
        for j in range(groups):
            for c in range(0, shard, span):
                v = x_ref[0, 0, :, pl.ds(pl.multiple_of(starts[j] + c, span), span)].astype(f32)
                d = block_refs[j][:, c : c + span].astype(f32) * v
                v = v * v
                for k in range(0, span, 128):
                    squares = squares + v[:, k : k + 128]
                    dots = dots + d[:, k : k + 128]
        scale = lax.rsqrt(jnp.sum(squares, axis=1, keepdims=True) / width + norm_eps)
        mean = jnp.sum(dots, axis=1, keepdims=True) * scale / width
        slope = scale * mean
        for j in range(groups):
            for c in range(0, shard, span):
                at = pl.ds(pl.multiple_of(starts[j] + c, span), span)
                v = x_ref[0, 0, :, at].astype(f32)
                piece = (scale * (block_refs[j][:, c : c + span].astype(f32) - v * slope)).astype(bf16)
                piece_ref[:, at] = piece
                upper_ref[:, at] = (top_ref[0, :, at].astype(f32) + piece.astype(f32)).astype(bf16)

    return pl.pallas_call(
        kernel,
        grid=(rows // step,),
        out_shape=[jax.ShapeDtypeStruct((rows, width), bf16)] * 2,
        in_specs=[
            SMEM_ARG,
            pl.BlockSpec((1, 1, step, width), lambda i: (0, m, i, 0)),
            pl.BlockSpec((1, step, width), lambda i: (m, i, 0)),
        ]
        + [pl.BlockSpec((step, shard), lambda i: (i, 0))] * groups,
        out_specs=[pl.BlockSpec((step, width), lambda i: (i, 0))] * 2,
        compiler_params=params(8),
        cost_estimate=cost(12 * rows * width, 10 * rows * width),
        name="row_gradient",
    )(me, x, top, *blocks)


def input_gradient(upper, piece, passed, is_upper, shape, m, earlier):
    rows, width = upper.shape
    step = min(rows, 32)

    def kernel(is_upper_ref, upper_ref, piece_ref, passed_ref, *refs):
        lower = (passed_ref[...].astype(f32) + piece_ref[...].astype(f32)).astype(bf16)
        refs[-1][0, 0] = jnp.where(is_upper_ref[0] == 1, upper_ref[...], lower)

    spec = pl.BlockSpec((step, width), lambda i: (i, 0))
    return pl.pallas_call(
        kernel,
        grid=(rows // step,),
        out_shape=jax.ShapeDtypeStruct(shape, bf16),
        in_specs=[SMEM_ARG, spec, spec, spec] + [ANY_ARG] * len(earlier),
        out_specs=pl.BlockSpec((1, 1, step, width), lambda i: (0, m, i, 0)),
        input_output_aliases={4: 0} if earlier else {},
        compiler_params=params(8),
        cost_estimate=cost(4 * rows * width, 8 * rows * width),
        name="input_gradient",
    )(is_upper, upper, piece, passed, *earlier)


def finished_half(sums, rep, order, half, c, chunks, earlier):
    pieces = (1 << len(order)) // 2
    rows = sums.shape[0] // pieces - 16
    features = sums.shape[1]
    shard = rows * chunks * pieces * 2

    def place(i, rep_ref):
        return (rep_ref[0] ^ mask_of(i + half * pieces, order)) * chunks + c

    def total(under):
        return under[0:1, :rows] + under[1:2, :rows] + under[2:3, :rows]

    if rows % 128:
        earlier = earlier or (jnp.zeros((shard, features), f32), jnp.zeros((1, shard), f32))
        for i in range(pieces):
            piece = sums[i * (rows + 16) : (i + 1) * (rows + 16)].astype(f32)
            at = place(i, rep) * rows
            earlier = (
                lax.dynamic_update_slice(earlier[0], piece[:rows], (at, 0)),
                lax.dynamic_update_slice(earlier[1], total(piece[rows:]), (0, at)),
            )
        return earlier

    def kernel(rep_ref, sum_ref, *refs):
        refs[-2][...] = sum_ref[:rows, :].astype(f32)
        refs[-1][...] = total(sum_ref[rows:, :].astype(f32))

    return pl.pallas_call(
        kernel,
        grid_spec=pltpu.PrefetchScalarGridSpec(
            num_scalar_prefetch=1,
            grid=(pieces,),
            in_specs=[pl.BlockSpec((rows + 16, features), lambda i, rep_ref: (i, 0))] + [ANY_ARG] * len(earlier),
            out_specs=[
                pl.BlockSpec((rows, features), lambda i, rep_ref: (place(i, rep_ref), 0)),
                pl.BlockSpec((1, rows), lambda i, rep_ref: (0, place(i, rep_ref))),
            ],
        ),
        out_shape=[jax.ShapeDtypeStruct((shard, features), f32), jax.ShapeDtypeStruct((1, shard), f32)],
        input_output_aliases={2: 0, 3: 1} if earlier else {},
        compiler_params=params(8),
        cost_estimate=cost(sums.size, 6 * sums.size),
        name="finished_half",
    )(rep, sums, *earlier)


def local(layer_input, value_grad, value_weight, norm_gain, top_grad):
    groups = lax.axis_size("fsdp")
    reps = lax.axis_size("rep")
    bits = reps.bit_length() - 1
    me = lax.axis_index("fsdp").astype(jnp.int32)[None]
    rep = lax.axis_index("rep").astype(jnp.int32)[None]
    _, micro, rows, width = layer_input.shape
    tokens = micro * rows
    norm_scale = float(tokens * reps * groups) ** (-0.5)
    chunks = 2
    orders = [tuple(range(bits)), tuple(reversed(range(bits)))]

    weight = value_weight[0]
    is_upper = lax.axis_index("section").astype(jnp.int32)[None]
    inputs = after(layer_input[0].reshape(tokens, width), me, rep, is_upper)

    hats = scaled_blocks(inputs, me, rep, groups, reps, 1)[0]
    plane = list(hats)
    for e in range(1, reps):
        plane[e] = flipped(hats[e], "rep", e)
    grads = after(value_grad[0].reshape(tokens, -1), hats[0])
    slots = [grads] + [cyclic(grads, "fsdp", j) for j in range(1, groups)]

    plane[0] = after(plane[0], *slots[1:])
    sent = regrouped(plane, groups)
    back = returned_blocks(slots, weight, norm_gain, micro)
    lines = [[back[j][m] for j in range(groups)] for m in range(micro)]
    far = groups // 2
    near = [j for j in range(1, groups) if j != far]
    columns = list(sent)
    columns[far] = cyclic(sent[far], "fsdp", far)
    columns[near[0]] = cyclic(sent[near[0]], "fsdp", near[0])
    for j in near[1:]:
        columns[j] = cyclic(after(sent[j], back[0][0], columns[near[0]]), "fsdp", j)
    held = after(joined(slots), sent[0])
    values = [held if e == 0 else flipped(held, "rep", e) for e in range(reps)]

    def send_back(m, j, *ties):
        lines[m][j] = cyclic(after(lines[m][j], *ties), "fsdp", -j)

    send_back(0, near[0], columns[far])
    for m, j in [(0, far), *((0, j) for j in near[1:]), (1, near[0])]:
        send_back(m, j, columns[near[-1]])
    for j in [far, *near[1:]]:
        send_back(1, j, *lines[0][1:], lines[1][near[0]])
    columns[0] = after(columns[0], lines[0][near[0]])
    sums = weight_product(columns, values, weight, norm_gain, rep, groups, chunks, norm_scale)
    gathered = [doubled(sums[c], orders[c]) for c in range(chunks)]
    finished = ()
    for half in (0, 1):
        for c in range(chunks):
            finished = finished_half(gathered[c][half], rep, orders[c], half, c, chunks, finished)
        if half == 0:
            early = finished
    weight_grad, gain_grad = finished

    result = ()
    for m in range(micro):
        ties = [lines[-1][near[0]], *[g[0] for g in gathered]] if m == 0 else [*finished, *result]
        lines[m][0] = after(lines[m][0], *ties)
        upper, piece = row_gradient(layer_input, top_grad, lines[m], me, m)
        passed = lax.ppermute(upper, "section", [(1, 0)])
        result = (input_gradient(upper, piece, passed, is_upper, layer_input.shape, m, result),)
    return (result[0], weight_grad[None], gain_grad)


def solution(mesh):
    return jax.shard_map(
        local,
        mesh=mesh,
        in_specs=(
            P("section", None, ("rep", "fsdp"), None),
            P("section", None, ("rep", "fsdp"), None),
            P("section", "fsdp", None),
            P("section", "fsdp"),
            P(None, ("rep", "fsdp"), None),
        ),
        out_specs=(
            P("section", None, ("rep", "fsdp"), None),
            P("section", "fsdp", None),
            P("section", "fsdp"),
        ),
        check_vma=False,
    )
```

```python
import jax
import jax.numpy as jnp
from jax import lax
from jax.experimental import pallas as pl
from jax.experimental.pallas import tpu as pltpu
from jax.sharding import PartitionSpec as P

norm_eps = 1e-05
bf16 = jnp.bfloat16
f32 = jnp.float32
MIB = 1 << 20
SMEM_ARG = pl.BlockSpec(memory_space=pltpu.SMEM)
ANY_ARG = pl.BlockSpec(memory_space=pl.ANY)


def cyclic(value, axis, steps):
    count = lax.axis_size(axis)
    return lax.ppermute(value, axis, [(i, (i + steps) % count) for i in range(count)])


def flipped(value, axis, mask):
    count = lax.axis_size(axis)
    return lax.ppermute(value, axis, [(i, i ^ mask) for i in range(count)])


def after(value, *others):
    return lax.optimization_barrier((value, *others))[0]


def params(mib):
    return pltpu.CompilerParams(vmem_limit_bytes=mib * MIB)


def cost(flops, bytes_accessed):
    return pl.CostEstimate(flops=int(flops), bytes_accessed=int(bytes_accessed), transcendentals=0)


def scaled_blocks(x, me, rep, groups, reps, chunks):
    tokens, width = x.shape
    shard = width // groups
    piece = shard // reps
    chunk = piece // chunks
    if chunk % 128:
        x = x.astype(f32)
        hat = (x * lax.rsqrt(jnp.mean(x * x, axis=1, keepdims=True) + norm_eps)).astype(bf16)
        hat = jnp.roll(hat.reshape(tokens, groups, reps, chunks, chunk), -me[0], axis=1)
        take = lambda e, c: lax.dynamic_index_in_dim(hat, rep[0] ^ e, 2, False)[:, :, c].reshape(tokens, groups * chunk)
        return [[take(e, c) for e in range(reps)] for c in range(chunks)]
    step = 16
    block = min(tokens, 32)

    def kernel(me_ref, rep_ref, x_ref, *out_refs):
        span = min(shard, 512)
        for row in range(0, block, step):
            rows = slice(row, row + step)
            total = jnp.zeros((step, 128), f32)
            for c in range(0, width, span):
                v = x_ref[rows, c : c + span].astype(f32)
                v = v * v
                for k in range(0, span, 128):
                    total = total + v[:, k : k + 128]
            scale = lax.rsqrt(jnp.sum(total, axis=1, keepdims=True) / width + norm_eps)
            for c in range(chunks):
                for e in range(reps):
                    for j in range(groups):
                        at = lax.rem(me_ref[0] + j, groups) * shard + (rep_ref[0] ^ e) * piece + c * chunk
                        v = x_ref[rows, pl.ds(pl.multiple_of(at, chunk), chunk)].astype(f32)
                        out_refs[c * reps + e][rows, j * chunk : (j + 1) * chunk] = (v * scale).astype(bf16)

    outs = pl.pallas_call(
        kernel,
        grid=(tokens // block,),
        out_shape=[jax.ShapeDtypeStruct((tokens, groups * chunk), bf16)] * (chunks * reps),
        in_specs=[SMEM_ARG, SMEM_ARG, pl.BlockSpec((block, width), lambda i: (i, 0))],
        out_specs=[pl.BlockSpec((block, groups * chunk), lambda i: (i, 0))] * (chunks * reps),
        compiler_params=params(8),
        cost_estimate=cost(6 * x.size, 4 * x.size),
        name="scaled_blocks",
    )(me, rep, x)
    return [list(outs[c * reps : (c + 1) * reps]) for c in range(chunks)]


def joined(arrays):
    rows, width = arrays[0].shape
    if rows % 16 or width % 128:
        return jnp.concatenate(arrays, axis=0)

    def kernel(*refs):
        copies = []
        for k in range(len(arrays)):
            target = refs[-2].at[k * rows : (k + 1) * rows, :]
            copies.append(pltpu.make_async_copy(refs[k], target, refs[-1].at[k]))
            copies[-1].start()
        for copy in copies:
            copy.wait()

    return pl.pallas_call(
        kernel,
        out_shape=jax.ShapeDtypeStruct((len(arrays) * rows, width), bf16),
        in_specs=[ANY_ARG] * len(arrays),
        out_specs=ANY_ARG,
        scratch_shapes=[pltpu.SemaphoreType.DMA((len(arrays),))],
        compiler_params=params(4),
        cost_estimate=cost(0, 4 * len(arrays) * rows * width),
        name="joined",
    )(*arrays)


def doubled(value, order):
    for bit in order[:-1]:
        value = joined([value, flipped(value, "rep", 1 << bit)])
    return value, flipped(value, "rep", 1 << order[-1])


def mask_of(pos, order):
    return sum(((pos >> i) & 1) << bit for i, bit in enumerate(order))


def regrouped(blocks, groups):
    tokens, width = blocks[0].shape
    chunk = width // groups
    reps = len(blocks)
    if chunk % 128:
        return [jnp.concatenate([b[:, j * chunk : (j + 1) * chunk] for b in blocks], axis=0) for j in range(groups)]

    def kernel(*refs):
        copies = []
        for e in range(reps):
            for j in range(groups):
                source = refs[e].at[:, j * chunk : (j + 1) * chunk]
                target = refs[reps + j].at[e * tokens : (e + 1) * tokens, :]
                copies.append(pltpu.make_async_copy(source, target, refs[-1].at[e * groups + j]))
                copies[-1].start()
        for copy in copies:
            copy.wait()

    return list(
        pl.pallas_call(
            kernel,
            out_shape=[jax.ShapeDtypeStruct((reps * tokens, chunk), bf16)] * groups,
            in_specs=[ANY_ARG] * reps,
            out_specs=[ANY_ARG] * groups,
            scratch_shapes=[pltpu.SemaphoreType.DMA((reps * groups,))],
            compiler_params=params(8),
            cost_estimate=cost(0, 4 * reps * tokens * width),
            name="regrouped",
        )(*blocks)
    )


def weight_product(columns, values, weight, gain, rep, groups, count, norm_scale):
    rows, width = columns[0].shape
    reps = len(values)
    tokens = rows // reps
    features = values[0].shape[1]
    chunk = width // count
    contract = (((0,), (0,)), ((), ()))

    def thirds(row):
        first = row.astype(bf16)
        rest = row - first.astype(f32)
        second = rest.astype(bf16)
        return first, second, (rest - second.astype(f32)).astype(bf16)

    if chunk % 128:
        order = jnp.stack([v.reshape(groups, tokens, features) for v in values], axis=1)
        raw = lax.dot_general(
            jnp.concatenate(columns, axis=0), order.reshape(-1, features), contract, preferred_element_type=f32
        )
        own = lax.dynamic_slice_in_dim(weight, rep[0] * width, width, 0).astype(f32)
        dots = jnp.sum(raw * own, axis=1) * norm_scale
        factor = lax.dynamic_slice_in_dim(gain[0], rep[0] * width, width, 0).astype(f32) * norm_scale
        raw = (raw * factor[:, None]).astype(bf16)
        outs = []
        for c in range(count):
            at = slice(c * chunk, (c + 1) * chunk)
            under = jnp.stack(thirds(dots[at]) + (jnp.zeros((chunk,), bf16),) * 13)
            outs.append(jnp.concatenate([raw[at], jnp.pad(under, ((0, 0), (0, features - chunk)))], axis=0))
        return outs

    def kernel(rep_ref, *refs):
        column_refs, value_refs = refs[:groups], refs[groups : groups + reps]
        weight_ref, gain_ref = refs[groups + reps], refs[groups + reps + 1]
        out_refs, total = refs[groups + reps + 2 : -1], refs[-1]
        start = pl.multiple_of(rep_ref[0] * width, width)
        for j in range(groups):
            right = jnp.concatenate([v[j * tokens : (j + 1) * tokens, :] for v in value_refs], axis=0)
            for c in range(count):
                block = column_refs[j][:, c * chunk : (c + 1) * chunk]
                product = lax.dot_general(block, right, contract, preferred_element_type=f32)
                if j == 0:
                    total[c] = product
                else:
                    total[c] += product
        for c in range(count):
            at = pl.ds(pl.multiple_of(start + c * chunk, chunk), chunk)
            raw = total[c]
            factor = gain_ref[:, at].astype(f32) * norm_scale
            factor = jnp.transpose(jnp.broadcast_to(factor, (128, chunk)))[:, 0:1]
            out_refs[c][:chunk, :] = (raw * factor).astype(bf16)
            terms = raw * weight_ref[at, :].astype(f32)
            terms = sum(terms[:, k : k + 128] for k in range(0, features, 128))
            dots = lax.dot_general(
                jnp.full((8, 128), norm_scale, f32),
                terms,
                (((1,), (1,)), ((), ())),
                precision=lax.Precision.HIGHEST,
                preferred_element_type=f32,
            )
            under = jnp.concatenate([row[0:1, :].astype(f32) for row in thirds(dots)] + [jnp.zeros((13, chunk), f32)], axis=0)
            out_refs[c][chunk:, :chunk] = under.astype(bf16)
            out_refs[c][chunk:, chunk:] = jnp.zeros((16, features - chunk), bf16)

    vmem = pl.BlockSpec(memory_space=pltpu.VMEM)
    return pl.pallas_call(
        kernel,
        out_shape=[jax.ShapeDtypeStruct((chunk + 16, features), bf16)] * count,
        in_specs=[SMEM_ARG] + [vmem] * (groups + reps + 2),
        out_specs=[vmem] * count,
        scratch_shapes=[pltpu.VMEM((count, chunk, features), f32)],
        compiler_params=params(24),
        cost_estimate=cost(2 * groups * rows * width * features, 2 * groups * rows * (width + features) + 4 * width * features),
        name="weight_product",
    )(rep, *columns, *values, weight, gain)


def returned_blocks(slots, weight, gain, micro):
    groups = len(slots)
    tokens, features = slots[0].shape
    rows = tokens // micro
    shard = weight.shape[0]
    tile = min(shard, 512)

    def kernel(*refs):
        slot_refs, weight_ref, gain_ref = refs[:groups], refs[groups], refs[groups + 1]
        out_refs = refs[groups + 2 :]
        factor = gain_ref[...].astype(f32)
        pair = 2 if groups % 2 == 0 else 1
        for j in range(0, groups, pair):
            values = jnp.concatenate([slot_refs[j + i][...] for i in range(pair)], axis=0)
            back = lax.dot_general(values, weight_ref[...], (((1,), (1,)), ((), ())), preferred_element_type=f32)
            back = (back * factor).astype(bf16)
            for i in range(pair):
                for m in range(micro):
                    at = i * tokens + m * rows
                    out_refs[(j + i) * micro + m][...] = back[at : at + rows, :]

    outs = pl.pallas_call(
        kernel,
        grid=(shard // tile,),
        out_shape=[jax.ShapeDtypeStruct((rows, shard), bf16)] * (groups * micro),
        in_specs=[pl.BlockSpec((tokens, features), lambda i: (0, 0))] * groups
        + [pl.BlockSpec((tile, features), lambda i: (i, 0)), pl.BlockSpec((1, tile), lambda i: (0, i))],
        out_specs=[pl.BlockSpec((rows, tile), lambda i: (0, i))] * (groups * micro),
        compiler_params=params(8),
        cost_estimate=cost(2 * groups * tokens * shard * features, 2 * groups * tokens * (shard + features) + 2 * shard * features),
        name="returned_blocks",
    )(*slots, weight, gain)
    return [list(outs[j * micro : (j + 1) * micro]) for j in range(groups)]


def row_gradient(x, top, blocks, me, m):
    groups = len(blocks)
    rows, shard = blocks[0].shape
    width = shard * groups
    step = 16

    def kernel(me_ref, x_ref, top_ref, *refs):
        block_refs, upper_ref, piece_ref = refs[:groups], refs[groups], refs[groups + 1]
        squares = jnp.zeros((step, 128), f32)
        dots = jnp.zeros((step, 128), f32)
        starts = [pl.multiple_of(lax.rem(me_ref[0] + j, groups) * shard, shard) for j in range(groups)]
        span = min(shard, 512)
        for j in range(groups):
            for c in range(0, shard, span):
                v = x_ref[0, 0, :, pl.ds(pl.multiple_of(starts[j] + c, span), span)].astype(f32)
                d = block_refs[j][:, c : c + span].astype(f32) * v
                v = v * v
                for k in range(0, span, 128):
                    squares = squares + v[:, k : k + 128]
                    dots = dots + d[:, k : k + 128]
        scale = lax.rsqrt(jnp.sum(squares, axis=1, keepdims=True) / width + norm_eps)
        mean = jnp.sum(dots, axis=1, keepdims=True) * scale / width
        slope = scale * mean
        for j in range(groups):
            for c in range(0, shard, span):
                at = pl.ds(pl.multiple_of(starts[j] + c, span), span)
                v = x_ref[0, 0, :, at].astype(f32)
                piece = (scale * (block_refs[j][:, c : c + span].astype(f32) - v * slope)).astype(bf16)
                piece_ref[:, at] = piece
                upper_ref[:, at] = (top_ref[0, :, at].astype(f32) + piece.astype(f32)).astype(bf16)

    return pl.pallas_call(
        kernel,
        grid=(rows // step,),
        out_shape=[jax.ShapeDtypeStruct((rows, width), bf16)] * 2,
        in_specs=[
            SMEM_ARG,
            pl.BlockSpec((1, 1, step, width), lambda i: (0, m, i, 0)),
            pl.BlockSpec((1, step, width), lambda i: (m, i, 0)),
        ]
        + [pl.BlockSpec((step, shard), lambda i: (i, 0))] * groups,
        out_specs=[pl.BlockSpec((step, width), lambda i: (i, 0))] * 2,
        compiler_params=params(8),
        cost_estimate=cost(12 * rows * width, 10 * rows * width),
        name="row_gradient",
    )(me, x, top, *blocks)


def input_gradient(upper, piece, passed, is_upper, shape, m, earlier):
    rows, width = upper.shape
    step = min(rows, 32)

    def kernel(is_upper_ref, upper_ref, piece_ref, passed_ref, *refs):
        lower = (passed_ref[...].astype(f32) + piece_ref[...].astype(f32)).astype(bf16)
        refs[-1][0, 0] = jnp.where(is_upper_ref[0] == 1, upper_ref[...], lower)

    spec = pl.BlockSpec((step, width), lambda i: (i, 0))
    return pl.pallas_call(
        kernel,
        grid=(rows // step,),
        out_shape=jax.ShapeDtypeStruct(shape, bf16),
        in_specs=[SMEM_ARG, spec, spec, spec] + [ANY_ARG] * len(earlier),
        out_specs=pl.BlockSpec((1, 1, step, width), lambda i: (0, m, i, 0)),
        input_output_aliases={4: 0} if earlier else {},
        compiler_params=params(8),
        cost_estimate=cost(4 * rows * width, 8 * rows * width),
        name="input_gradient",
    )(is_upper, upper, piece, passed, *earlier)


def finished_half(sums, rep, order, half, c, chunks, earlier):
    pieces = (1 << len(order)) // 2
    rows = sums.shape[0] // pieces - 16
    features = sums.shape[1]
    shard = rows * chunks * pieces * 2

    def place(i, rep_ref):
        return (rep_ref[0] ^ mask_of(i + half * pieces, order)) * chunks + c

    def total(under):
        return under[0:1, :rows] + under[1:2, :rows] + under[2:3, :rows]

    if rows % 128:
        earlier = earlier or (jnp.zeros((shard, features), f32), jnp.zeros((1, shard), f32))
        for i in range(pieces):
            piece = sums[i * (rows + 16) : (i + 1) * (rows + 16)].astype(f32)
            at = place(i, rep) * rows
            earlier = (
                lax.dynamic_update_slice(earlier[0], piece[:rows], (at, 0)),
                lax.dynamic_update_slice(earlier[1], total(piece[rows:]), (0, at)),
            )
        return earlier

    def kernel(rep_ref, sum_ref, *refs):
        refs[-2][...] = sum_ref[:rows, :].astype(f32)
        refs[-1][...] = total(sum_ref[rows:, :].astype(f32))

    return pl.pallas_call(
        kernel,
        grid_spec=pltpu.PrefetchScalarGridSpec(
            num_scalar_prefetch=1,
            grid=(pieces,),
            in_specs=[pl.BlockSpec((rows + 16, features), lambda i, rep_ref: (i, 0))] + [ANY_ARG] * len(earlier),
            out_specs=[
                pl.BlockSpec((rows, features), lambda i, rep_ref: (place(i, rep_ref), 0)),
                pl.BlockSpec((1, rows), lambda i, rep_ref: (0, place(i, rep_ref))),
            ],
        ),
        out_shape=[jax.ShapeDtypeStruct((shard, features), f32), jax.ShapeDtypeStruct((1, shard), f32)],
        input_output_aliases={2: 0, 3: 1} if earlier else {},
        compiler_params=params(8),
        cost_estimate=cost(sums.size, 6 * sums.size),
        name="finished_half",
    )(rep, sums, *earlier)


def local(layer_input, value_grad, value_weight, norm_gain, top_grad):
    groups = lax.axis_size("fsdp")
    reps = lax.axis_size("rep")
    bits = reps.bit_length() - 1
    me = lax.axis_index("fsdp").astype(jnp.int32)[None]
    rep = lax.axis_index("rep").astype(jnp.int32)[None]
    _, micro, rows, width = layer_input.shape
    tokens = micro * rows
    norm_scale = float(tokens * reps * groups) ** (-0.5)
    chunks = 2
    orders = [tuple(range(bits)), tuple(reversed(range(bits)))]

    weight = value_weight[0]
    is_upper = lax.axis_index("section").astype(jnp.int32)[None]
    inputs = after(layer_input[0].reshape(tokens, width), me, rep, is_upper)

    hats = scaled_blocks(inputs, me, rep, groups, reps, 1)[0]
    plane = list(hats)
    for e in range(1, reps):
        plane[e] = flipped(hats[e], "rep", e)
    grads = after(value_grad[0].reshape(tokens, -1), hats[0])
    slots = [grads] + [cyclic(grads, "fsdp", j) for j in range(1, groups)]

    plane[0] = after(plane[0], *slots[1:])
    sent = regrouped(plane, groups)
    back = returned_blocks(slots, weight, norm_gain, micro)
    lines = [[back[j][m] for j in range(groups)] for m in range(micro)]
    far = groups // 2
    near = [j for j in range(1, groups) if j != far]
    columns = list(sent)
    columns[far] = cyclic(sent[far], "fsdp", far)
    columns[near[0]] = cyclic(sent[near[0]], "fsdp", near[0])
    for j in near[1:]:
        columns[j] = cyclic(after(sent[j], back[0][0], columns[near[0]]), "fsdp", j)
    held = after(joined(slots), sent[0])
    values = [held if e == 0 else flipped(held, "rep", e) for e in range(reps)]

    def send_back(m, j, *ties):
        lines[m][j] = cyclic(after(lines[m][j], *ties), "fsdp", -j)

    send_back(0, far, columns[far])
    for j in near:
        send_back(0, j, columns[far])
    send_back(1, near[0], lines[0][far])
    for j in near[1:]:
        send_back(1, j, lines[1][near[0]])
    send_back(1, far, *[lines[0][j] for j in near])
    sums = weight_product(columns, values, weight, norm_gain, rep, groups, chunks, norm_scale)
    gathered = [doubled(sums[c], orders[c]) for c in range(chunks)]
    finished = ()
    for half in (0, 1):
        for c in range(chunks):
            finished = finished_half(gathered[c][half], rep, orders[c], half, c, chunks, finished)
        if half == 0:
            early = finished
    weight_grad, gain_grad = finished

    result = ()
    for m in range(micro):
        ties = [*finished, *result] if m else [lines[1][near[-1]], *[g[0] for g in gathered]]
        lines[m][0] = after(lines[m][0], *ties)
        upper, piece = row_gradient(layer_input, top_grad, lines[m], me, m)
        passed = lax.ppermute(upper, "section", [(1, 0)])
        result = (input_gradient(upper, piece, passed, is_upper, layer_input.shape, m, result),)
    return (result[0], weight_grad[None], gain_grad)


def solution(mesh):
    return jax.shard_map(
        local,
        mesh=mesh,
        in_specs=(
            P("section", None, ("rep", "fsdp"), None),
            P("section", None, ("rep", "fsdp"), None),
            P("section", "fsdp", None),
            P("section", "fsdp"),
            P(None, ("rep", "fsdp"), None),
        ),
        out_specs=(
            P("section", None, ("rep", "fsdp"), None),
            P("section", "fsdp", None),
            P("section", "fsdp"),
        ),
        check_vma=False,
    )
```

```python
import jax
import jax.numpy as jnp
from jax import lax
from jax.experimental import pallas as pl
from jax.experimental.pallas import tpu as pltpu
from jax.sharding import PartitionSpec as P

norm_eps = 1e-05
bf16 = jnp.bfloat16
f32 = jnp.float32
MIB = 1 << 20
SMEM_ARG = pl.BlockSpec(memory_space=pltpu.SMEM)
ANY_ARG = pl.BlockSpec(memory_space=pl.ANY)


def cyclic(value, axis, steps):
    count = lax.axis_size(axis)
    return lax.ppermute(value, axis, [(i, (i + steps) % count) for i in range(count)])


def flipped(value, axis, mask):
    count = lax.axis_size(axis)
    return lax.ppermute(value, axis, [(i, i ^ mask) for i in range(count)])


def after(value, *others):
    return lax.optimization_barrier((value, *others))[0]


def params(mib):
    return pltpu.CompilerParams(vmem_limit_bytes=mib * MIB)


def cost(flops, bytes_accessed):
    return pl.CostEstimate(flops=int(flops), bytes_accessed=int(bytes_accessed), transcendentals=0)


def scaled_blocks(x, me, rep, groups, reps, chunks):
    tokens, width = x.shape
    shard = width // groups
    piece = shard // reps
    chunk = piece // chunks
    if chunk % 128:
        x = x.astype(f32)
        hat = (x * lax.rsqrt(jnp.mean(x * x, axis=1, keepdims=True) + norm_eps)).astype(bf16)
        hat = jnp.roll(hat.reshape(tokens, groups, reps, chunks, chunk), -me[0], axis=1)
        take = lambda e, c: lax.dynamic_index_in_dim(hat, rep[0] ^ e, 2, False)[:, :, c].reshape(tokens, groups * chunk)
        return [[take(e, c) for e in range(reps)] for c in range(chunks)]
    step = 16
    block = min(tokens, 32)

    def kernel(me_ref, rep_ref, x_ref, *out_refs):
        span = min(shard, 512)
        for row in range(0, block, step):
            rows = slice(row, row + step)
            total = jnp.zeros((step, 128), f32)
            for c in range(0, width, span):
                v = x_ref[rows, c : c + span].astype(f32)
                v = v * v
                for k in range(0, span, 128):
                    total = total + v[:, k : k + 128]
            scale = lax.rsqrt(jnp.sum(total, axis=1, keepdims=True) / width + norm_eps)
            for c in range(chunks):
                for e in range(reps):
                    for j in range(groups):
                        at = lax.rem(me_ref[0] + j, groups) * shard + (rep_ref[0] ^ e) * piece + c * chunk
                        v = x_ref[rows, pl.ds(pl.multiple_of(at, chunk), chunk)].astype(f32)
                        out_refs[c * reps + e][rows, j * chunk : (j + 1) * chunk] = (v * scale).astype(bf16)

    outs = pl.pallas_call(
        kernel,
        grid=(tokens // block,),
        out_shape=[jax.ShapeDtypeStruct((tokens, groups * chunk), bf16)] * (chunks * reps),
        in_specs=[SMEM_ARG, SMEM_ARG, pl.BlockSpec((block, width), lambda i: (i, 0))],
        out_specs=[pl.BlockSpec((block, groups * chunk), lambda i: (i, 0))] * (chunks * reps),
        compiler_params=params(8),
        cost_estimate=cost(6 * x.size, 4 * x.size),
        name="scaled_blocks",
    )(me, rep, x)
    return [list(outs[c * reps : (c + 1) * reps]) for c in range(chunks)]


def joined(arrays):
    rows, width = arrays[0].shape
    if rows % 16 or width % 128:
        return jnp.concatenate(arrays, axis=0)

    def kernel(*refs):
        copies = []
        for k in range(len(arrays)):
            target = refs[-2].at[k * rows : (k + 1) * rows, :]
            copies.append(pltpu.make_async_copy(refs[k], target, refs[-1].at[k]))
            copies[-1].start()
        for copy in copies:
            copy.wait()

    return pl.pallas_call(
        kernel,
        out_shape=jax.ShapeDtypeStruct((len(arrays) * rows, width), bf16),
        in_specs=[ANY_ARG] * len(arrays),
        out_specs=ANY_ARG,
        scratch_shapes=[pltpu.SemaphoreType.DMA((len(arrays),))],
        compiler_params=params(4),
        cost_estimate=cost(0, 4 * len(arrays) * rows * width),
        name="joined",
    )(*arrays)


def doubled(value, order):
    for bit in order[:-1]:
        value = joined([value, flipped(value, "rep", 1 << bit)])
    return value, flipped(value, "rep", 1 << order[-1])


def mask_of(pos, order):
    return sum(((pos >> i) & 1) << bit for i, bit in enumerate(order))


def regrouped(blocks, me, groups):
    tokens, width = blocks[0].shape
    piece = width // groups
    reps = len(blocks)
    rows = reps * tokens
    if piece % 128:
        parts = jnp.stack([jnp.concatenate([b[:, j * piece : (j + 1) * piece] for b in blocks], axis=0) for j in range(groups)])
        return jnp.roll(parts, me[0], axis=0).reshape(groups * rows, piece)

    def kernel(me_ref, *refs):
        copies = []
        for e in range(reps):
            for j in range(groups):
                source = refs[e].at[:, j * piece : (j + 1) * piece]
                at = pl.multiple_of(lax.rem(me_ref[0] + j, groups) * rows + e * tokens, tokens)
                copies.append(pltpu.make_async_copy(source, refs[reps].at[pl.ds(at, tokens), :], refs[-1].at[e * groups + j]))
                copies[-1].start()
        for copy in copies:
            copy.wait()

    return pl.pallas_call(
        kernel,
        out_shape=jax.ShapeDtypeStruct((groups * rows, piece), bf16),
        in_specs=[SMEM_ARG] + [ANY_ARG] * reps,
        out_specs=ANY_ARG,
        scratch_shapes=[pltpu.SemaphoreType.DMA((reps * groups,))],
        compiler_params=params(8),
        cost_estimate=cost(0, 4 * rows * width),
        name="regrouped",
    )(me, *blocks)


def weight_product(columns, values, weight, gain, me, rep, groups, count, norm_scale):
    rows, width = columns.shape[0] // groups, columns.shape[1]
    reps = len(values)
    tokens = rows // reps
    features = values[0].shape[1]
    chunk = width // count
    contract = (((0,), (0,)), ((), ()))

    def thirds(row):
        first = row.astype(bf16)
        rest = row - first.astype(f32)
        second = rest.astype(bf16)
        return first, second, (rest - second.astype(f32)).astype(bf16)

    if chunk % 128:
        order = jnp.stack([v.reshape(groups, tokens, features) for v in values], axis=1)
        order = jnp.roll(jnp.flip(order, axis=0), me[0] + 1, axis=0)
        raw = lax.dot_general(columns, order.reshape(-1, features), contract, preferred_element_type=f32)
        own = lax.dynamic_slice_in_dim(weight, rep[0] * width, width, 0).astype(f32)
        dots = jnp.sum(raw * own, axis=1) * norm_scale
        factor = lax.dynamic_slice_in_dim(gain[0], rep[0] * width, width, 0).astype(f32) * norm_scale
        raw = (raw * factor[:, None]).astype(bf16)
        outs = []
        for c in range(count):
            at = slice(c * chunk, (c + 1) * chunk)
            under = jnp.stack(thirds(dots[at]) + (jnp.zeros((chunk,), bf16),) * 13)
            outs.append(jnp.concatenate([raw[at], jnp.pad(under, ((0, 0), (0, features - chunk)))], axis=0))
        return outs

    def kernel(me_ref, rep_ref, column_ref, *refs):
        value_refs, weight_ref, gain_ref = refs[:reps], refs[reps], refs[reps + 1]
        out_refs, total = refs[reps + 2 : -1], refs[-1]
        start = pl.multiple_of(rep_ref[0] * width, width)
        for j in range(groups):
            right = jnp.concatenate([v[j * tokens : (j + 1) * tokens, :] for v in value_refs], axis=0)
            at = pl.multiple_of(lax.rem(me_ref[0] - j + groups, groups) * rows, rows)
            for c in range(count):
                block = column_ref[pl.ds(at, rows), c * chunk : (c + 1) * chunk]
                product = lax.dot_general(block, right, contract, preferred_element_type=f32)
                if j == 0:
                    total[c] = product
                else:
                    total[c] += product
        for c in range(count):
            at = pl.ds(pl.multiple_of(start + c * chunk, chunk), chunk)
            raw = total[c]
            factor = gain_ref[:, at].astype(f32) * norm_scale
            factor = jnp.transpose(jnp.broadcast_to(factor, (128, chunk)))[:, 0:1]
            out_refs[c][:chunk, :] = (raw * factor).astype(bf16)
            terms = raw * weight_ref[at, :].astype(f32)
            terms = sum(terms[:, k : k + 128] for k in range(0, features, 128))
            dots = lax.dot_general(
                jnp.full((8, 128), norm_scale, f32),
                terms,
                (((1,), (1,)), ((), ())),
                precision=lax.Precision.HIGHEST,
                preferred_element_type=f32,
            )
            under = jnp.concatenate([row[0:1, :].astype(f32) for row in thirds(dots)] + [jnp.zeros((13, chunk), f32)], axis=0)
            out_refs[c][chunk:, :chunk] = under.astype(bf16)
            out_refs[c][chunk:, chunk:] = jnp.zeros((16, features - chunk), bf16)

    vmem = pl.BlockSpec(memory_space=pltpu.VMEM)
    return pl.pallas_call(
        kernel,
        out_shape=[jax.ShapeDtypeStruct((chunk + 16, features), bf16)] * count,
        in_specs=[SMEM_ARG] * 2 + [vmem] * (reps + 3),
        out_specs=[vmem] * count,
        scratch_shapes=[pltpu.VMEM((count, chunk, features), f32)],
        compiler_params=params(24),
        cost_estimate=cost(2 * groups * rows * width * features, 2 * groups * rows * (width + features) + 4 * width * features),
        name="weight_product",
    )(me, rep, columns, *values, weight, gain)


def returned_blocks(slots, weight, gain, micro):
    groups = len(slots)
    tokens, features = slots[0].shape
    rows = tokens // micro
    shard = weight.shape[0]
    tile = min(shard, 512)

    def kernel(*refs):
        slot_refs, weight_ref, gain_ref = refs[:groups], refs[groups], refs[groups + 1]
        out_refs = refs[groups + 2 :]
        factor = gain_ref[...].astype(f32)
        pair = 2 if groups % 2 == 0 else 1
        for j in range(0, groups, pair):
            values = jnp.concatenate([slot_refs[j + i][...] for i in range(pair)], axis=0)
            back = lax.dot_general(values, weight_ref[...], (((1,), (1,)), ((), ())), preferred_element_type=f32)
            back = (back * factor).astype(bf16)
            for i in range(pair):
                for m in range(micro):
                    at = i * tokens + m * rows
                    out_refs[(j + i) * micro + m][...] = back[at : at + rows, :]

    outs = pl.pallas_call(
        kernel,
        grid=(shard // tile,),
        out_shape=[jax.ShapeDtypeStruct((rows, shard), bf16)] * (groups * micro),
        in_specs=[pl.BlockSpec((tokens, features), lambda i: (0, 0))] * groups
        + [pl.BlockSpec((tile, features), lambda i: (i, 0)), pl.BlockSpec((1, tile), lambda i: (0, i))],
        out_specs=[pl.BlockSpec((rows, tile), lambda i: (0, i))] * (groups * micro),
        compiler_params=params(8),
        cost_estimate=cost(2 * groups * tokens * shard * features, 2 * groups * tokens * (shard + features) + 2 * shard * features),
        name="returned_blocks",
    )(*slots, weight, gain)
    return [list(outs[j * micro : (j + 1) * micro]) for j in range(groups)]


def row_gradient(x, top, blocks, me, m):
    groups = len(blocks)
    rows, shard = blocks[0].shape
    width = shard * groups
    step = 16

    def kernel(me_ref, x_ref, top_ref, *refs):
        block_refs, upper_ref, piece_ref = refs[:groups], refs[groups], refs[groups + 1]
        squares = jnp.zeros((step, 128), f32)
        dots = jnp.zeros((step, 128), f32)
        starts = [pl.multiple_of(lax.rem(me_ref[0] + j, groups) * shard, shard) for j in range(groups)]
        span = min(shard, 512)
        for j in range(groups):
            for c in range(0, shard, span):
                v = x_ref[0, 0, :, pl.ds(pl.multiple_of(starts[j] + c, span), span)].astype(f32)
                d = block_refs[j][:, c : c + span].astype(f32) * v
                v = v * v
                for k in range(0, span, 128):
                    squares = squares + v[:, k : k + 128]
                    dots = dots + d[:, k : k + 128]
        scale = lax.rsqrt(jnp.sum(squares, axis=1, keepdims=True) / width + norm_eps)
        mean = jnp.sum(dots, axis=1, keepdims=True) * scale / width
        slope = scale * mean
        for j in range(groups):
            for c in range(0, shard, span):
                at = pl.ds(pl.multiple_of(starts[j] + c, span), span)
                v = x_ref[0, 0, :, at].astype(f32)
                piece = (scale * (block_refs[j][:, c : c + span].astype(f32) - v * slope)).astype(bf16)
                piece_ref[:, at] = piece
                upper_ref[:, at] = (top_ref[0, :, at].astype(f32) + piece.astype(f32)).astype(bf16)

    return pl.pallas_call(
        kernel,
        grid=(rows // step,),
        out_shape=[jax.ShapeDtypeStruct((rows, width), bf16)] * 2,
        in_specs=[
            SMEM_ARG,
            pl.BlockSpec((1, 1, step, width), lambda i: (0, m, i, 0)),
            pl.BlockSpec((1, step, width), lambda i: (m, i, 0)),
        ]
        + [pl.BlockSpec((step, shard), lambda i: (i, 0))] * groups,
        out_specs=[pl.BlockSpec((step, width), lambda i: (i, 0))] * 2,
        compiler_params=params(8),
        cost_estimate=cost(12 * rows * width, 10 * rows * width),
        name="row_gradient",
    )(me, x, top, *blocks)


def input_gradient(upper, piece, passed, is_upper, shape, m, earlier):
    rows, width = upper.shape
    step = min(rows, 32)

    def kernel(is_upper_ref, upper_ref, piece_ref, passed_ref, *refs):
        lower = (passed_ref[...].astype(f32) + piece_ref[...].astype(f32)).astype(bf16)
        refs[-1][0, 0] = jnp.where(is_upper_ref[0] == 1, upper_ref[...], lower)

    spec = pl.BlockSpec((step, width), lambda i: (i, 0))
    return pl.pallas_call(
        kernel,
        grid=(rows // step,),
        out_shape=jax.ShapeDtypeStruct(shape, bf16),
        in_specs=[SMEM_ARG, spec, spec, spec] + [ANY_ARG] * len(earlier),
        out_specs=pl.BlockSpec((1, 1, step, width), lambda i: (0, m, i, 0)),
        input_output_aliases={4: 0} if earlier else {},
        compiler_params=params(8),
        cost_estimate=cost(4 * rows * width, 8 * rows * width),
        name="input_gradient",
    )(is_upper, upper, piece, passed, *earlier)


def finished_half(sums, rep, order, half, c, chunks, earlier):
    pieces = (1 << len(order)) // 2
    rows = sums.shape[0] // pieces - 16
    features = sums.shape[1]
    shard = rows * chunks * pieces * 2

    def place(i, rep_ref):
        return (rep_ref[0] ^ mask_of(i + half * pieces, order)) * chunks + c

    def total(under):
        return under[0:1, :rows] + under[1:2, :rows] + under[2:3, :rows]

    if rows % 128:
        earlier = earlier or (jnp.zeros((shard, features), f32), jnp.zeros((1, shard), f32))
        for i in range(pieces):
            piece = sums[i * (rows + 16) : (i + 1) * (rows + 16)].astype(f32)
            at = place(i, rep) * rows
            earlier = (
                lax.dynamic_update_slice(earlier[0], piece[:rows], (at, 0)),
                lax.dynamic_update_slice(earlier[1], total(piece[rows:]), (0, at)),
            )
        return earlier

    def kernel(rep_ref, sum_ref, *refs):
        refs[-2][...] = sum_ref[:rows, :].astype(f32)
        refs[-1][...] = total(sum_ref[rows:, :].astype(f32))

    return pl.pallas_call(
        kernel,
        grid_spec=pltpu.PrefetchScalarGridSpec(
            num_scalar_prefetch=1,
            grid=(pieces,),
            in_specs=[pl.BlockSpec((rows + 16, features), lambda i, rep_ref: (i, 0))] + [ANY_ARG] * len(earlier),
            out_specs=[
                pl.BlockSpec((rows, features), lambda i, rep_ref: (place(i, rep_ref), 0)),
                pl.BlockSpec((1, rows), lambda i, rep_ref: (0, place(i, rep_ref))),
            ],
        ),
        out_shape=[jax.ShapeDtypeStruct((shard, features), f32), jax.ShapeDtypeStruct((1, shard), f32)],
        input_output_aliases={2: 0, 3: 1} if earlier else {},
        compiler_params=params(8),
        cost_estimate=cost(sums.size, 6 * sums.size),
        name="finished_half",
    )(rep, sums, *earlier)


def local(layer_input, value_grad, value_weight, norm_gain, top_grad):
    groups = lax.axis_size("fsdp")
    reps = lax.axis_size("rep")
    bits = reps.bit_length() - 1
    me = lax.axis_index("fsdp").astype(jnp.int32)[None]
    rep = lax.axis_index("rep").astype(jnp.int32)[None]
    _, micro, rows, width = layer_input.shape
    tokens = micro * rows
    norm_scale = float(tokens * reps * groups) ** (-0.5)
    chunks = 2
    orders = [tuple(range(bits)), tuple(reversed(range(bits)))]

    weight = value_weight[0]
    is_upper = lax.axis_index("section").astype(jnp.int32)[None]
    inputs = after(layer_input[0].reshape(tokens, width), me, rep, is_upper)

    hats = scaled_blocks(inputs, me, rep, groups, reps, 1)[0]
    plane = list(hats)
    for e in range(1, reps):
        plane[e] = flipped(hats[e], "rep", e)
    grads = after(value_grad[0].reshape(tokens, -1), hats[0])
    slots = [grads] + [cyclic(grads, "fsdp", j) for j in range(1, groups)]

    plane[0] = after(plane[0], *slots[1:])
    sent = regrouped(plane, me, groups)
    columns = lax.all_to_all(sent, "fsdp", split_axis=0, concat_axis=0, tiled=True)
    back = returned_blocks([after(slots[0], sent), *slots[1:]], weight, norm_gain, micro)
    lines = [[back[j][m] for j in range(groups)] for m in range(micro)]
    far = groups // 2
    near = [j for j in range(1, groups) if j != far]
    held = after(joined(slots), sent)
    values = [held if e == 0 else flipped(held, "rep", e) for e in range(reps)]

    def send_back(m, j, *ties):
        lines[m][j] = cyclic(after(lines[m][j], *ties), "fsdp", -j)

    for j in [far, *near]:
        send_back(0, j, columns)
    send_back(1, near[0], lines[0][far])
    for j in near[1:]:
        send_back(1, j, lines[1][near[0]])
    send_back(1, far, *[lines[0][j] for j in near])
    columns = after(columns, back[0][0])
    sums = weight_product(columns, values, weight, norm_gain, me, rep, groups, chunks, norm_scale)
    gathered = [doubled(sums[c], orders[c]) for c in range(chunks)]
    finished = ()
    for half in (0, 1):
        for c in range(chunks):
            finished = finished_half(gathered[c][half], rep, orders[c], half, c, chunks, finished)
        if half == 0:
            early = finished
    weight_grad, gain_grad = finished

    result = ()
    for m in range(micro):
        ties = [*finished, *result] if m else [lines[1][near[-1]], *[g[0] for g in gathered]]
        lines[m][0] = after(lines[m][0], *ties)
        upper, piece = row_gradient(layer_input, top_grad, lines[m], me, m)
        passed = lax.ppermute(upper, "section", [(1, 0)])
        result = (input_gradient(upper, piece, passed, is_upper, layer_input.shape, m, result),)
    return (result[0], weight_grad[None], gain_grad)


def solution(mesh):
    return jax.shard_map(
        local,
        mesh=mesh,
        in_specs=(
            P("section", None, ("rep", "fsdp"), None),
            P("section", None, ("rep", "fsdp"), None),
            P("section", "fsdp", None),
            P("section", "fsdp"),
            P(None, ("rep", "fsdp"), None),
        ),
        out_specs=(
            P("section", None, ("rep", "fsdp"), None),
            P("section", "fsdp", None),
            P("section", "fsdp"),
        ),
        check_vma=False,
    )
```

```python
import jax
import jax.numpy as jnp
from jax import lax
from jax.experimental import pallas as pl
from jax.experimental.pallas import tpu as pltpu
from jax.sharding import PartitionSpec as P

norm_eps = 1e-05
bf16 = jnp.bfloat16
f32 = jnp.float32
MIB = 1 << 20
SMEM_ARG = pl.BlockSpec(memory_space=pltpu.SMEM)
ANY_ARG = pl.BlockSpec(memory_space=pl.ANY)


def cyclic(value, axis, steps):
    count = lax.axis_size(axis)
    return lax.ppermute(value, axis, [(i, (i + steps) % count) for i in range(count)])


def flipped(value, axis, mask):
    count = lax.axis_size(axis)
    return lax.ppermute(value, axis, [(i, i ^ mask) for i in range(count)])


def after(value, *others):
    return lax.optimization_barrier((value, *others))[0]


def params(mib):
    return pltpu.CompilerParams(vmem_limit_bytes=mib * MIB)


def cost(flops, bytes_accessed):
    return pl.CostEstimate(flops=int(flops), bytes_accessed=int(bytes_accessed), transcendentals=0)


def scaled_blocks(x, me, rep, groups, reps, chunks):
    tokens, width = x.shape
    shard = width // groups
    piece = shard // reps
    chunk = piece // chunks
    if chunk % 128:
        x = x.astype(f32)
        hat = (x * lax.rsqrt(jnp.mean(x * x, axis=1, keepdims=True) + norm_eps)).astype(bf16)
        hat = jnp.roll(hat.reshape(tokens, groups, reps, chunks, chunk), -me[0], axis=1)
        take = lambda e, c: lax.dynamic_index_in_dim(hat, rep[0] ^ e, 2, False)[:, :, c].reshape(tokens, groups * chunk)
        return [[take(e, c) for e in range(reps)] for c in range(chunks)]
    step = 16
    block = min(tokens, 32)

    def kernel(me_ref, rep_ref, x_ref, *out_refs):
        span = min(shard, 512)
        for row in range(0, block, step):
            rows = slice(row, row + step)
            total = jnp.zeros((step, 128), f32)
            for c in range(0, width, span):
                v = x_ref[rows, c : c + span].astype(f32)
                v = v * v
                for k in range(0, span, 128):
                    total = total + v[:, k : k + 128]
            scale = lax.rsqrt(jnp.sum(total, axis=1, keepdims=True) / width + norm_eps)
            for c in range(chunks):
                for e in range(reps):
                    for j in range(groups):
                        at = lax.rem(me_ref[0] + j, groups) * shard + (rep_ref[0] ^ e) * piece + c * chunk
                        v = x_ref[rows, pl.ds(pl.multiple_of(at, chunk), chunk)].astype(f32)
                        out_refs[c * reps + e][rows, j * chunk : (j + 1) * chunk] = (v * scale).astype(bf16)

    outs = pl.pallas_call(
        kernel,
        grid=(tokens // block,),
        out_shape=[jax.ShapeDtypeStruct((tokens, groups * chunk), bf16)] * (chunks * reps),
        in_specs=[SMEM_ARG, SMEM_ARG, pl.BlockSpec((block, width), lambda i: (i, 0))],
        out_specs=[pl.BlockSpec((block, groups * chunk), lambda i: (i, 0))] * (chunks * reps),
        compiler_params=params(8),
        cost_estimate=cost(6 * x.size, 4 * x.size),
        name="scaled_blocks",
    )(me, rep, x)
    return [list(outs[c * reps : (c + 1) * reps]) for c in range(chunks)]


def joined(arrays):
    rows, width = arrays[0].shape
    if rows % 16 or width % 128:
        return jnp.concatenate(arrays, axis=0)

    def kernel(*refs):
        copies = []
        for k in range(len(arrays)):
            target = refs[-2].at[k * rows : (k + 1) * rows, :]
            copies.append(pltpu.make_async_copy(refs[k], target, refs[-1].at[k]))
            copies[-1].start()
        for copy in copies:
            copy.wait()

    return pl.pallas_call(
        kernel,
        out_shape=jax.ShapeDtypeStruct((len(arrays) * rows, width), bf16),
        in_specs=[ANY_ARG] * len(arrays),
        out_specs=ANY_ARG,
        scratch_shapes=[pltpu.SemaphoreType.DMA((len(arrays),))],
        compiler_params=params(4),
        cost_estimate=cost(0, 4 * len(arrays) * rows * width),
        name="joined",
    )(*arrays)


def doubled(value, order):
    for bit in order[:-1]:
        value = joined([value, flipped(value, "rep", 1 << bit)])
    return value, flipped(value, "rep", 1 << order[-1])


def mask_of(pos, order):
    return sum(((pos >> i) & 1) << bit for i, bit in enumerate(order))


def regrouped(blocks, groups):
    tokens, width = blocks[0].shape
    chunk = width // groups
    reps = len(blocks)
    if chunk % 128:
        return [jnp.concatenate([b[:, j * chunk : (j + 1) * chunk] for b in blocks], axis=0) for j in range(groups)]

    def kernel(*refs):
        copies = []
        for e in range(reps):
            for j in range(groups):
                source = refs[e].at[:, j * chunk : (j + 1) * chunk]
                target = refs[reps + j].at[e * tokens : (e + 1) * tokens, :]
                copies.append(pltpu.make_async_copy(source, target, refs[-1].at[e * groups + j]))
                copies[-1].start()
        for copy in copies:
            copy.wait()

    return list(
        pl.pallas_call(
            kernel,
            out_shape=[jax.ShapeDtypeStruct((reps * tokens, chunk), bf16)] * groups,
            in_specs=[ANY_ARG] * reps,
            out_specs=[ANY_ARG] * groups,
            scratch_shapes=[pltpu.SemaphoreType.DMA((reps * groups,))],
            compiler_params=params(8),
            cost_estimate=cost(0, 4 * reps * tokens * width),
            name="regrouped",
        )(*blocks)
    )


def weight_product(columns, values, weight, gain, rep, groups, count, norm_scale):
    rows, width = columns[0].shape
    reps = len(values)
    tokens = rows // reps
    features = values[0].shape[1]
    chunk = width // count
    contract = (((0,), (0,)), ((), ()))

    def thirds(row):
        first = row.astype(bf16)
        rest = row - first.astype(f32)
        second = rest.astype(bf16)
        return first, second, (rest - second.astype(f32)).astype(bf16)

    if chunk % 128:
        order = jnp.stack([v.reshape(groups, tokens, features) for v in values], axis=1)
        raw = lax.dot_general(
            jnp.concatenate(columns, axis=0), order.reshape(-1, features), contract, preferred_element_type=f32
        )
        own = lax.dynamic_slice_in_dim(weight, rep[0] * width, width, 0).astype(f32)
        dots = jnp.sum(raw * own, axis=1) * norm_scale
        factor = lax.dynamic_slice_in_dim(gain[0], rep[0] * width, width, 0).astype(f32) * norm_scale
        raw = (raw * factor[:, None]).astype(bf16)
        outs = []
        for c in range(count):
            at = slice(c * chunk, (c + 1) * chunk)
            under = jnp.stack(thirds(dots[at]) + (jnp.zeros((chunk,), bf16),) * 13)
            outs.append(jnp.concatenate([raw[at], jnp.pad(under, ((0, 0), (0, features - chunk)))], axis=0))
        return outs

    def kernel(rep_ref, *refs):
        column_refs, value_refs = refs[:groups], refs[groups : groups + reps]
        weight_ref, gain_ref = refs[groups + reps], refs[groups + reps + 1]
        out_refs, total = refs[groups + reps + 2 : -1], refs[-1]
        start = pl.multiple_of(rep_ref[0] * width, width)
        for j in range(groups):
            right = jnp.concatenate([v[j * tokens : (j + 1) * tokens, :] for v in value_refs], axis=0)
            for c in range(count):
                block = column_refs[j][:, c * chunk : (c + 1) * chunk]
                product = lax.dot_general(block, right, contract, preferred_element_type=f32)
                if j == 0:
                    total[c] = product
                else:
                    total[c] += product
        for c in range(count):
            at = pl.ds(pl.multiple_of(start + c * chunk, chunk), chunk)
            raw = total[c]
            factor = gain_ref[:, at].astype(f32) * norm_scale
            factor = jnp.transpose(jnp.broadcast_to(factor, (128, chunk)))[:, 0:1]
            out_refs[c][:chunk, :] = (raw * factor).astype(bf16)
            terms = raw * weight_ref[at, :].astype(f32)
            terms = sum(terms[:, k : k + 128] for k in range(0, features, 128))
            dots = lax.dot_general(
                jnp.full((8, 128), norm_scale, f32),
                terms,
                (((1,), (1,)), ((), ())),
                precision=lax.Precision.HIGHEST,
                preferred_element_type=f32,
            )
            under = jnp.concatenate([row[0:1, :].astype(f32) for row in thirds(dots)] + [jnp.zeros((13, chunk), f32)], axis=0)
            out_refs[c][chunk:, :chunk] = under.astype(bf16)
            out_refs[c][chunk:, chunk:] = jnp.zeros((16, features - chunk), bf16)

    vmem = pl.BlockSpec(memory_space=pltpu.VMEM)
    return pl.pallas_call(
        kernel,
        out_shape=[jax.ShapeDtypeStruct((chunk + 16, features), bf16)] * count,
        in_specs=[SMEM_ARG] + [vmem] * (groups + reps + 2),
        out_specs=[vmem] * count,
        scratch_shapes=[pltpu.VMEM((count, chunk, features), f32)],
        compiler_params=params(24),
        cost_estimate=cost(2 * groups * rows * width * features, 2 * groups * rows * (width + features) + 4 * width * features),
        name="weight_product",
    )(rep, *columns, *values, weight, gain)


def returned_blocks(slots, weight, gain, micro):
    groups = len(slots)
    tokens, features = slots[0].shape
    rows = tokens // micro
    shard = weight.shape[0]
    tile = min(shard, 512)

    def kernel(*refs):
        slot_refs, weight_ref, gain_ref = refs[:groups], refs[groups], refs[groups + 1]
        out_refs = refs[groups + 2 :]
        factor = gain_ref[...].astype(f32)
        pair = 2 if groups % 2 == 0 else 1
        for j in range(0, groups, pair):
            values = jnp.concatenate([slot_refs[j + i][...] for i in range(pair)], axis=0)
            back = lax.dot_general(values, weight_ref[...], (((1,), (1,)), ((), ())), preferred_element_type=f32)
            back = (back * factor).astype(bf16)
            for i in range(pair):
                for m in range(micro):
                    at = i * tokens + m * rows
                    out_refs[(j + i) * micro + m][...] = back[at : at + rows, :]

    outs = pl.pallas_call(
        kernel,
        grid=(shard // tile,),
        out_shape=[jax.ShapeDtypeStruct((rows, shard), bf16)] * (groups * micro),
        in_specs=[pl.BlockSpec((tokens, features), lambda i: (0, 0))] * groups
        + [pl.BlockSpec((tile, features), lambda i: (i, 0)), pl.BlockSpec((1, tile), lambda i: (0, i))],
        out_specs=[pl.BlockSpec((rows, tile), lambda i: (0, i))] * (groups * micro),
        compiler_params=params(8),
        cost_estimate=cost(2 * groups * tokens * shard * features, 2 * groups * tokens * (shard + features) + 2 * shard * features),
        name="returned_blocks",
    )(*slots, weight, gain)
    return [list(outs[j * micro : (j + 1) * micro]) for j in range(groups)]


def row_gradient(x, top, blocks, me, m):
    groups = len(blocks)
    rows, shard = blocks[0].shape
    width = shard * groups
    step = 16

    def kernel(me_ref, x_ref, top_ref, *refs):
        block_refs, upper_ref, piece_ref = refs[:groups], refs[groups], refs[groups + 1]
        squares = jnp.zeros((step, 128), f32)
        dots = jnp.zeros((step, 128), f32)
        starts = [pl.multiple_of(lax.rem(me_ref[0] + j, groups) * shard, shard) for j in range(groups)]
        span = min(shard, 512)
        for j in range(groups):
            for c in range(0, shard, span):
                v = x_ref[0, 0, :, pl.ds(pl.multiple_of(starts[j] + c, span), span)].astype(f32)
                d = block_refs[j][:, c : c + span].astype(f32) * v
                v = v * v
                for k in range(0, span, 128):
                    squares = squares + v[:, k : k + 128]
                    dots = dots + d[:, k : k + 128]
        scale = lax.rsqrt(jnp.sum(squares, axis=1, keepdims=True) / width + norm_eps)
        mean = jnp.sum(dots, axis=1, keepdims=True) * scale / width
        slope = scale * mean
        for j in range(groups):
            for c in range(0, shard, span):
                at = pl.ds(pl.multiple_of(starts[j] + c, span), span)
                v = x_ref[0, 0, :, at].astype(f32)
                piece = (scale * (block_refs[j][:, c : c + span].astype(f32) - v * slope)).astype(bf16)
                piece_ref[:, at] = piece
                upper_ref[:, at] = (top_ref[0, :, at].astype(f32) + piece.astype(f32)).astype(bf16)

    return pl.pallas_call(
        kernel,
        grid=(rows // step,),
        out_shape=[jax.ShapeDtypeStruct((rows, width), bf16)] * 2,
        in_specs=[
            SMEM_ARG,
            pl.BlockSpec((1, 1, step, width), lambda i: (0, m, i, 0)),
            pl.BlockSpec((1, step, width), lambda i: (m, i, 0)),
        ]
        + [pl.BlockSpec((step, shard), lambda i: (i, 0))] * groups,
        out_specs=[pl.BlockSpec((step, width), lambda i: (i, 0))] * 2,
        compiler_params=params(8),
        cost_estimate=cost(12 * rows * width, 10 * rows * width),
        name="row_gradient",
    )(me, x, top, *blocks)


def input_gradient(upper, piece, passed, is_upper, shape, m, earlier):
    rows, width = upper.shape
    step = min(rows, 32)

    def kernel(is_upper_ref, upper_ref, piece_ref, passed_ref, *refs):
        lower = (passed_ref[...].astype(f32) + piece_ref[...].astype(f32)).astype(bf16)
        refs[-1][0, 0] = jnp.where(is_upper_ref[0] == 1, upper_ref[...], lower)

    spec = pl.BlockSpec((step, width), lambda i: (i, 0))
    return pl.pallas_call(
        kernel,
        grid=(rows // step,),
        out_shape=jax.ShapeDtypeStruct(shape, bf16),
        in_specs=[SMEM_ARG, spec, spec, spec] + [ANY_ARG] * len(earlier),
        out_specs=pl.BlockSpec((1, 1, step, width), lambda i: (0, m, i, 0)),
        input_output_aliases={4: 0} if earlier else {},
        compiler_params=params(8),
        cost_estimate=cost(4 * rows * width, 8 * rows * width),
        name="input_gradient",
    )(is_upper, upper, piece, passed, *earlier)


def finished_half(sums, rep, order, half, c, chunks, earlier):
    pieces = (1 << len(order)) // 2
    rows = sums.shape[0] // pieces - 16
    features = sums.shape[1]
    shard = rows * chunks * pieces * 2

    def place(i, rep_ref):
        return (rep_ref[0] ^ mask_of(i + half * pieces, order)) * chunks + c

    def total(under):
        return under[0:1, :rows] + under[1:2, :rows] + under[2:3, :rows]

    if rows % 128:
        earlier = earlier or (jnp.zeros((shard, features), f32), jnp.zeros((1, shard), f32))
        for i in range(pieces):
            piece = sums[i * (rows + 16) : (i + 1) * (rows + 16)].astype(f32)
            at = place(i, rep) * rows
            earlier = (
                lax.dynamic_update_slice(earlier[0], piece[:rows], (at, 0)),
                lax.dynamic_update_slice(earlier[1], total(piece[rows:]), (0, at)),
            )
        return earlier

    def kernel(rep_ref, sum_ref, *refs):
        refs[-2][...] = sum_ref[:rows, :].astype(f32)
        refs[-1][...] = total(sum_ref[rows:, :].astype(f32))

    return pl.pallas_call(
        kernel,
        grid_spec=pltpu.PrefetchScalarGridSpec(
            num_scalar_prefetch=1,
            grid=(pieces,),
            in_specs=[pl.BlockSpec((rows + 16, features), lambda i, rep_ref: (i, 0))] + [ANY_ARG] * len(earlier),
            out_specs=[
                pl.BlockSpec((rows, features), lambda i, rep_ref: (place(i, rep_ref), 0)),
                pl.BlockSpec((1, rows), lambda i, rep_ref: (0, place(i, rep_ref))),
            ],
        ),
        out_shape=[jax.ShapeDtypeStruct((shard, features), f32), jax.ShapeDtypeStruct((1, shard), f32)],
        input_output_aliases={2: 0, 3: 1} if earlier else {},
        compiler_params=params(8),
        cost_estimate=cost(sums.size, 6 * sums.size),
        name="finished_half",
    )(rep, sums, *earlier)


def local(layer_input, value_grad, value_weight, norm_gain, top_grad):
    groups = lax.axis_size("fsdp")
    reps = lax.axis_size("rep")
    bits = reps.bit_length() - 1
    me = lax.axis_index("fsdp").astype(jnp.int32)[None]
    rep = lax.axis_index("rep").astype(jnp.int32)[None]
    _, micro, rows, width = layer_input.shape
    tokens = micro * rows
    norm_scale = float(tokens * reps * groups) ** (-0.5)
    chunks = 2
    orders = [tuple(range(bits)), tuple(reversed(range(bits)))]

    weight = value_weight[0]
    is_upper = lax.axis_index("section").astype(jnp.int32)[None]
    inputs = after(layer_input[0].reshape(tokens, width), me, rep, is_upper)

    hats = scaled_blocks(inputs, me, rep, groups, reps, 1)[0]
    plane = list(hats)
    for e in range(1, reps):
        plane[e] = flipped(hats[e], "rep", e)
    grads = after(value_grad[0].reshape(tokens, -1), hats[0])
    slots = [grads] + [cyclic(grads, "fsdp", j) for j in range(1, groups)]

    plane[0] = after(plane[0], *slots[1:])
    sent = regrouped(plane, groups)
    back = returned_blocks(slots, weight, norm_gain, micro)
    lines = [[back[j][m] for j in range(groups)] for m in range(micro)]
    far = groups // 2
    near = [j for j in range(1, groups) if j != far]
    columns = list(sent)
    for j in near:
        columns[j] = cyclic(sent[j], "fsdp", j)
    columns[far] = cyclic(after(sent[far], back[0][0], *[columns[j] for j in near]), "fsdp", far)
    held = after(joined(slots), sent[0])
    values = [held if e == 0 else flipped(held, "rep", e) for e in range(reps)]

    def send_back(m, j, *ties):
        lines[m][j] = cyclic(after(lines[m][j], *ties), "fsdp", -j)

    send_back(0, far, columns[far])
    for j in near:
        send_back(0, j, columns[far])
    send_back(1, near[0], lines[0][far])
    for j in near[1:]:
        send_back(1, j, lines[1][near[0]])
    send_back(1, far, *[lines[0][j] for j in near])
    sums = weight_product(columns, values, weight, norm_gain, rep, groups, chunks, norm_scale)
    gathered = [doubled(sums[c], orders[c]) for c in range(chunks)]
    finished = ()
    for half in (0, 1):
        for c in range(chunks):
            finished = finished_half(gathered[c][half], rep, orders[c], half, c, chunks, finished)
        if half == 0:
            early = finished
    weight_grad, gain_grad = finished

    result = ()
    for m in range(micro):
        ties = [*finished, *result] if m else [lines[1][near[-1]], *[g[0] for g in gathered]]
        lines[m][0] = after(lines[m][0], *ties)
        upper, piece = row_gradient(layer_input, top_grad, lines[m], me, m)
        passed = lax.ppermute(upper, "section", [(1, 0)])
        result = (input_gradient(upper, piece, passed, is_upper, layer_input.shape, m, result),)
    return (result[0], weight_grad[None], gain_grad)


def solution(mesh):
    return jax.shard_map(
        local,
        mesh=mesh,
        in_specs=(
            P("section", None, ("rep", "fsdp"), None),
            P("section", None, ("rep", "fsdp"), None),
            P("section", "fsdp", None),
            P("section", "fsdp"),
            P(None, ("rep", "fsdp"), None),
        ),
        out_specs=(
            P("section", None, ("rep", "fsdp"), None),
            P("section", "fsdp", None),
            P("section", "fsdp"),
        ),
        check_vma=False,
    )
```

```python
import jax
import jax.numpy as jnp
from jax import lax
from jax.experimental import pallas as pl
from jax.experimental.pallas import tpu as pltpu
from jax.sharding import PartitionSpec as P

norm_eps = 1e-05
bf16 = jnp.bfloat16
f32 = jnp.float32
MIB = 1 << 20
SMEM_ARG = pl.BlockSpec(memory_space=pltpu.SMEM)
ANY_ARG = pl.BlockSpec(memory_space=pl.ANY)


def cyclic(value, axis, steps):
    count = lax.axis_size(axis)
    return lax.ppermute(value, axis, [(i, (i + steps) % count) for i in range(count)])


def flipped(value, axis, mask):
    count = lax.axis_size(axis)
    return lax.ppermute(value, axis, [(i, i ^ mask) for i in range(count)])


def after(value, *others):
    return lax.optimization_barrier((value, *others))[0]


def params(mib):
    return pltpu.CompilerParams(vmem_limit_bytes=mib * MIB)


def cost(flops, bytes_accessed):
    return pl.CostEstimate(flops=int(flops), bytes_accessed=int(bytes_accessed), transcendentals=0)


def scaled_blocks(x, me, rep, groups, reps, chunks):
    tokens, width = x.shape
    shard = width // groups
    piece = shard // reps
    chunk = piece // chunks
    if chunk % 128:
        x = x.astype(f32)
        hat = (x * lax.rsqrt(jnp.mean(x * x, axis=1, keepdims=True) + norm_eps)).astype(bf16)
        hat = jnp.roll(hat.reshape(tokens, groups, reps, chunks, chunk), -me[0], axis=1)
        take = lambda e, c: lax.dynamic_index_in_dim(hat, rep[0] ^ e, 2, False)[:, :, c].reshape(tokens, groups * chunk)
        return [[take(e, c) for e in range(reps)] for c in range(chunks)]
    step = 16
    block = min(tokens, 32)

    def kernel(me_ref, rep_ref, x_ref, *out_refs):
        span = min(shard, 512)
        for row in range(0, block, step):
            rows = slice(row, row + step)
            total = jnp.zeros((step, 128), f32)
            for c in range(0, width, span):
                v = x_ref[rows, c : c + span].astype(f32)
                v = v * v
                for k in range(0, span, 128):
                    total = total + v[:, k : k + 128]
            scale = lax.rsqrt(jnp.sum(total, axis=1, keepdims=True) / width + norm_eps)
            for c in range(chunks):
                for e in range(reps):
                    for j in range(groups):
                        at = lax.rem(me_ref[0] + j, groups) * shard + (rep_ref[0] ^ e) * piece + c * chunk
                        v = x_ref[rows, pl.ds(pl.multiple_of(at, chunk), chunk)].astype(f32)
                        out_refs[c * reps + e][rows, j * chunk : (j + 1) * chunk] = (v * scale).astype(bf16)

    outs = pl.pallas_call(
        kernel,
        grid=(tokens // block,),
        out_shape=[jax.ShapeDtypeStruct((tokens, groups * chunk), bf16)] * (chunks * reps),
        in_specs=[SMEM_ARG, SMEM_ARG, pl.BlockSpec((block, width), lambda i: (i, 0))],
        out_specs=[pl.BlockSpec((block, groups * chunk), lambda i: (i, 0))] * (chunks * reps),
        compiler_params=params(8),
        cost_estimate=cost(6 * x.size, 4 * x.size),
        name="scaled_blocks",
    )(me, rep, x)
    return [list(outs[c * reps : (c + 1) * reps]) for c in range(chunks)]


def joined(arrays):
    rows, width = arrays[0].shape
    if rows % 16 or width % 128:
        return jnp.concatenate(arrays, axis=0)

    def kernel(*refs):
        copies = []
        for k in range(len(arrays)):
            target = refs[-2].at[k * rows : (k + 1) * rows, :]
            copies.append(pltpu.make_async_copy(refs[k], target, refs[-1].at[k]))
            copies[-1].start()
        for copy in copies:
            copy.wait()

    return pl.pallas_call(
        kernel,
        out_shape=jax.ShapeDtypeStruct((len(arrays) * rows, width), bf16),
        in_specs=[ANY_ARG] * len(arrays),
        out_specs=ANY_ARG,
        scratch_shapes=[pltpu.SemaphoreType.DMA((len(arrays),))],
        compiler_params=params(4),
        cost_estimate=cost(0, 4 * len(arrays) * rows * width),
        name="joined",
    )(*arrays)


def doubled(value, order):
    for bit in order[:-1]:
        value = joined([value, flipped(value, "rep", 1 << bit)])
    return value, flipped(value, "rep", 1 << order[-1])


def mask_of(pos, order):
    return sum(((pos >> i) & 1) << bit for i, bit in enumerate(order))


def regrouped(blocks, groups):
    tokens, width = blocks[0].shape
    chunk = width // groups
    reps = len(blocks)
    if chunk % 128:
        return [jnp.concatenate([b[:, j * chunk : (j + 1) * chunk] for b in blocks], axis=0) for j in range(groups)]

    def kernel(*refs):
        copies = []
        for e in range(reps):
            for j in range(groups):
                source = refs[e].at[:, j * chunk : (j + 1) * chunk]
                target = refs[reps + j].at[e * tokens : (e + 1) * tokens, :]
                copies.append(pltpu.make_async_copy(source, target, refs[-1].at[e * groups + j]))
                copies[-1].start()
        for copy in copies:
            copy.wait()

    return list(
        pl.pallas_call(
            kernel,
            out_shape=[jax.ShapeDtypeStruct((reps * tokens, chunk), bf16)] * groups,
            in_specs=[ANY_ARG] * reps,
            out_specs=[ANY_ARG] * groups,
            scratch_shapes=[pltpu.SemaphoreType.DMA((reps * groups,))],
            compiler_params=params(8),
            cost_estimate=cost(0, 4 * reps * tokens * width),
            name="regrouped",
        )(*blocks)
    )


def weight_product(columns, values, weight, gain, rep, groups, count, norm_scale):
    rows, width = columns[0].shape
    reps = len(values)
    tokens = rows // reps
    features = values[0].shape[1]
    chunk = width // count
    contract = (((0,), (0,)), ((), ()))

    def thirds(row):
        first = row.astype(bf16)
        rest = row - first.astype(f32)
        second = rest.astype(bf16)
        return first, second, (rest - second.astype(f32)).astype(bf16)

    if chunk % 128:
        order = jnp.stack([v.reshape(groups, tokens, features) for v in values], axis=1)
        raw = lax.dot_general(
            jnp.concatenate(columns, axis=0), order.reshape(-1, features), contract, preferred_element_type=f32
        )
        own = lax.dynamic_slice_in_dim(weight, rep[0] * width, width, 0).astype(f32)
        dots = jnp.sum(raw * own, axis=1) * norm_scale
        factor = lax.dynamic_slice_in_dim(gain[0], rep[0] * width, width, 0).astype(f32) * norm_scale
        raw = (raw * factor[:, None]).astype(bf16)
        outs = []
        for c in range(count):
            at = slice(c * chunk, (c + 1) * chunk)
            under = jnp.stack(thirds(dots[at]) + (jnp.zeros((chunk,), bf16),) * 13)
            outs.append(jnp.concatenate([raw[at], jnp.pad(under, ((0, 0), (0, features - chunk)))], axis=0))
        return outs

    def kernel(rep_ref, *refs):
        column_refs, value_refs = refs[:groups], refs[groups : groups + reps]
        weight_ref, gain_ref = refs[groups + reps], refs[groups + reps + 1]
        out_refs, total = refs[groups + reps + 2 : -1], refs[-1]
        start = pl.multiple_of(rep_ref[0] * width, width)
        for j in range(groups):
            right = jnp.concatenate([v[j * tokens : (j + 1) * tokens, :] for v in value_refs], axis=0)
            for c in range(count):
                block = column_refs[j][:, c * chunk : (c + 1) * chunk]
                product = lax.dot_general(block, right, contract, preferred_element_type=f32)
                if j == 0:
                    total[c] = product
                else:
                    total[c] += product
        for c in range(count):
            at = pl.ds(pl.multiple_of(start + c * chunk, chunk), chunk)
            raw = total[c]
            factor = gain_ref[:, at].astype(f32) * norm_scale
            factor = jnp.transpose(jnp.broadcast_to(factor, (128, chunk)))[:, 0:1]
            out_refs[c][:chunk, :] = (raw * factor).astype(bf16)
            terms = raw * weight_ref[at, :].astype(f32)
            terms = sum(terms[:, k : k + 128] for k in range(0, features, 128))
            dots = lax.dot_general(
                jnp.full((8, 128), norm_scale, f32),
                terms,
                (((1,), (1,)), ((), ())),
                precision=lax.Precision.HIGHEST,
                preferred_element_type=f32,
            )
            under = jnp.concatenate([row[0:1, :].astype(f32) for row in thirds(dots)] + [jnp.zeros((13, chunk), f32)], axis=0)
            out_refs[c][chunk:, :chunk] = under.astype(bf16)
            out_refs[c][chunk:, chunk:] = jnp.zeros((16, features - chunk), bf16)

    vmem = pl.BlockSpec(memory_space=pltpu.VMEM)
    return pl.pallas_call(
        kernel,
        out_shape=[jax.ShapeDtypeStruct((chunk + 16, features), bf16)] * count,
        in_specs=[SMEM_ARG] + [vmem] * (groups + reps + 2),
        out_specs=[vmem] * count,
        scratch_shapes=[pltpu.VMEM((count, chunk, features), f32)],
        compiler_params=params(24),
        cost_estimate=cost(2 * groups * rows * width * features, 2 * groups * rows * (width + features) + 4 * width * features),
        name="weight_product",
    )(rep, *columns, *values, weight, gain)


def returned_blocks(slots, weight, gain, micro, far):
    groups = len(slots)
    tokens, features = slots[0].shape
    counts = [micro if j == far else 1 for j in range(groups)]
    starts = [sum(counts[:j]) for j in range(groups)]
    parts = [tokens // n for n in counts for _ in range(n)]
    shard = weight.shape[0]
    tile = min(shard, 512)

    def kernel(*refs):
        slot_refs, weight_ref, gain_ref = refs[:groups], refs[groups], refs[groups + 1]
        out_refs = refs[groups + 2 :]
        factor = gain_ref[...].astype(f32)
        pair = 2 if groups % 2 == 0 else 1
        out_refs = [out_refs[at : at + n] for at, n in zip(starts, counts)]
        for j in range(0, groups, pair):
            values = jnp.concatenate([slot_refs[j + i][...] for i in range(pair)], axis=0)
            back = lax.dot_general(values, weight_ref[...], (((1,), (1,)), ((), ())), preferred_element_type=f32)
            back = (back * factor).astype(bf16)
            for i in range(pair):
                part = tokens // counts[j + i]
                for m in range(counts[j + i]):
                    at = i * tokens + m * part
                    out_refs[j + i][m][...] = back[at : at + part, :]

    outs = pl.pallas_call(
        kernel,
        grid=(shard // tile,),
        out_shape=[jax.ShapeDtypeStruct((part, shard), bf16) for part in parts],
        in_specs=[pl.BlockSpec((tokens, features), lambda i: (0, 0))] * groups
        + [pl.BlockSpec((tile, features), lambda i: (i, 0)), pl.BlockSpec((1, tile), lambda i: (0, i))],
        out_specs=[pl.BlockSpec((part, tile), lambda i: (0, i)) for part in parts],
        compiler_params=params(8),
        cost_estimate=cost(2 * groups * tokens * shard * features, 2 * groups * tokens * (shard + features) + 2 * shard * features),
        name="returned_blocks",
    )(*slots, weight, gain)
    return [list(outs[at : at + n]) for at, n in zip(starts, counts)]


def row_gradient(x, top, blocks, me, m):
    groups = len(blocks)
    shard = blocks[0].shape[1]
    rows = x.shape[2]
    width = shard * groups
    step = 16

    def block_spec(block):
        base = m * rows // step if block.shape[0] > rows else 0
        return pl.BlockSpec((step, shard), lambda i: (base + i, 0))

    def kernel(me_ref, x_ref, top_ref, *refs):
        block_refs, upper_ref, piece_ref = refs[:groups], refs[groups], refs[groups + 1]
        squares = jnp.zeros((step, 128), f32)
        dots = jnp.zeros((step, 128), f32)
        starts = [pl.multiple_of(lax.rem(me_ref[0] + j, groups) * shard, shard) for j in range(groups)]
        span = min(shard, 512)
        for j in range(groups):
            for c in range(0, shard, span):
                v = x_ref[0, 0, :, pl.ds(pl.multiple_of(starts[j] + c, span), span)].astype(f32)
                d = block_refs[j][:, c : c + span].astype(f32) * v
                v = v * v
                for k in range(0, span, 128):
                    squares = squares + v[:, k : k + 128]
                    dots = dots + d[:, k : k + 128]
        scale = lax.rsqrt(jnp.sum(squares, axis=1, keepdims=True) / width + norm_eps)
        mean = jnp.sum(dots, axis=1, keepdims=True) * scale / width
        slope = scale * mean
        for j in range(groups):
            for c in range(0, shard, span):
                at = pl.ds(pl.multiple_of(starts[j] + c, span), span)
                v = x_ref[0, 0, :, at].astype(f32)
                piece = (scale * (block_refs[j][:, c : c + span].astype(f32) - v * slope)).astype(bf16)
                piece_ref[:, at] = piece
                upper_ref[:, at] = (top_ref[0, :, at].astype(f32) + piece.astype(f32)).astype(bf16)

    return pl.pallas_call(
        kernel,
        grid=(rows // step,),
        out_shape=[jax.ShapeDtypeStruct((rows, width), bf16)] * 2,
        in_specs=[
            SMEM_ARG,
            pl.BlockSpec((1, 1, step, width), lambda i: (0, m, i, 0)),
            pl.BlockSpec((1, step, width), lambda i: (m, i, 0)),
        ]
        + [block_spec(block) for block in blocks],
        out_specs=[pl.BlockSpec((step, width), lambda i: (i, 0))] * 2,
        compiler_params=params(8),
        cost_estimate=cost(12 * rows * width, 10 * rows * width),
        name="row_gradient",
    )(me, x, top, *blocks)


def input_gradient(upper, piece, passed, is_upper, shape, m, earlier):
    rows, width = upper.shape
    step = min(rows, 32)

    def kernel(is_upper_ref, upper_ref, piece_ref, passed_ref, *refs):
        lower = (passed_ref[...].astype(f32) + piece_ref[...].astype(f32)).astype(bf16)
        refs[-1][0, 0] = jnp.where(is_upper_ref[0] == 1, upper_ref[...], lower)

    spec = pl.BlockSpec((step, width), lambda i: (i, 0))
    return pl.pallas_call(
        kernel,
        grid=(rows // step,),
        out_shape=jax.ShapeDtypeStruct(shape, bf16),
        in_specs=[SMEM_ARG, spec, spec, spec] + [ANY_ARG] * len(earlier),
        out_specs=pl.BlockSpec((1, 1, step, width), lambda i: (0, m, i, 0)),
        input_output_aliases={4: 0} if earlier else {},
        compiler_params=params(8),
        cost_estimate=cost(4 * rows * width, 8 * rows * width),
        name="input_gradient",
    )(is_upper, upper, piece, passed, *earlier)


def finished_half(sums, rep, order, half, c, chunks, earlier):
    pieces = (1 << len(order)) // 2
    rows = sums.shape[0] // pieces - 16
    features = sums.shape[1]
    shard = rows * chunks * pieces * 2

    def place(i, rep_ref):
        return (rep_ref[0] ^ mask_of(i + half * pieces, order)) * chunks + c

    def total(under):
        return under[0:1, :rows] + under[1:2, :rows] + under[2:3, :rows]

    if rows % 128:
        earlier = earlier or (jnp.zeros((shard, features), f32), jnp.zeros((1, shard), f32))
        for i in range(pieces):
            piece = sums[i * (rows + 16) : (i + 1) * (rows + 16)].astype(f32)
            at = place(i, rep) * rows
            earlier = (
                lax.dynamic_update_slice(earlier[0], piece[:rows], (at, 0)),
                lax.dynamic_update_slice(earlier[1], total(piece[rows:]), (0, at)),
            )
        return earlier

    def kernel(rep_ref, sum_ref, *refs):
        refs[-2][...] = sum_ref[:rows, :].astype(f32)
        refs[-1][...] = total(sum_ref[rows:, :].astype(f32))

    return pl.pallas_call(
        kernel,
        grid_spec=pltpu.PrefetchScalarGridSpec(
            num_scalar_prefetch=1,
            grid=(pieces,),
            in_specs=[pl.BlockSpec((rows + 16, features), lambda i, rep_ref: (i, 0))] + [ANY_ARG] * len(earlier),
            out_specs=[
                pl.BlockSpec((rows, features), lambda i, rep_ref: (place(i, rep_ref), 0)),
                pl.BlockSpec((1, rows), lambda i, rep_ref: (0, place(i, rep_ref))),
            ],
        ),
        out_shape=[jax.ShapeDtypeStruct((shard, features), f32), jax.ShapeDtypeStruct((1, shard), f32)],
        input_output_aliases={2: 0, 3: 1} if earlier else {},
        compiler_params=params(8),
        cost_estimate=cost(sums.size, 6 * sums.size),
        name="finished_half",
    )(rep, sums, *earlier)


def local(layer_input, value_grad, value_weight, norm_gain, top_grad):
    groups = lax.axis_size("fsdp")
    reps = lax.axis_size("rep")
    bits = reps.bit_length() - 1
    me = lax.axis_index("fsdp").astype(jnp.int32)[None]
    rep = lax.axis_index("rep").astype(jnp.int32)[None]
    _, micro, rows, width = layer_input.shape
    tokens = micro * rows
    norm_scale = float(tokens * reps * groups) ** (-0.5)
    chunks = 2
    orders = [tuple(range(bits)), tuple(reversed(range(bits)))]

    weight = value_weight[0]
    is_upper = lax.axis_index("section").astype(jnp.int32)[None]
    inputs = after(layer_input[0].reshape(tokens, width), me, rep, is_upper)

    hats = scaled_blocks(inputs, me, rep, groups, reps, 1)[0]
    plane = list(hats)
    for e in range(1, reps):
        plane[e] = flipped(hats[e], "rep", e)
    grads = after(value_grad[0].reshape(tokens, -1), hats[0])
    slots = [grads] + [cyclic(grads, "fsdp", j) for j in range(1, groups)]

    plane[0] = after(plane[0], *slots[1:])
    sent = regrouped(plane, groups)
    far = groups // 2
    near = [j for j in range(1, groups) if j != far]
    back = returned_blocks(slots, weight, norm_gain, micro, far)
    columns = list(sent)
    columns[far] = cyclic(sent[far], "fsdp", far)
    columns[near[0]] = cyclic(sent[near[0]], "fsdp", near[0])
    for j in near[1:]:
        columns[j] = cyclic(after(sent[j], back[0][0], columns[near[0]]), "fsdp", j)
    held = after(joined(slots), sent[0])
    values = [held if e == 0 else flipped(held, "rep", e) for e in range(reps)]

    lines = [list(arrays) for arrays in back]

    def send_back(j, m, *ties):
        lines[j][m] = cyclic(after(lines[j][m], *ties), "fsdp", -j)

    send_back(far, 0, columns[far])
    send_back(near[-1], 0, columns[far])
    for j in near[:-1]:
        send_back(j, 0, lines[far][0])
    for m in range(1, micro):
        send_back(far, m, lines[far][m - 1])
    sums = weight_product(columns, values, weight, norm_gain, rep, groups, chunks, norm_scale)
    gathered = [doubled(sums[c], orders[c]) for c in range(chunks)]
    finished = ()
    for half in (0, 1):
        for c in range(chunks):
            finished = finished_half(gathered[c][half], rep, orders[c], half, c, chunks, finished)
        if half == 0:
            early = finished
    weight_grad, gain_grad = finished

    uppers = []
    for m in range(micro):
        line = [arrays[m if j == far else 0] for j, arrays in enumerate(lines)]
        line[0] = after(line[0], *([*early] if m else [*early]))
        line[0] = after(line[0], *[u for u, _ in uppers])
        uppers.append(row_gradient(layer_input, top_grad, line, me, m))
    result = ()
    for m, (upper, piece) in enumerate(uppers):
        passed = lax.ppermute(upper, "section", [(1, 0)])
        piece = after(piece, *finished)
        result = (input_gradient(upper, piece, passed, is_upper, layer_input.shape, m, result),)
    return (result[0], weight_grad[None], gain_grad)


def solution(mesh):
    return jax.shard_map(
        local,
        mesh=mesh,
        in_specs=(
            P("section", None, ("rep", "fsdp"), None),
            P("section", None, ("rep", "fsdp"), None),
            P("section", "fsdp", None),
            P("section", "fsdp"),
            P(None, ("rep", "fsdp"), None),
        ),
        out_specs=(
            P("section", None, ("rep", "fsdp"), None),
            P("section", "fsdp", None),
            P("section", "fsdp"),
        ),
        check_vma=False,
    )
```

```python
import jax
import jax.numpy as jnp
from jax import lax
from jax.experimental import pallas as pl
from jax.experimental.pallas import tpu as pltpu
from jax.sharding import PartitionSpec as P

norm_eps = 1e-05
bf16 = jnp.bfloat16
f32 = jnp.float32
MIB = 1 << 20
SMEM_ARG = pl.BlockSpec(memory_space=pltpu.SMEM)
ANY_ARG = pl.BlockSpec(memory_space=pl.ANY)


def cyclic(value, axis, steps):
    count = lax.axis_size(axis)
    return lax.ppermute(value, axis, [(i, (i + steps) % count) for i in range(count)])


def flipped(value, axis, mask):
    count = lax.axis_size(axis)
    return lax.ppermute(value, axis, [(i, i ^ mask) for i in range(count)])


def after(value, *others):
    return lax.optimization_barrier((value, *others))[0]


def params(mib):
    return pltpu.CompilerParams(vmem_limit_bytes=mib * MIB)


def cost(flops, bytes_accessed):
    return pl.CostEstimate(flops=int(flops), bytes_accessed=int(bytes_accessed), transcendentals=0)


def scaled_blocks(x, me, rep, groups, reps, chunks):
    tokens, width = x.shape
    shard = width // groups
    piece = shard // reps
    chunk = piece // chunks
    if chunk % 128:
        x = x.astype(f32)
        hat = (x * lax.rsqrt(jnp.mean(x * x, axis=1, keepdims=True) + norm_eps)).astype(bf16)
        hat = jnp.roll(hat.reshape(tokens, groups, reps, chunks, chunk), -me[0], axis=1)
        take = lambda e, c: lax.dynamic_index_in_dim(hat, rep[0] ^ e, 2, False)[:, :, c].reshape(tokens, groups * chunk)
        return [[take(e, c) for e in range(reps)] for c in range(chunks)]
    step = 16
    block = min(tokens, 32)

    def kernel(me_ref, rep_ref, x_ref, *out_refs):
        span = min(shard, 512)
        for row in range(0, block, step):
            rows = slice(row, row + step)
            total = jnp.zeros((step, 128), f32)
            for c in range(0, width, span):
                v = x_ref[rows, c : c + span].astype(f32)
                v = v * v
                for k in range(0, span, 128):
                    total = total + v[:, k : k + 128]
            scale = lax.rsqrt(jnp.sum(total, axis=1, keepdims=True) / width + norm_eps)
            for c in range(chunks):
                for e in range(reps):
                    for j in range(groups):
                        at = lax.rem(me_ref[0] + j, groups) * shard + (rep_ref[0] ^ e) * piece + c * chunk
                        v = x_ref[rows, pl.ds(pl.multiple_of(at, chunk), chunk)].astype(f32)
                        out_refs[c * reps + e][rows, j * chunk : (j + 1) * chunk] = (v * scale).astype(bf16)

    outs = pl.pallas_call(
        kernel,
        grid=(tokens // block,),
        out_shape=[jax.ShapeDtypeStruct((tokens, groups * chunk), bf16)] * (chunks * reps),
        in_specs=[SMEM_ARG, SMEM_ARG, pl.BlockSpec((block, width), lambda i: (i, 0))],
        out_specs=[pl.BlockSpec((block, groups * chunk), lambda i: (i, 0))] * (chunks * reps),
        compiler_params=params(8),
        cost_estimate=cost(6 * x.size, 4 * x.size),
        name="scaled_blocks",
    )(me, rep, x)
    return [list(outs[c * reps : (c + 1) * reps]) for c in range(chunks)]


def joined(arrays):
    rows, width = arrays[0].shape
    if rows % 16 or width % 128:
        return jnp.concatenate(arrays, axis=0)

    def kernel(*refs):
        copies = []
        for k in range(len(arrays)):
            target = refs[-2].at[k * rows : (k + 1) * rows, :]
            copies.append(pltpu.make_async_copy(refs[k], target, refs[-1].at[k]))
            copies[-1].start()
        for copy in copies:
            copy.wait()

    return pl.pallas_call(
        kernel,
        out_shape=jax.ShapeDtypeStruct((len(arrays) * rows, width), bf16),
        in_specs=[ANY_ARG] * len(arrays),
        out_specs=ANY_ARG,
        scratch_shapes=[pltpu.SemaphoreType.DMA((len(arrays),))],
        compiler_params=params(4),
        cost_estimate=cost(0, 4 * len(arrays) * rows * width),
        name="joined",
    )(*arrays)


def doubled(value, order):
    for bit in order[:-1]:
        value = joined([value, flipped(value, "rep", 1 << bit)])
    return value, flipped(value, "rep", 1 << order[-1])


def mask_of(pos, order):
    return sum(((pos >> i) & 1) << bit for i, bit in enumerate(order))


def regrouped(blocks, groups):
    tokens, width = blocks[0].shape
    chunk = width // groups
    reps = len(blocks)
    if chunk % 128:
        return [jnp.concatenate([b[:, j * chunk : (j + 1) * chunk] for b in blocks], axis=0) for j in range(groups)]

    def kernel(*refs):
        copies = []
        for e in range(reps):
            for j in range(groups):
                source = refs[e].at[:, j * chunk : (j + 1) * chunk]
                target = refs[reps + j].at[e * tokens : (e + 1) * tokens, :]
                copies.append(pltpu.make_async_copy(source, target, refs[-1].at[e * groups + j]))
                copies[-1].start()
        for copy in copies:
            copy.wait()

    return list(
        pl.pallas_call(
            kernel,
            out_shape=[jax.ShapeDtypeStruct((reps * tokens, chunk), bf16)] * groups,
            in_specs=[ANY_ARG] * reps,
            out_specs=[ANY_ARG] * groups,
            scratch_shapes=[pltpu.SemaphoreType.DMA((reps * groups,))],
            compiler_params=params(8),
            cost_estimate=cost(0, 4 * reps * tokens * width),
            name="regrouped",
        )(*blocks)
    )


def weight_product(columns, values, weight, gain, rep, groups, count, norm_scale):
    rows, width = columns[0].shape
    reps = len(values)
    tokens = rows // reps
    features = values[0].shape[1]
    chunk = width // count
    contract = (((0,), (0,)), ((), ()))

    def thirds(row):
        first = row.astype(bf16)
        rest = row - first.astype(f32)
        second = rest.astype(bf16)
        return first, second, (rest - second.astype(f32)).astype(bf16)

    if chunk % 128:
        order = jnp.stack([v.reshape(groups, tokens, features) for v in values], axis=1)
        raw = lax.dot_general(
            jnp.concatenate(columns, axis=0), order.reshape(-1, features), contract, preferred_element_type=f32
        )
        own = lax.dynamic_slice_in_dim(weight, rep[0] * width, width, 0).astype(f32)
        dots = jnp.sum(raw * own, axis=1) * norm_scale
        factor = lax.dynamic_slice_in_dim(gain[0], rep[0] * width, width, 0).astype(f32) * norm_scale
        raw = (raw * factor[:, None]).astype(bf16)
        outs = []
        for c in range(count):
            at = slice(c * chunk, (c + 1) * chunk)
            under = jnp.stack(thirds(dots[at]) + (jnp.zeros((chunk,), bf16),) * 13)
            outs.append(jnp.concatenate([raw[at], jnp.pad(under, ((0, 0), (0, features - chunk)))], axis=0))
        return outs

    def kernel(rep_ref, *refs):
        column_refs, value_refs = refs[:groups], refs[groups : groups + reps]
        weight_ref, gain_ref = refs[groups + reps], refs[groups + reps + 1]
        out_refs, total = refs[groups + reps + 2 : -1], refs[-1]
        start = pl.multiple_of(rep_ref[0] * width, width)
        for j in range(groups):
            right = jnp.concatenate([v[j * tokens : (j + 1) * tokens, :] for v in value_refs], axis=0)
            for c in range(count):
                block = column_refs[j][:, c * chunk : (c + 1) * chunk]
                product = lax.dot_general(block, right, contract, preferred_element_type=f32)
                if j == 0:
                    total[c] = product
                else:
                    total[c] += product
        for c in range(count):
            at = pl.ds(pl.multiple_of(start + c * chunk, chunk), chunk)
            raw = total[c]
            factor = gain_ref[:, at].astype(f32) * norm_scale
            factor = jnp.transpose(jnp.broadcast_to(factor, (128, chunk)))[:, 0:1]
            out_refs[c][:chunk, :] = (raw * factor).astype(bf16)
            terms = raw * weight_ref[at, :].astype(f32)
            terms = sum(terms[:, k : k + 128] for k in range(0, features, 128))
            dots = lax.dot_general(
                jnp.full((8, 128), norm_scale, f32),
                terms,
                (((1,), (1,)), ((), ())),
                precision=lax.Precision.HIGHEST,
                preferred_element_type=f32,
            )
            under = jnp.concatenate([row[0:1, :].astype(f32) for row in thirds(dots)] + [jnp.zeros((13, chunk), f32)], axis=0)
            out_refs[c][chunk:, :chunk] = under.astype(bf16)
            out_refs[c][chunk:, chunk:] = jnp.zeros((16, features - chunk), bf16)

    vmem = pl.BlockSpec(memory_space=pltpu.VMEM)
    return pl.pallas_call(
        kernel,
        out_shape=[jax.ShapeDtypeStruct((chunk + 16, features), bf16)] * count,
        in_specs=[SMEM_ARG] + [vmem] * (groups + reps + 2),
        out_specs=[vmem] * count,
        scratch_shapes=[pltpu.VMEM((count, chunk, features), f32)],
        compiler_params=params(24),
        cost_estimate=cost(2 * groups * rows * width * features, 2 * groups * rows * (width + features) + 4 * width * features),
        name="weight_product",
    )(rep, *columns, *values, weight, gain)


def returned_blocks(slots, weight, gain, micro, far):
    groups = len(slots)
    tokens, features = slots[0].shape
    counts = [micro if j == far else 1 for j in range(groups)]
    starts = [sum(counts[:j]) for j in range(groups)]
    parts = [tokens // n for n in counts for _ in range(n)]
    shard = weight.shape[0]
    tile = min(shard, 512)

    def kernel(*refs):
        slot_refs, weight_ref, gain_ref = refs[:groups], refs[groups], refs[groups + 1]
        out_refs = refs[groups + 2 :]
        factor = gain_ref[...].astype(f32)
        pair = 2 if groups % 2 == 0 else 1
        out_refs = [out_refs[at : at + n] for at, n in zip(starts, counts)]
        for j in range(0, groups, pair):
            values = jnp.concatenate([slot_refs[j + i][...] for i in range(pair)], axis=0)
            back = lax.dot_general(values, weight_ref[...], (((1,), (1,)), ((), ())), preferred_element_type=f32)
            back = (back * factor).astype(bf16)
            for i in range(pair):
                part = tokens // counts[j + i]
                for m in range(counts[j + i]):
                    at = i * tokens + m * part
                    out_refs[j + i][m][...] = back[at : at + part, :]

    outs = pl.pallas_call(
        kernel,
        grid=(shard // tile,),
        out_shape=[jax.ShapeDtypeStruct((part, shard), bf16) for part in parts],
        in_specs=[pl.BlockSpec((tokens, features), lambda i: (0, 0))] * groups
        + [pl.BlockSpec((tile, features), lambda i: (i, 0)), pl.BlockSpec((1, tile), lambda i: (0, i))],
        out_specs=[pl.BlockSpec((part, tile), lambda i: (0, i)) for part in parts],
        compiler_params=params(8),
        cost_estimate=cost(2 * groups * tokens * shard * features, 2 * groups * tokens * (shard + features) + 2 * shard * features),
        name="returned_blocks",
    )(*slots, weight, gain)
    return [list(outs[at : at + n]) for at, n in zip(starts, counts)]


def row_gradient(x, top, blocks, me, m):
    groups = len(blocks)
    shard = blocks[0].shape[1]
    rows = x.shape[2]
    width = shard * groups
    step = 16

    def block_spec(block):
        base = m * rows // step if block.shape[0] > rows else 0
        return pl.BlockSpec((step, shard), lambda i: (base + i, 0))

    def kernel(me_ref, x_ref, top_ref, *refs):
        block_refs, upper_ref, piece_ref = refs[:groups], refs[groups], refs[groups + 1]
        squares = jnp.zeros((step, 128), f32)
        dots = jnp.zeros((step, 128), f32)
        starts = [pl.multiple_of(lax.rem(me_ref[0] + j, groups) * shard, shard) for j in range(groups)]
        span = min(shard, 512)
        for j in range(groups):
            for c in range(0, shard, span):
                v = x_ref[0, 0, :, pl.ds(pl.multiple_of(starts[j] + c, span), span)].astype(f32)
                d = block_refs[j][:, c : c + span].astype(f32) * v
                v = v * v
                for k in range(0, span, 128):
                    squares = squares + v[:, k : k + 128]
                    dots = dots + d[:, k : k + 128]
        scale = lax.rsqrt(jnp.sum(squares, axis=1, keepdims=True) / width + norm_eps)
        mean = jnp.sum(dots, axis=1, keepdims=True) * scale / width
        slope = scale * mean
        for j in range(groups):
            for c in range(0, shard, span):
                at = pl.ds(pl.multiple_of(starts[j] + c, span), span)
                v = x_ref[0, 0, :, at].astype(f32)
                piece = (scale * (block_refs[j][:, c : c + span].astype(f32) - v * slope)).astype(bf16)
                piece_ref[:, at] = piece
                upper_ref[:, at] = (top_ref[0, :, at].astype(f32) + piece.astype(f32)).astype(bf16)

    return pl.pallas_call(
        kernel,
        grid=(rows // step,),
        out_shape=[jax.ShapeDtypeStruct((rows, width), bf16)] * 2,
        in_specs=[
            SMEM_ARG,
            pl.BlockSpec((1, 1, step, width), lambda i: (0, m, i, 0)),
            pl.BlockSpec((1, step, width), lambda i: (m, i, 0)),
        ]
        + [block_spec(block) for block in blocks],
        out_specs=[pl.BlockSpec((step, width), lambda i: (i, 0))] * 2,
        compiler_params=params(8),
        cost_estimate=cost(12 * rows * width, 10 * rows * width),
        name="row_gradient",
    )(me, x, top, *blocks)


def input_gradient(upper, piece, passed, is_upper, shape, m, earlier):
    rows, width = upper.shape
    step = min(rows, 32)

    def kernel(is_upper_ref, upper_ref, piece_ref, passed_ref, *refs):
        lower = (passed_ref[...].astype(f32) + piece_ref[...].astype(f32)).astype(bf16)
        refs[-1][0, 0] = jnp.where(is_upper_ref[0] == 1, upper_ref[...], lower)

    spec = pl.BlockSpec((step, width), lambda i: (i, 0))
    return pl.pallas_call(
        kernel,
        grid=(rows // step,),
        out_shape=jax.ShapeDtypeStruct(shape, bf16),
        in_specs=[SMEM_ARG, spec, spec, spec] + [ANY_ARG] * len(earlier),
        out_specs=pl.BlockSpec((1, 1, step, width), lambda i: (0, m, i, 0)),
        input_output_aliases={4: 0} if earlier else {},
        compiler_params=params(8),
        cost_estimate=cost(4 * rows * width, 8 * rows * width),
        name="input_gradient",
    )(is_upper, upper, piece, passed, *earlier)


def finished_half(sums, rep, order, half, c, chunks, earlier):
    pieces = (1 << len(order)) // 2
    rows = sums.shape[0] // pieces - 16
    features = sums.shape[1]
    shard = rows * chunks * pieces * 2

    def place(i, rep_ref):
        return (rep_ref[0] ^ mask_of(i + half * pieces, order)) * chunks + c

    def total(under):
        return under[0:1, :rows] + under[1:2, :rows] + under[2:3, :rows]

    if rows % 128:
        earlier = earlier or (jnp.zeros((shard, features), f32), jnp.zeros((1, shard), f32))
        for i in range(pieces):
            piece = sums[i * (rows + 16) : (i + 1) * (rows + 16)].astype(f32)
            at = place(i, rep) * rows
            earlier = (
                lax.dynamic_update_slice(earlier[0], piece[:rows], (at, 0)),
                lax.dynamic_update_slice(earlier[1], total(piece[rows:]), (0, at)),
            )
        return earlier

    def kernel(rep_ref, sum_ref, *refs):
        refs[-2][...] = sum_ref[:rows, :].astype(f32)
        refs[-1][...] = total(sum_ref[rows:, :].astype(f32))

    return pl.pallas_call(
        kernel,
        grid_spec=pltpu.PrefetchScalarGridSpec(
            num_scalar_prefetch=1,
            grid=(pieces,),
            in_specs=[pl.BlockSpec((rows + 16, features), lambda i, rep_ref: (i, 0))] + [ANY_ARG] * len(earlier),
            out_specs=[
                pl.BlockSpec((rows, features), lambda i, rep_ref: (place(i, rep_ref), 0)),
                pl.BlockSpec((1, rows), lambda i, rep_ref: (0, place(i, rep_ref))),
            ],
        ),
        out_shape=[jax.ShapeDtypeStruct((shard, features), f32), jax.ShapeDtypeStruct((1, shard), f32)],
        input_output_aliases={2: 0, 3: 1} if earlier else {},
        compiler_params=params(8),
        cost_estimate=cost(sums.size, 6 * sums.size),
        name="finished_half",
    )(rep, sums, *earlier)


def local(layer_input, value_grad, value_weight, norm_gain, top_grad):
    groups = lax.axis_size("fsdp")
    reps = lax.axis_size("rep")
    bits = reps.bit_length() - 1
    me = lax.axis_index("fsdp").astype(jnp.int32)[None]
    rep = lax.axis_index("rep").astype(jnp.int32)[None]
    _, micro, rows, width = layer_input.shape
    tokens = micro * rows
    norm_scale = float(tokens * reps * groups) ** (-0.5)
    chunks = 2
    orders = [tuple(range(bits)), tuple(reversed(range(bits)))]

    weight = value_weight[0]
    is_upper = lax.axis_index("section").astype(jnp.int32)[None]
    inputs = after(layer_input[0].reshape(tokens, width), me, rep, is_upper)

    hats = scaled_blocks(inputs, me, rep, groups, reps, 1)[0]
    plane = list(hats)
    for e in range(1, reps):
        plane[e] = flipped(hats[e], "rep", e)
    grads = after(value_grad[0].reshape(tokens, -1), hats[0])
    slots = [grads] + [cyclic(grads, "fsdp", j) for j in range(1, groups)]

    plane[0] = after(plane[0], *slots[1:])
    sent = regrouped(plane, groups)
    far = groups // 2
    near = [j for j in range(1, groups) if j != far]
    back = returned_blocks(slots, weight, norm_gain, micro, far)
    columns = list(sent)
    for j in near:
        columns[j] = cyclic(sent[j], "fsdp", j)
    columns[far] = cyclic(after(sent[far], back[0][0], *[columns[j] for j in near]), "fsdp", far)
    held = after(joined(slots), sent[0])
    values = [held if e == 0 else flipped(held, "rep", e) for e in range(reps)]

    lines = [list(arrays) for arrays in back]

    def send_back(j, m, *ties):
        lines[j][m] = cyclic(after(lines[j][m], *ties), "fsdp", -j)

    send_back(far, 0, columns[far])
    send_back(near[-1], 0, columns[far])
    for j in near[:-1]:
        send_back(j, 0, lines[far][0])
    for m in range(1, micro):
        send_back(far, m, lines[far][m - 1])
    sums = weight_product(columns, values, weight, norm_gain, rep, groups, chunks, norm_scale)
    gathered = [doubled(sums[c], orders[c]) for c in range(chunks)]
    finished = ()
    for half in (0, 1):
        for c in range(chunks):
            finished = finished_half(gathered[c][half], rep, orders[c], half, c, chunks, finished)
        if half == 0:
            early = finished
    weight_grad, gain_grad = finished

    uppers = []
    for m in range(micro):
        line = [arrays[m if j == far else 0] for j, arrays in enumerate(lines)]
        line[0] = after(line[0], *([*early] if m else [*early]))
        line[0] = after(line[0], *[u for u, _ in uppers])
        uppers.append(row_gradient(layer_input, top_grad, line, me, m))
    result = ()
    for m, (upper, piece) in enumerate(uppers):
        passed = lax.ppermute(upper, "section", [(1, 0)])
        piece = after(piece, *finished)
        result = (input_gradient(upper, piece, passed, is_upper, layer_input.shape, m, result),)
    return (result[0], weight_grad[None], gain_grad)


def solution(mesh):
    return jax.shard_map(
        local,
        mesh=mesh,
        in_specs=(
            P("section", None, ("rep", "fsdp"), None),
            P("section", None, ("rep", "fsdp"), None),
            P("section", "fsdp", None),
            P("section", "fsdp"),
            P(None, ("rep", "fsdp"), None),
        ),
        out_specs=(
            P("section", None, ("rep", "fsdp"), None),
            P("section", "fsdp", None),
            P("section", "fsdp"),
        ),
        check_vma=False,
    )
```

```python
import jax
import jax.numpy as jnp
from jax import lax
from jax.experimental import pallas as pl
from jax.experimental.pallas import tpu as pltpu
from jax.sharding import PartitionSpec as P

norm_eps = 1e-05
bf16 = jnp.bfloat16
f32 = jnp.float32
MIB = 1 << 20
SMEM_ARG = pl.BlockSpec(memory_space=pltpu.SMEM)
ANY_ARG = pl.BlockSpec(memory_space=pl.ANY)


def cyclic(value, axis, steps):
    count = lax.axis_size(axis)
    return lax.ppermute(value, axis, [(i, (i + steps) % count) for i in range(count)])


def flipped(value, axis, mask):
    count = lax.axis_size(axis)
    return lax.ppermute(value, axis, [(i, i ^ mask) for i in range(count)])


def after(value, *others):
    return lax.optimization_barrier((value, *others))[0]


def params(mib):
    return pltpu.CompilerParams(vmem_limit_bytes=mib * MIB)


def cost(flops, bytes_accessed):
    return pl.CostEstimate(flops=int(flops), bytes_accessed=int(bytes_accessed), transcendentals=0)


def scaled_blocks(x, me, rep, groups, reps, chunks):
    tokens, width = x.shape
    shard = width // groups
    piece = shard // reps
    chunk = piece // chunks
    if chunk % 128:
        x = x.astype(f32)
        hat = (x * lax.rsqrt(jnp.mean(x * x, axis=1, keepdims=True) + norm_eps)).astype(bf16)
        hat = jnp.roll(hat.reshape(tokens, groups, reps, chunks, chunk), -me[0], axis=1)
        take = lambda e, c: lax.dynamic_index_in_dim(hat, rep[0] ^ e, 2, False)[:, :, c].reshape(tokens, groups * chunk)
        return [[take(e, c) for e in range(reps)] for c in range(chunks)]
    step = 16
    block = min(tokens, 32)

    def kernel(me_ref, rep_ref, x_ref, *out_refs):
        span = min(shard, 512)
        for row in range(0, block, step):
            rows = slice(row, row + step)
            total = jnp.zeros((step, 128), f32)
            for c in range(0, width, span):
                v = x_ref[rows, c : c + span].astype(f32)
                v = v * v
                for k in range(0, span, 128):
                    total = total + v[:, k : k + 128]
            scale = lax.rsqrt(jnp.sum(total, axis=1, keepdims=True) / width + norm_eps)
            for c in range(chunks):
                for e in range(reps):
                    for j in range(groups):
                        at = lax.rem(me_ref[0] + j, groups) * shard + (rep_ref[0] ^ e) * piece + c * chunk
                        v = x_ref[rows, pl.ds(pl.multiple_of(at, chunk), chunk)].astype(f32)
                        out_refs[c * reps + e][rows, j * chunk : (j + 1) * chunk] = (v * scale).astype(bf16)

    outs = pl.pallas_call(
        kernel,
        grid=(tokens // block,),
        out_shape=[jax.ShapeDtypeStruct((tokens, groups * chunk), bf16)] * (chunks * reps),
        in_specs=[SMEM_ARG, SMEM_ARG, pl.BlockSpec((block, width), lambda i: (i, 0))],
        out_specs=[pl.BlockSpec((block, groups * chunk), lambda i: (i, 0))] * (chunks * reps),
        compiler_params=params(8),
        cost_estimate=cost(6 * x.size, 4 * x.size),
        name="scaled_blocks",
    )(me, rep, x)
    return [list(outs[c * reps : (c + 1) * reps]) for c in range(chunks)]


def joined(arrays):
    rows, width = arrays[0].shape
    if rows % 16 or width % 128:
        return jnp.concatenate(arrays, axis=0)

    def kernel(*refs):
        copies = []
        for k in range(len(arrays)):
            target = refs[-2].at[k * rows : (k + 1) * rows, :]
            copies.append(pltpu.make_async_copy(refs[k], target, refs[-1].at[k]))
            copies[-1].start()
        for copy in copies:
            copy.wait()

    return pl.pallas_call(
        kernel,
        out_shape=jax.ShapeDtypeStruct((len(arrays) * rows, width), bf16),
        in_specs=[ANY_ARG] * len(arrays),
        out_specs=ANY_ARG,
        scratch_shapes=[pltpu.SemaphoreType.DMA((len(arrays),))],
        compiler_params=params(4),
        cost_estimate=cost(0, 4 * len(arrays) * rows * width),
        name="joined",
    )(*arrays)


def doubled(value, order):
    for bit in order[:-1]:
        value = joined([value, flipped(value, "rep", 1 << bit)])
    return value, flipped(value, "rep", 1 << order[-1])


def mask_of(pos, order):
    return sum(((pos >> i) & 1) << bit for i, bit in enumerate(order))


def regrouped(blocks, groups):
    tokens, width = blocks[0].shape
    chunk = width // groups
    reps = len(blocks)
    if chunk % 128:
        return [jnp.concatenate([b[:, j * chunk : (j + 1) * chunk] for b in blocks], axis=0) for j in range(groups)]

    def kernel(*refs):
        copies = []
        for e in range(reps):
            for j in range(groups):
                source = refs[e].at[:, j * chunk : (j + 1) * chunk]
                target = refs[reps + j].at[e * tokens : (e + 1) * tokens, :]
                copies.append(pltpu.make_async_copy(source, target, refs[-1].at[e * groups + j]))
                copies[-1].start()
        for copy in copies:
            copy.wait()

    return list(
        pl.pallas_call(
            kernel,
            out_shape=[jax.ShapeDtypeStruct((reps * tokens, chunk), bf16)] * groups,
            in_specs=[ANY_ARG] * reps,
            out_specs=[ANY_ARG] * groups,
            scratch_shapes=[pltpu.SemaphoreType.DMA((reps * groups,))],
            compiler_params=params(8),
            cost_estimate=cost(0, 4 * reps * tokens * width),
            name="regrouped",
        )(*blocks)
    )


def weight_product(columns, values, weight, gain, rep, groups, count, norm_scale):
    rows, width = columns[0].shape
    reps = len(values)
    tokens = rows // reps
    features = values[0].shape[1]
    chunk = width // count
    contract = (((0,), (0,)), ((), ()))

    def thirds(row):
        first = row.astype(bf16)
        rest = row - first.astype(f32)
        second = rest.astype(bf16)
        return first, second, (rest - second.astype(f32)).astype(bf16)

    if chunk % 128:
        order = jnp.stack([v.reshape(groups, tokens, features) for v in values], axis=1)
        raw = lax.dot_general(
            jnp.concatenate(columns, axis=0), order.reshape(-1, features), contract, preferred_element_type=f32
        )
        own = lax.dynamic_slice_in_dim(weight, rep[0] * width, width, 0).astype(f32)
        dots = jnp.sum(raw * own, axis=1) * norm_scale
        factor = lax.dynamic_slice_in_dim(gain[0], rep[0] * width, width, 0).astype(f32) * norm_scale
        raw = (raw * factor[:, None]).astype(bf16)
        outs = []
        for c in range(count):
            at = slice(c * chunk, (c + 1) * chunk)
            under = jnp.stack(thirds(dots[at]) + (jnp.zeros((chunk,), bf16),) * 13)
            outs.append(jnp.concatenate([raw[at], jnp.pad(under, ((0, 0), (0, features - chunk)))], axis=0))
        return outs

    def kernel(rep_ref, *refs):
        column_refs, value_refs = refs[:groups], refs[groups : groups + reps]
        weight_ref, gain_ref = refs[groups + reps], refs[groups + reps + 1]
        out_refs, total = refs[groups + reps + 2 : -1], refs[-1]
        start = pl.multiple_of(rep_ref[0] * width, width)
        for j in range(groups):
            right = jnp.concatenate([v[j * tokens : (j + 1) * tokens, :] for v in value_refs], axis=0)
            for c in range(count):
                block = column_refs[j][:, c * chunk : (c + 1) * chunk]
                product = lax.dot_general(block, right, contract, preferred_element_type=f32)
                if j == 0:
                    total[c] = product
                else:
                    total[c] += product
        for c in range(count):
            at = pl.ds(pl.multiple_of(start + c * chunk, chunk), chunk)
            raw = total[c]
            factor = gain_ref[:, at].astype(f32) * norm_scale
            factor = jnp.transpose(jnp.broadcast_to(factor, (128, chunk)))[:, 0:1]
            out_refs[c][:chunk, :] = (raw * factor).astype(bf16)
            terms = raw * weight_ref[at, :].astype(f32)
            terms = sum(terms[:, k : k + 128] for k in range(0, features, 128))
            dots = lax.dot_general(
                jnp.full((8, 128), norm_scale, f32),
                terms,
                (((1,), (1,)), ((), ())),
                precision=lax.Precision.HIGHEST,
                preferred_element_type=f32,
            )
            under = jnp.concatenate([row[0:1, :].astype(f32) for row in thirds(dots)] + [jnp.zeros((13, chunk), f32)], axis=0)
            out_refs[c][chunk:, :chunk] = under.astype(bf16)
            out_refs[c][chunk:, chunk:] = jnp.zeros((16, features - chunk), bf16)

    vmem = pl.BlockSpec(memory_space=pltpu.VMEM)
    return pl.pallas_call(
        kernel,
        out_shape=[jax.ShapeDtypeStruct((chunk + 16, features), bf16)] * count,
        in_specs=[SMEM_ARG] + [vmem] * (groups + reps + 2),
        out_specs=[vmem] * count,
        scratch_shapes=[pltpu.VMEM((count, chunk, features), f32)],
        compiler_params=params(24),
        cost_estimate=cost(2 * groups * rows * width * features, 2 * groups * rows * (width + features) + 4 * width * features),
        name="weight_product",
    )(rep, *columns, *values, weight, gain)


def returned_blocks(slots, weight, gain, micro, far):
    groups = len(slots)
    tokens, features = slots[0].shape
    counts = [micro if j == far else 1 for j in range(groups)]
    starts = [sum(counts[:j]) for j in range(groups)]
    parts = [tokens // n for n in counts for _ in range(n)]
    shard = weight.shape[0]
    tile = min(shard, 512)

    def kernel(*refs):
        slot_refs, weight_ref, gain_ref = refs[:groups], refs[groups], refs[groups + 1]
        out_refs = refs[groups + 2 :]
        factor = gain_ref[...].astype(f32)
        pair = 2 if groups % 2 == 0 else 1
        out_refs = [out_refs[at : at + n] for at, n in zip(starts, counts)]
        for j in range(0, groups, pair):
            values = jnp.concatenate([slot_refs[j + i][...] for i in range(pair)], axis=0)
            back = lax.dot_general(values, weight_ref[...], (((1,), (1,)), ((), ())), preferred_element_type=f32)
            back = (back * factor).astype(bf16)
            for i in range(pair):
                part = tokens // counts[j + i]
                for m in range(counts[j + i]):
                    at = i * tokens + m * part
                    out_refs[j + i][m][...] = back[at : at + part, :]

    outs = pl.pallas_call(
        kernel,
        grid=(shard // tile,),
        out_shape=[jax.ShapeDtypeStruct((part, shard), bf16) for part in parts],
        in_specs=[pl.BlockSpec((tokens, features), lambda i: (0, 0))] * groups
        + [pl.BlockSpec((tile, features), lambda i: (i, 0)), pl.BlockSpec((1, tile), lambda i: (0, i))],
        out_specs=[pl.BlockSpec((part, tile), lambda i: (0, i)) for part in parts],
        compiler_params=params(8),
        cost_estimate=cost(2 * groups * tokens * shard * features, 2 * groups * tokens * (shard + features) + 2 * shard * features),
        name="returned_blocks",
    )(*slots, weight, gain)
    return [list(outs[at : at + n]) for at, n in zip(starts, counts)]


def row_gradient(x, top, blocks, me, m):
    groups = len(blocks)
    shard = blocks[0].shape[1]
    rows = x.shape[2]
    width = shard * groups
    step = 16

    def block_spec(block):
        base = m * rows // step if block.shape[0] > rows else 0
        return pl.BlockSpec((step, shard), lambda i: (base + i, 0))

    def kernel(me_ref, x_ref, top_ref, *refs):
        block_refs, upper_ref, piece_ref = refs[:groups], refs[groups], refs[groups + 1]
        squares = jnp.zeros((step, 128), f32)
        dots = jnp.zeros((step, 128), f32)
        starts = [pl.multiple_of(lax.rem(me_ref[0] + j, groups) * shard, shard) for j in range(groups)]
        span = min(shard, 512)
        for j in range(groups):
            for c in range(0, shard, span):
                v = x_ref[0, 0, :, pl.ds(pl.multiple_of(starts[j] + c, span), span)].astype(f32)
                d = block_refs[j][:, c : c + span].astype(f32) * v
                v = v * v
                for k in range(0, span, 128):
                    squares = squares + v[:, k : k + 128]
                    dots = dots + d[:, k : k + 128]
        scale = lax.rsqrt(jnp.sum(squares, axis=1, keepdims=True) / width + norm_eps)
        mean = jnp.sum(dots, axis=1, keepdims=True) * scale / width
        slope = scale * mean
        for j in range(groups):
            for c in range(0, shard, span):
                at = pl.ds(pl.multiple_of(starts[j] + c, span), span)
                v = x_ref[0, 0, :, at].astype(f32)
                piece = (scale * (block_refs[j][:, c : c + span].astype(f32) - v * slope)).astype(bf16)
                piece_ref[:, at] = piece
                upper_ref[:, at] = (top_ref[0, :, at].astype(f32) + piece.astype(f32)).astype(bf16)

    return pl.pallas_call(
        kernel,
        grid=(rows // step,),
        out_shape=[jax.ShapeDtypeStruct((rows, width), bf16)] * 2,
        in_specs=[
            SMEM_ARG,
            pl.BlockSpec((1, 1, step, width), lambda i: (0, m, i, 0)),
            pl.BlockSpec((1, step, width), lambda i: (m, i, 0)),
        ]
        + [block_spec(block) for block in blocks],
        out_specs=[pl.BlockSpec((step, width), lambda i: (i, 0))] * 2,
        compiler_params=params(8),
        cost_estimate=cost(12 * rows * width, 10 * rows * width),
        name="row_gradient",
    )(me, x, top, *blocks)


def input_gradient(upper, piece, passed, is_upper, shape, m, earlier):
    rows, width = upper.shape
    step = min(rows, 32)

    def kernel(is_upper_ref, upper_ref, piece_ref, passed_ref, *refs):
        lower = (passed_ref[...].astype(f32) + piece_ref[...].astype(f32)).astype(bf16)
        refs[-1][0, 0] = jnp.where(is_upper_ref[0] == 1, upper_ref[...], lower)

    spec = pl.BlockSpec((step, width), lambda i: (i, 0))
    return pl.pallas_call(
        kernel,
        grid=(rows // step,),
        out_shape=jax.ShapeDtypeStruct(shape, bf16),
        in_specs=[SMEM_ARG, spec, spec, spec] + [ANY_ARG] * len(earlier),
        out_specs=pl.BlockSpec((1, 1, step, width), lambda i: (0, m, i, 0)),
        input_output_aliases={4: 0} if earlier else {},
        compiler_params=params(8),
        cost_estimate=cost(4 * rows * width, 8 * rows * width),
        name="input_gradient",
    )(is_upper, upper, piece, passed, *earlier)


def finished_half(sums, rep, order, half, c, chunks, earlier):
    pieces = (1 << len(order)) // 2
    rows = sums.shape[0] // pieces - 16
    features = sums.shape[1]
    shard = rows * chunks * pieces * 2

    def place(i, rep_ref):
        return (rep_ref[0] ^ mask_of(i + half * pieces, order)) * chunks + c

    def total(under):
        return under[0:1, :rows] + under[1:2, :rows] + under[2:3, :rows]

    if rows % 128:
        earlier = earlier or (jnp.zeros((shard, features), f32), jnp.zeros((1, shard), f32))
        for i in range(pieces):
            piece = sums[i * (rows + 16) : (i + 1) * (rows + 16)].astype(f32)
            at = place(i, rep) * rows
            earlier = (
                lax.dynamic_update_slice(earlier[0], piece[:rows], (at, 0)),
                lax.dynamic_update_slice(earlier[1], total(piece[rows:]), (0, at)),
            )
        return earlier

    def kernel(rep_ref, sum_ref, *refs):
        refs[-2][...] = sum_ref[:rows, :].astype(f32)
        refs[-1][...] = total(sum_ref[rows:, :].astype(f32))

    return pl.pallas_call(
        kernel,
        grid_spec=pltpu.PrefetchScalarGridSpec(
            num_scalar_prefetch=1,
            grid=(pieces,),
            in_specs=[pl.BlockSpec((rows + 16, features), lambda i, rep_ref: (i, 0))] + [ANY_ARG] * len(earlier),
            out_specs=[
                pl.BlockSpec((rows, features), lambda i, rep_ref: (place(i, rep_ref), 0)),
                pl.BlockSpec((1, rows), lambda i, rep_ref: (0, place(i, rep_ref))),
            ],
        ),
        out_shape=[jax.ShapeDtypeStruct((shard, features), f32), jax.ShapeDtypeStruct((1, shard), f32)],
        input_output_aliases={2: 0, 3: 1} if earlier else {},
        compiler_params=params(8),
        cost_estimate=cost(sums.size, 6 * sums.size),
        name="finished_half",
    )(rep, sums, *earlier)


def local(layer_input, value_grad, value_weight, norm_gain, top_grad):
    groups = lax.axis_size("fsdp")
    reps = lax.axis_size("rep")
    bits = reps.bit_length() - 1
    me = lax.axis_index("fsdp").astype(jnp.int32)[None]
    rep = lax.axis_index("rep").astype(jnp.int32)[None]
    _, micro, rows, width = layer_input.shape
    tokens = micro * rows
    norm_scale = float(tokens * reps * groups) ** (-0.5)
    chunks = 2
    orders = [tuple(range(bits)), tuple(reversed(range(bits)))]

    weight = value_weight[0]
    is_upper = lax.axis_index("section").astype(jnp.int32)[None]
    inputs = after(layer_input[0].reshape(tokens, width), me, rep, is_upper)

    hats = scaled_blocks(inputs, me, rep, groups, reps, 1)[0]
    plane = list(hats)
    for e in range(1, reps):
        plane[e] = flipped(hats[e], "rep", e)
    grads = after(value_grad[0].reshape(tokens, -1), hats[0])
    slots = [grads] + [cyclic(after(grads, plane[1]) if j == groups - 1 else grads, "fsdp", j) for j in range(1, groups)]

    plane[0] = after(plane[0], *slots[1:-1])
    sent = regrouped(plane, groups)
    far = groups // 2
    near = [j for j in range(1, groups) if j != far]
    back = returned_blocks(slots, weight, norm_gain, micro, far)
    columns = list(sent)
    columns[far] = cyclic(sent[far], "fsdp", far)
    columns[near[0]] = cyclic(sent[near[0]], "fsdp", near[0])
    for j in near[1:]:
        columns[j] = cyclic(after(sent[j], back[0][0], columns[near[0]]), "fsdp", j)
    held = after(joined(slots), sent[0])
    values = [held if e == 0 else flipped(held, "rep", e) for e in range(reps)]

    lines = [list(arrays) for arrays in back]

    def send_back(j, m, *ties):
        lines[j][m] = cyclic(after(lines[j][m], *ties), "fsdp", -j)

    send_back(far, 0, columns[far])
    send_back(near[-1], 0, columns[far])
    for j in near[:-1]:
        send_back(j, 0, lines[far][0])
    for m in range(1, micro):
        send_back(far, m, lines[far][m - 1])
    sums = weight_product(columns, values, weight, norm_gain, rep, groups, chunks, norm_scale)
    gathered = [doubled(sums[c], orders[c]) for c in range(chunks)]
    finished = ()
    for half in (0, 1):
        for c in range(chunks):
            finished = finished_half(gathered[c][half], rep, orders[c], half, c, chunks, finished)
        if half == 0:
            early = finished
    weight_grad, gain_grad = finished

    uppers = []
    for m in range(micro):
        line = [arrays[m if j == far else 0] for j, arrays in enumerate(lines)]
        line[0] = after(line[0], *([*early] if m else [*early]))
        line[0] = after(line[0], *[u for u, _ in uppers])
        uppers.append(row_gradient(layer_input, top_grad, line, me, m))
    result = ()
    for m, (upper, piece) in enumerate(uppers):
        passed = lax.ppermute(upper, "section", [(1, 0)])
        piece = after(piece, *finished)
        result = (input_gradient(upper, piece, passed, is_upper, layer_input.shape, m, result),)
    return (result[0], weight_grad[None], gain_grad)


def solution(mesh):
    return jax.shard_map(
        local,
        mesh=mesh,
        in_specs=(
            P("section", None, ("rep", "fsdp"), None),
            P("section", None, ("rep", "fsdp"), None),
            P("section", "fsdp", None),
            P("section", "fsdp"),
            P(None, ("rep", "fsdp"), None),
        ),
        out_specs=(
            P("section", None, ("rep", "fsdp"), None),
            P("section", "fsdp", None),
            P("section", "fsdp"),
        ),
        check_vma=False,
    )
```

```python
import jax
import jax.numpy as jnp
from jax import lax
from jax.experimental import pallas as pl
from jax.experimental.pallas import tpu as pltpu
from jax.sharding import PartitionSpec as P

norm_eps = 1e-05
bf16 = jnp.bfloat16
f32 = jnp.float32
MIB = 1 << 20
SMEM_ARG = pl.BlockSpec(memory_space=pltpu.SMEM)
ANY_ARG = pl.BlockSpec(memory_space=pl.ANY)


def cyclic(value, axis, steps):
    count = lax.axis_size(axis)
    return lax.ppermute(value, axis, [(i, (i + steps) % count) for i in range(count)])


def flipped(value, axis, mask):
    count = lax.axis_size(axis)
    return lax.ppermute(value, axis, [(i, i ^ mask) for i in range(count)])


def after(value, *others):
    return lax.optimization_barrier((value, *others))[0]


def params(mib):
    return pltpu.CompilerParams(vmem_limit_bytes=mib * MIB)


def cost(flops, bytes_accessed):
    return pl.CostEstimate(flops=int(flops), bytes_accessed=int(bytes_accessed), transcendentals=0)


def scaled_blocks(x, me, rep, groups, reps, chunks):
    tokens, width = x.shape
    shard = width // groups
    piece = shard // reps
    chunk = piece // chunks
    if chunk % 128:
        x = x.astype(f32)
        hat = (x * lax.rsqrt(jnp.mean(x * x, axis=1, keepdims=True) + norm_eps)).astype(bf16)
        hat = jnp.roll(hat.reshape(tokens, groups, reps, chunks, chunk), -me[0], axis=1)
        take = lambda e, c: lax.dynamic_index_in_dim(hat, rep[0] ^ e, 2, False)[:, :, c].reshape(tokens, groups * chunk)
        return [[take(e, c) for e in range(reps)] for c in range(chunks)]
    step = 16
    block = min(tokens, 32)

    def kernel(me_ref, rep_ref, x_ref, *out_refs):
        span = min(shard, 512)
        for row in range(0, block, step):
            rows = slice(row, row + step)
            total = jnp.zeros((step, 128), f32)
            for c in range(0, width, span):
                v = x_ref[rows, c : c + span].astype(f32)
                v = v * v
                for k in range(0, span, 128):
                    total = total + v[:, k : k + 128]
            scale = lax.rsqrt(jnp.sum(total, axis=1, keepdims=True) / width + norm_eps)
            for c in range(chunks):
                for e in range(reps):
                    for j in range(groups):
                        at = lax.rem(me_ref[0] + j, groups) * shard + (rep_ref[0] ^ e) * piece + c * chunk
                        v = x_ref[rows, pl.ds(pl.multiple_of(at, chunk), chunk)].astype(f32)
                        out_refs[c * reps + e][rows, j * chunk : (j + 1) * chunk] = (v * scale).astype(bf16)

    outs = pl.pallas_call(
        kernel,
        grid=(tokens // block,),
        out_shape=[jax.ShapeDtypeStruct((tokens, groups * chunk), bf16)] * (chunks * reps),
        in_specs=[SMEM_ARG, SMEM_ARG, pl.BlockSpec((block, width), lambda i: (i, 0))],
        out_specs=[pl.BlockSpec((block, groups * chunk), lambda i: (i, 0))] * (chunks * reps),
        compiler_params=params(56),
        cost_estimate=cost(6 * x.size, 4 * x.size),
        name="scaled_blocks",
    )(me, rep, x)
    return [list(outs[c * reps : (c + 1) * reps]) for c in range(chunks)]


def joined(arrays):
    rows, width = arrays[0].shape
    if rows % 16 or width % 128:
        return jnp.concatenate(arrays, axis=0)

    def kernel(*refs):
        copies = []
        for k in range(len(arrays)):
            target = refs[-2].at[k * rows : (k + 1) * rows, :]
            copies.append(pltpu.make_async_copy(refs[k], target, refs[-1].at[k]))
            copies[-1].start()
        for copy in copies:
            copy.wait()

    return pl.pallas_call(
        kernel,
        out_shape=jax.ShapeDtypeStruct((len(arrays) * rows, width), bf16),
        in_specs=[ANY_ARG] * len(arrays),
        out_specs=ANY_ARG,
        scratch_shapes=[pltpu.SemaphoreType.DMA((len(arrays),))],
        compiler_params=params(4),
        cost_estimate=cost(0, 4 * len(arrays) * rows * width),
        name="joined",
    )(*arrays)


def doubled(value, order):
    for bit in order[:-1]:
        value = joined([value, flipped(value, "rep", 1 << bit)])
    return value, flipped(value, "rep", 1 << order[-1])


def mask_of(pos, order):
    return sum(((pos >> i) & 1) << bit for i, bit in enumerate(order))


def regrouped(blocks, groups):
    tokens, width = blocks[0].shape
    chunk = width // groups
    reps = len(blocks)
    if chunk % 128:
        return [jnp.concatenate([b[:, j * chunk : (j + 1) * chunk] for b in blocks], axis=0) for j in range(groups)]

    def kernel(*refs):
        copies = []
        for e in range(reps):
            for j in range(groups):
                source = refs[e].at[:, j * chunk : (j + 1) * chunk]
                target = refs[reps + j].at[e * tokens : (e + 1) * tokens, :]
                copies.append(pltpu.make_async_copy(source, target, refs[-1].at[e * groups + j]))
                copies[-1].start()
        for copy in copies:
            copy.wait()

    return list(
        pl.pallas_call(
            kernel,
            out_shape=[jax.ShapeDtypeStruct((reps * tokens, chunk), bf16)] * groups,
            in_specs=[ANY_ARG] * reps,
            out_specs=[ANY_ARG] * groups,
            scratch_shapes=[pltpu.SemaphoreType.DMA((reps * groups,))],
            compiler_params=params(8),
            cost_estimate=cost(0, 4 * reps * tokens * width),
            name="regrouped",
        )(*blocks)
    )


def weight_product(columns, values, weight, gain, rep, groups, count, norm_scale):
    rows, width = columns[0].shape
    reps = len(values)
    tokens = rows // reps
    features = values[0].shape[1]
    chunk = width // count
    contract = (((0,), (0,)), ((), ()))

    def thirds(row):
        first = row.astype(bf16)
        rest = row - first.astype(f32)
        second = rest.astype(bf16)
        return first, second, (rest - second.astype(f32)).astype(bf16)

    if chunk % 128:
        order = jnp.stack([v.reshape(groups, tokens, features) for v in values], axis=1)
        raw = lax.dot_general(
            jnp.concatenate(columns, axis=0), order.reshape(-1, features), contract, preferred_element_type=f32
        )
        own = lax.dynamic_slice_in_dim(weight, rep[0] * width, width, 0).astype(f32)
        dots = jnp.sum(raw * own, axis=1) * norm_scale
        factor = lax.dynamic_slice_in_dim(gain[0], rep[0] * width, width, 0).astype(f32) * norm_scale
        raw = (raw * factor[:, None]).astype(bf16)
        outs = []
        for c in range(count):
            at = slice(c * chunk, (c + 1) * chunk)
            under = jnp.stack(thirds(dots[at]) + (jnp.zeros((chunk,), bf16),) * 13)
            outs.append(jnp.concatenate([raw[at], jnp.pad(under, ((0, 0), (0, features - chunk)))], axis=0))
        return outs

    def kernel(rep_ref, *refs):
        column_refs, value_refs = refs[:groups], refs[groups : groups + reps]
        weight_ref, gain_ref = refs[groups + reps], refs[groups + reps + 1]
        out_refs, total = refs[groups + reps + 2 : -1], refs[-1]
        start = pl.multiple_of(rep_ref[0] * width, width)
        for j in range(groups):
            right = jnp.concatenate([v[j * tokens : (j + 1) * tokens, :] for v in value_refs], axis=0)
            for c in range(count):
                block = column_refs[j][:, c * chunk : (c + 1) * chunk]
                product = lax.dot_general(block, right, contract, preferred_element_type=f32)
                if j == 0:
                    total[c] = product
                else:
                    total[c] += product
        for c in range(count):
            at = pl.ds(pl.multiple_of(start + c * chunk, chunk), chunk)
            raw = total[c]
            factor = gain_ref[:, at].astype(f32) * norm_scale
            factor = jnp.transpose(jnp.broadcast_to(factor, (128, chunk)))[:, 0:1]
            out_refs[c][:chunk, :] = (raw * factor).astype(bf16)
            terms = raw * weight_ref[at, :].astype(f32)
            terms = sum(terms[:, k : k + 128] for k in range(0, features, 128))
            dots = lax.dot_general(
                jnp.full((8, 128), norm_scale, f32),
                terms,
                (((1,), (1,)), ((), ())),
                precision=lax.Precision.HIGHEST,
                preferred_element_type=f32,
            )
            under = jnp.concatenate([row[0:1, :].astype(f32) for row in thirds(dots)] + [jnp.zeros((13, chunk), f32)], axis=0)
            out_refs[c][chunk:, :chunk] = under.astype(bf16)
            out_refs[c][chunk:, chunk:] = jnp.zeros((16, features - chunk), bf16)

    vmem = pl.BlockSpec(memory_space=pltpu.VMEM)
    return pl.pallas_call(
        kernel,
        out_shape=[jax.ShapeDtypeStruct((chunk + 16, features), bf16)] * count,
        in_specs=[SMEM_ARG] + [vmem] * (groups + reps + 2),
        out_specs=[vmem] * count,
        scratch_shapes=[pltpu.VMEM((count, chunk, features), f32)],
        compiler_params=params(24),
        cost_estimate=cost(2 * groups * rows * width * features, 2 * groups * rows * (width + features) + 4 * width * features),
        name="weight_product",
    )(rep, *columns, *values, weight, gain)


def returned_blocks(slots, weight, gain, micro, far):
    groups = len(slots)
    tokens, features = slots[0].shape
    counts = [micro if j == far else 1 for j in range(groups)]
    starts = [sum(counts[:j]) for j in range(groups)]
    parts = [tokens // n for n in counts for _ in range(n)]
    shard = weight.shape[0]
    tile = min(shard, 512)

    def kernel(*refs):
        slot_refs, weight_ref, gain_ref = refs[:groups], refs[groups], refs[groups + 1]
        out_refs = refs[groups + 2 :]
        factor = gain_ref[...].astype(f32)
        pair = 2 if groups % 2 == 0 else 1
        out_refs = [out_refs[at : at + n] for at, n in zip(starts, counts)]
        for j in range(0, groups, pair):
            values = jnp.concatenate([slot_refs[j + i][...] for i in range(pair)], axis=0)
            back = lax.dot_general(values, weight_ref[...], (((1,), (1,)), ((), ())), preferred_element_type=f32)
            back = (back * factor).astype(bf16)
            for i in range(pair):
                part = tokens // counts[j + i]
                for m in range(counts[j + i]):
                    at = i * tokens + m * part
                    out_refs[j + i][m][...] = back[at : at + part, :]

    outs = pl.pallas_call(
        kernel,
        grid=(shard // tile,),
        out_shape=[jax.ShapeDtypeStruct((part, shard), bf16) for part in parts],
        in_specs=[pl.BlockSpec((tokens, features), lambda i: (0, 0))] * groups
        + [pl.BlockSpec((tile, features), lambda i: (i, 0)), pl.BlockSpec((1, tile), lambda i: (0, i))],
        out_specs=[pl.BlockSpec((part, tile), lambda i: (0, i)) for part in parts],
        compiler_params=params(8),
        cost_estimate=cost(2 * groups * tokens * shard * features, 2 * groups * tokens * (shard + features) + 2 * shard * features),
        name="returned_blocks",
    )(*slots, weight, gain)
    return [list(outs[at : at + n]) for at, n in zip(starts, counts)]


def row_gradient(x, top, blocks, me, m):
    groups = len(blocks)
    shard = blocks[0].shape[1]
    rows = x.shape[2]
    width = shard * groups
    step = 16

    def block_spec(block):
        base = m * rows // step if block.shape[0] > rows else 0
        return pl.BlockSpec((step, shard), lambda i: (base + i, 0))

    def kernel(me_ref, x_ref, top_ref, *refs):
        block_refs, upper_ref, piece_ref = refs[:groups], refs[groups], refs[groups + 1]
        squares = jnp.zeros((step, 128), f32)
        dots = jnp.zeros((step, 128), f32)
        starts = [pl.multiple_of(lax.rem(me_ref[0] + j, groups) * shard, shard) for j in range(groups)]
        span = min(shard, 512)
        for j in range(groups):
            for c in range(0, shard, span):
                v = x_ref[0, 0, :, pl.ds(pl.multiple_of(starts[j] + c, span), span)].astype(f32)
                d = block_refs[j][:, c : c + span].astype(f32) * v
                v = v * v
                for k in range(0, span, 128):
                    squares = squares + v[:, k : k + 128]
                    dots = dots + d[:, k : k + 128]
        scale = lax.rsqrt(jnp.sum(squares, axis=1, keepdims=True) / width + norm_eps)
        mean = jnp.sum(dots, axis=1, keepdims=True) * scale / width
        slope = scale * mean
        for j in range(groups):
            for c in range(0, shard, span):
                at = pl.ds(pl.multiple_of(starts[j] + c, span), span)
                v = x_ref[0, 0, :, at].astype(f32)
                piece = (scale * (block_refs[j][:, c : c + span].astype(f32) - v * slope)).astype(bf16)
                piece_ref[:, at] = piece
                upper_ref[:, at] = (top_ref[0, :, at].astype(f32) + piece.astype(f32)).astype(bf16)

    return pl.pallas_call(
        kernel,
        grid=(rows // step,),
        out_shape=[jax.ShapeDtypeStruct((rows, width), bf16)] * 2,
        in_specs=[
            SMEM_ARG,
            pl.BlockSpec((1, 1, step, width), lambda i: (0, m, i, 0)),
            pl.BlockSpec((1, step, width), lambda i: (m, i, 0)),
        ]
        + [block_spec(block) for block in blocks],
        out_specs=[pl.BlockSpec((step, width), lambda i: (i, 0))] * 2,
        compiler_params=params(8),
        cost_estimate=cost(12 * rows * width, 10 * rows * width),
        name="row_gradient",
    )(me, x, top, *blocks)


def input_gradient(upper, piece, passed, is_upper, shape, m, earlier):
    rows, width = upper.shape
    step = min(rows, 32)

    def kernel(is_upper_ref, upper_ref, piece_ref, passed_ref, *refs):
        lower = (passed_ref[...].astype(f32) + piece_ref[...].astype(f32)).astype(bf16)
        refs[-1][0, 0] = jnp.where(is_upper_ref[0] == 1, upper_ref[...], lower)

    spec = pl.BlockSpec((step, width), lambda i: (i, 0))
    return pl.pallas_call(
        kernel,
        grid=(rows // step,),
        out_shape=jax.ShapeDtypeStruct(shape, bf16),
        in_specs=[SMEM_ARG, spec, spec, spec] + [ANY_ARG] * len(earlier),
        out_specs=pl.BlockSpec((1, 1, step, width), lambda i: (0, m, i, 0)),
        input_output_aliases={4: 0} if earlier else {},
        compiler_params=params(8),
        cost_estimate=cost(4 * rows * width, 8 * rows * width),
        name="input_gradient",
    )(is_upper, upper, piece, passed, *earlier)


def finished_half(sums, rep, order, half, c, chunks, earlier):
    pieces = (1 << len(order)) // 2
    rows = sums.shape[0] // pieces - 16
    features = sums.shape[1]
    shard = rows * chunks * pieces * 2

    def place(i, rep_ref):
        return (rep_ref[0] ^ mask_of(i + half * pieces, order)) * chunks + c

    def total(under):
        return under[0:1, :rows] + under[1:2, :rows] + under[2:3, :rows]

    if rows % 128:
        earlier = earlier or (jnp.zeros((shard, features), f32), jnp.zeros((1, shard), f32))
        for i in range(pieces):
            piece = sums[i * (rows + 16) : (i + 1) * (rows + 16)].astype(f32)
            at = place(i, rep) * rows
            earlier = (
                lax.dynamic_update_slice(earlier[0], piece[:rows], (at, 0)),
                lax.dynamic_update_slice(earlier[1], total(piece[rows:]), (0, at)),
            )
        return earlier

    def kernel(rep_ref, sum_ref, *refs):
        refs[-2][...] = sum_ref[:rows, :].astype(f32)
        refs[-1][...] = total(sum_ref[rows:, :].astype(f32))

    return pl.pallas_call(
        kernel,
        grid_spec=pltpu.PrefetchScalarGridSpec(
            num_scalar_prefetch=1,
            grid=(pieces,),
            in_specs=[pl.BlockSpec((rows + 16, features), lambda i, rep_ref: (i, 0))] + [ANY_ARG] * len(earlier),
            out_specs=[
                pl.BlockSpec((rows, features), lambda i, rep_ref: (place(i, rep_ref), 0)),
                pl.BlockSpec((1, rows), lambda i, rep_ref: (0, place(i, rep_ref))),
            ],
        ),
        out_shape=[jax.ShapeDtypeStruct((shard, features), f32), jax.ShapeDtypeStruct((1, shard), f32)],
        input_output_aliases={2: 0, 3: 1} if earlier else {},
        compiler_params=params(8),
        cost_estimate=cost(sums.size, 6 * sums.size),
        name="finished_half",
    )(rep, sums, *earlier)


def local(layer_input, value_grad, value_weight, norm_gain, top_grad):
    groups = lax.axis_size("fsdp")
    reps = lax.axis_size("rep")
    bits = reps.bit_length() - 1
    me = lax.axis_index("fsdp").astype(jnp.int32)[None]
    rep = lax.axis_index("rep").astype(jnp.int32)[None]
    _, micro, rows, width = layer_input.shape
    tokens = micro * rows
    norm_scale = float(tokens * reps * groups) ** (-0.5)
    chunks = 2
    orders = [tuple(range(bits)), tuple(reversed(range(bits)))]

    weight = value_weight[0]
    is_upper = lax.axis_index("section").astype(jnp.int32)[None]
    inputs = after(layer_input[0].reshape(tokens, width), me, rep, is_upper)

    hats = scaled_blocks(inputs, me, rep, groups, reps, 1)[0]
    plane = list(hats)
    for e in range(1, reps):
        plane[e] = flipped(hats[e], "rep", e)
    grads = after(value_grad[0].reshape(tokens, -1), hats[0])
    slots = [grads] + [cyclic(after(grads, plane[1]) if j == groups - 1 else grads, "fsdp", j) for j in range(1, groups)]

    plane[0] = after(plane[0], *slots[1:-1])
    sent = regrouped(plane, groups)
    far = groups // 2
    near = [j for j in range(1, groups) if j != far]
    back = returned_blocks(slots, weight, norm_gain, micro, far)
    columns = list(sent)
    columns[far] = cyclic(sent[far], "fsdp", far)
    columns[near[0]] = cyclic(sent[near[0]], "fsdp", near[0])
    for j in near[1:]:
        columns[j] = cyclic(after(sent[j], back[0][0], columns[near[0]]), "fsdp", j)
    held = after(joined(slots), sent[0])
    values = [held if e == 0 else flipped(held, "rep", e) for e in range(reps)]

    lines = [list(arrays) for arrays in back]

    def send_back(j, m, *ties):
        lines[j][m] = cyclic(after(lines[j][m], *ties), "fsdp", -j)

    send_back(far, 0, columns[far])
    send_back(near[-1], 0, columns[far])
    for j in near[:-1]:
        send_back(j, 0, lines[far][0])
    for m in range(1, micro):
        send_back(far, m, lines[far][m - 1])
    sums = weight_product(columns, values, weight, norm_gain, rep, groups, chunks, norm_scale)
    gathered = [doubled(sums[c], orders[c]) for c in range(chunks)]
    finished = ()
    for half in (0, 1):
        for c in range(chunks):
            finished = finished_half(gathered[c][half], rep, orders[c], half, c, chunks, finished)
        if half == 0:
            early = finished
    weight_grad, gain_grad = finished

    uppers = []
    for m in range(micro):
        line = [arrays[m if j == far else 0] for j, arrays in enumerate(lines)]
        line[0] = after(line[0], *([*early] if m else [*early]))
        line[0] = after(line[0], *[u for u, _ in uppers])
        uppers.append(row_gradient(layer_input, top_grad, line, me, m))
    result = ()
    for m, (upper, piece) in enumerate(uppers):
        passed = lax.ppermute(upper, "section", [(1, 0)])
        piece = after(piece, *finished)
        result = (input_gradient(upper, piece, passed, is_upper, layer_input.shape, m, result),)
    return (result[0], weight_grad[None], gain_grad)


def solution(mesh):
    return jax.shard_map(
        local,
        mesh=mesh,
        in_specs=(
            P("section", None, ("rep", "fsdp"), None),
            P("section", None, ("rep", "fsdp"), None),
            P("section", "fsdp", None),
            P("section", "fsdp"),
            P(None, ("rep", "fsdp"), None),
        ),
        out_specs=(
            P("section", None, ("rep", "fsdp"), None),
            P("section", "fsdp", None),
            P("section", "fsdp"),
        ),
        check_vma=False,
    )
```

```python
import jax
import jax.numpy as jnp
from jax import lax
from jax.experimental import pallas as pl
from jax.experimental.pallas import tpu as pltpu
from jax.sharding import PartitionSpec as P

norm_eps = 1e-05
bf16 = jnp.bfloat16
f32 = jnp.float32
MIB = 1 << 20
SMEM_ARG = pl.BlockSpec(memory_space=pltpu.SMEM)
ANY_ARG = pl.BlockSpec(memory_space=pl.ANY)


def cyclic(value, axis, steps):
    count = lax.axis_size(axis)
    return lax.ppermute(value, axis, [(i, (i + steps) % count) for i in range(count)])


def flipped(value, axis, mask):
    count = lax.axis_size(axis)
    return lax.ppermute(value, axis, [(i, i ^ mask) for i in range(count)])


def after(value, *others):
    return lax.optimization_barrier((value, *others))[0]


def params(mib):
    return pltpu.CompilerParams(vmem_limit_bytes=mib * MIB)


def cost(flops, bytes_accessed):
    return pl.CostEstimate(flops=int(flops), bytes_accessed=int(bytes_accessed), transcendentals=0)


def scaled_blocks(x, me, rep, groups, reps, chunks):
    tokens, width = x.shape
    shard = width // groups
    piece = shard // reps
    chunk = piece // chunks
    if chunk % 128:
        x = x.astype(f32)
        hat = (x * lax.rsqrt(jnp.mean(x * x, axis=1, keepdims=True) + norm_eps)).astype(bf16)
        hat = jnp.roll(hat.reshape(tokens, groups, reps, chunks, chunk), -me[0], axis=1)
        take = lambda e, c: lax.dynamic_index_in_dim(hat, rep[0] ^ e, 2, False)[:, :, c].reshape(tokens, groups * chunk)
        return [[take(e, c) for e in range(reps)] for c in range(chunks)]
    step = 16
    block = min(tokens, 32)

    def kernel(me_ref, rep_ref, x_ref, *out_refs):
        span = min(shard, 512)
        for row in range(0, block, step):
            rows = slice(row, row + step)
            total = jnp.zeros((step, 128), f32)
            for c in range(0, width, span):
                v = x_ref[rows, c : c + span].astype(f32)
                v = v * v
                for k in range(0, span, 128):
                    total = total + v[:, k : k + 128]
            scale = lax.rsqrt(jnp.sum(total, axis=1, keepdims=True) / width + norm_eps)
            for c in range(chunks):
                for e in range(reps):
                    for j in range(groups):
                        at = lax.rem(me_ref[0] + j, groups) * shard + (rep_ref[0] ^ e) * piece + c * chunk
                        v = x_ref[rows, pl.ds(pl.multiple_of(at, chunk), chunk)].astype(f32)
                        out_refs[c * reps + e][rows, j * chunk : (j + 1) * chunk] = (v * scale).astype(bf16)

    outs = pl.pallas_call(
        kernel,
        grid=(tokens // block,),
        out_shape=[jax.ShapeDtypeStruct((tokens, groups * chunk), bf16)] * (chunks * reps),
        in_specs=[SMEM_ARG, SMEM_ARG, pl.BlockSpec((block, width), lambda i: (i, 0))],
        out_specs=[pl.BlockSpec((block, groups * chunk), lambda i: (i, 0))] * (chunks * reps),
        compiler_params=params(8),
        cost_estimate=cost(6 * x.size, 4 * x.size),
        name="scaled_blocks",
    )(me, rep, x)
    return [list(outs[c * reps : (c + 1) * reps]) for c in range(chunks)]


def joined(arrays):
    rows, width = arrays[0].shape
    if rows % 16 or width % 128:
        return jnp.concatenate(arrays, axis=0)

    def kernel(*refs):
        copies = []
        for k in range(len(arrays)):
            target = refs[-2].at[k * rows : (k + 1) * rows, :]
            copies.append(pltpu.make_async_copy(refs[k], target, refs[-1].at[k]))
            copies[-1].start()
        for copy in copies:
            copy.wait()

    return pl.pallas_call(
        kernel,
        out_shape=jax.ShapeDtypeStruct((len(arrays) * rows, width), bf16),
        in_specs=[ANY_ARG] * len(arrays),
        out_specs=ANY_ARG,
        scratch_shapes=[pltpu.SemaphoreType.DMA((len(arrays),))],
        compiler_params=params(4),
        cost_estimate=cost(0, 4 * len(arrays) * rows * width),
        name="joined",
    )(*arrays)


def doubled(value, order):
    for bit in order[:-1]:
        value = joined([value, flipped(value, "rep", 1 << bit)])
    return value, flipped(value, "rep", 1 << order[-1])


def mask_of(pos, order):
    return sum(((pos >> i) & 1) << bit for i, bit in enumerate(order))


def regrouped(blocks, groups):
    tokens, width = blocks[0].shape
    chunk = width // groups
    reps = len(blocks)
    if chunk % 128:
        return [jnp.concatenate([b[:, j * chunk : (j + 1) * chunk] for b in blocks], axis=0) for j in range(groups)]

    def kernel(*refs):
        copies = []
        for e in range(reps):
            for j in range(groups):
                source = refs[e].at[:, j * chunk : (j + 1) * chunk]
                target = refs[reps + j].at[e * tokens : (e + 1) * tokens, :]
                copies.append(pltpu.make_async_copy(source, target, refs[-1].at[e * groups + j]))
                copies[-1].start()
        for copy in copies:
            copy.wait()

    return list(
        pl.pallas_call(
            kernel,
            out_shape=[jax.ShapeDtypeStruct((reps * tokens, chunk), bf16)] * groups,
            in_specs=[ANY_ARG] * reps,
            out_specs=[ANY_ARG] * groups,
            scratch_shapes=[pltpu.SemaphoreType.DMA((reps * groups,))],
            compiler_params=params(8),
            cost_estimate=cost(0, 4 * reps * tokens * width),
            name="regrouped",
        )(*blocks)
    )


def weight_product(columns, values, weight, gain, rep, groups, count, norm_scale):
    rows, width = columns[0].shape
    reps = len(values)
    tokens = rows // reps
    features = values[0].shape[1]
    chunk = width // count
    contract = (((0,), (0,)), ((), ()))

    def thirds(row):
        first = row.astype(bf16)
        rest = row - first.astype(f32)
        second = rest.astype(bf16)
        return first, second, (rest - second.astype(f32)).astype(bf16)

    if chunk % 128:
        order = jnp.stack([v.reshape(groups, tokens, features) for v in values], axis=1)
        raw = lax.dot_general(
            jnp.concatenate(columns, axis=0), order.reshape(-1, features), contract, preferred_element_type=f32
        )
        own = lax.dynamic_slice_in_dim(weight, rep[0] * width, width, 0).astype(f32)
        dots = jnp.sum(raw * own, axis=1) * norm_scale
        factor = lax.dynamic_slice_in_dim(gain[0], rep[0] * width, width, 0).astype(f32) * norm_scale
        raw = (raw * factor[:, None]).astype(bf16)
        outs = []
        for c in range(count):
            at = slice(c * chunk, (c + 1) * chunk)
            under = jnp.stack(thirds(dots[at]) + (jnp.zeros((chunk,), bf16),) * 13)
            outs.append(jnp.concatenate([raw[at], jnp.pad(under, ((0, 0), (0, features - chunk)))], axis=0))
        return outs

    def kernel(rep_ref, *refs):
        column_refs, value_refs = refs[:groups], refs[groups : groups + reps]
        weight_ref, gain_ref = refs[groups + reps], refs[groups + reps + 1]
        out_refs, total = refs[groups + reps + 2 : -1], refs[-1]
        start = pl.multiple_of(rep_ref[0] * width, width)
        for j in range(groups):
            right = jnp.concatenate([v[j * tokens : (j + 1) * tokens, :] for v in value_refs], axis=0)
            for c in range(count):
                block = column_refs[j][:, c * chunk : (c + 1) * chunk]
                product = lax.dot_general(block, right, contract, preferred_element_type=f32)
                if j == 0:
                    total[c] = product
                else:
                    total[c] += product
        for c in range(count):
            at = pl.ds(pl.multiple_of(start + c * chunk, chunk), chunk)
            raw = total[c]
            factor = gain_ref[:, at].astype(f32) * norm_scale
            factor = jnp.transpose(jnp.broadcast_to(factor, (128, chunk)))[:, 0:1]
            out_refs[c][:chunk, :] = (raw * factor).astype(bf16)
            terms = raw * weight_ref[at, :].astype(f32)
            terms = sum(terms[:, k : k + 128] for k in range(0, features, 128))
            dots = lax.dot_general(
                jnp.full((8, 128), norm_scale, f32),
                terms,
                (((1,), (1,)), ((), ())),
                precision=lax.Precision.HIGHEST,
                preferred_element_type=f32,
            )
            under = jnp.concatenate([row[0:1, :].astype(f32) for row in thirds(dots)] + [jnp.zeros((13, chunk), f32)], axis=0)
            out_refs[c][chunk:, :chunk] = under.astype(bf16)
            out_refs[c][chunk:, chunk:] = jnp.zeros((16, features - chunk), bf16)

    vmem = pl.BlockSpec(memory_space=pltpu.VMEM)
    return pl.pallas_call(
        kernel,
        out_shape=[jax.ShapeDtypeStruct((chunk + 16, features), bf16)] * count,
        in_specs=[SMEM_ARG] + [vmem] * (groups + reps + 2),
        out_specs=[vmem] * count,
        scratch_shapes=[pltpu.VMEM((count, chunk, features), f32)],
        compiler_params=params(24),
        cost_estimate=cost(2 * groups * rows * width * features, 2 * groups * rows * (width + features) + 4 * width * features),
        name="weight_product",
    )(rep, *columns, *values, weight, gain)


def returned_blocks(slots, weight, gain, micro, far):
    groups = len(slots)
    tokens, features = slots[0].shape
    counts = [micro if j == far else 1 for j in range(groups)]
    starts = [sum(counts[:j]) for j in range(groups)]
    parts = [tokens // n for n in counts for _ in range(n)]
    shard = weight.shape[0]
    tile = min(shard, 512)

    def kernel(*refs):
        slot_refs, weight_ref, gain_ref = refs[:groups], refs[groups], refs[groups + 1]
        out_refs = refs[groups + 2 :]
        factor = gain_ref[...].astype(f32)
        pair = 2 if groups % 2 == 0 else 1
        out_refs = [out_refs[at : at + n] for at, n in zip(starts, counts)]
        for j in range(0, groups, pair):
            values = jnp.concatenate([slot_refs[j + i][...] for i in range(pair)], axis=0)
            back = lax.dot_general(values, weight_ref[...], (((1,), (1,)), ((), ())), preferred_element_type=f32)
            back = (back * factor).astype(bf16)
            for i in range(pair):
                part = tokens // counts[j + i]
                for m in range(counts[j + i]):
                    at = i * tokens + m * part
                    out_refs[j + i][m][...] = back[at : at + part, :]

    outs = pl.pallas_call(
        kernel,
        grid=(shard // tile,),
        out_shape=[jax.ShapeDtypeStruct((part, shard), bf16) for part in parts],
        in_specs=[pl.BlockSpec((tokens, features), lambda i: (0, 0))] * groups
        + [pl.BlockSpec((tile, features), lambda i: (i, 0)), pl.BlockSpec((1, tile), lambda i: (0, i))],
        out_specs=[pl.BlockSpec((part, tile), lambda i: (0, i)) for part in parts],
        compiler_params=params(8),
        cost_estimate=cost(2 * groups * tokens * shard * features, 2 * groups * tokens * (shard + features) + 2 * shard * features),
        name="returned_blocks",
    )(*slots, weight, gain)
    return [list(outs[at : at + n]) for at, n in zip(starts, counts)]


def row_gradient(x, top, blocks, me, m):
    groups = len(blocks)
    shard = blocks[0].shape[1]
    rows = x.shape[2]
    width = shard * groups
    step = min(rows, 32)

    def block_spec(block):
        base = m * rows // step if block.shape[0] > rows else 0
        return pl.BlockSpec((step, shard), lambda i: (base + i, 0))

    def kernel(me_ref, x_ref, top_ref, *refs):
        block_refs, upper_ref, piece_ref = refs[:groups], refs[groups], refs[groups + 1]
        squares = jnp.zeros((step, 128), f32)
        dots = jnp.zeros((step, 128), f32)
        starts = [pl.multiple_of(lax.rem(me_ref[0] + j, groups) * shard, shard) for j in range(groups)]
        span = min(shard, 512)
        for j in range(groups):
            for c in range(0, shard, span):
                v = x_ref[0, 0, :, pl.ds(pl.multiple_of(starts[j] + c, span), span)].astype(f32)
                d = block_refs[j][:, c : c + span].astype(f32) * v
                v = v * v
                for k in range(0, span, 128):
                    squares = squares + v[:, k : k + 128]
                    dots = dots + d[:, k : k + 128]
        scale = lax.rsqrt(jnp.sum(squares, axis=1, keepdims=True) / width + norm_eps)
        mean = jnp.sum(dots, axis=1, keepdims=True) * scale / width
        slope = scale * mean
        for j in range(groups):
            for c in range(0, shard, span):
                at = pl.ds(pl.multiple_of(starts[j] + c, span), span)
                v = x_ref[0, 0, :, at].astype(f32)
                piece = (scale * (block_refs[j][:, c : c + span].astype(f32) - v * slope)).astype(bf16)
                piece_ref[:, at] = piece
                upper_ref[:, at] = (top_ref[0, :, at].astype(f32) + piece.astype(f32)).astype(bf16)

    return pl.pallas_call(
        kernel,
        grid=(rows // step,),
        out_shape=[jax.ShapeDtypeStruct((rows, width), bf16)] * 2,
        in_specs=[
            SMEM_ARG,
            pl.BlockSpec((1, 1, step, width), lambda i: (0, m, i, 0)),
            pl.BlockSpec((1, step, width), lambda i: (m, i, 0)),
        ]
        + [block_spec(block) for block in blocks],
        out_specs=[pl.BlockSpec((step, width), lambda i: (i, 0))] * 2,
        compiler_params=params(8),
        cost_estimate=cost(12 * rows * width, 10 * rows * width),
        name="row_gradient",
    )(me, x, top, *blocks)


def input_gradient(upper, piece, passed, is_upper, shape, m, earlier):
    rows, width = upper.shape
    step = min(rows, 32)

    def kernel(is_upper_ref, upper_ref, piece_ref, passed_ref, *refs):
        lower = (passed_ref[...].astype(f32) + piece_ref[...].astype(f32)).astype(bf16)
        refs[-1][0, 0] = jnp.where(is_upper_ref[0] == 1, upper_ref[...], lower)

    spec = pl.BlockSpec((step, width), lambda i: (i, 0))
    return pl.pallas_call(
        kernel,
        grid=(rows // step,),
        out_shape=jax.ShapeDtypeStruct(shape, bf16),
        in_specs=[SMEM_ARG, spec, spec, spec] + [ANY_ARG] * len(earlier),
        out_specs=pl.BlockSpec((1, 1, step, width), lambda i: (0, m, i, 0)),
        input_output_aliases={4: 0} if earlier else {},
        compiler_params=params(8),
        cost_estimate=cost(4 * rows * width, 8 * rows * width),
        name="input_gradient",
    )(is_upper, upper, piece, passed, *earlier)


def finished_half(sums, rep, order, half, c, chunks, earlier):
    pieces = (1 << len(order)) // 2
    rows = sums.shape[0] // pieces - 16
    features = sums.shape[1]
    shard = rows * chunks * pieces * 2

    def place(i, rep_ref):
        return (rep_ref[0] ^ mask_of(i + half * pieces, order)) * chunks + c

    def total(under):
        return under[0:1, :rows] + under[1:2, :rows] + under[2:3, :rows]

    if rows % 128:
        earlier = earlier or (jnp.zeros((shard, features), f32), jnp.zeros((1, shard), f32))
        for i in range(pieces):
            piece = sums[i * (rows + 16) : (i + 1) * (rows + 16)].astype(f32)
            at = place(i, rep) * rows
            earlier = (
                lax.dynamic_update_slice(earlier[0], piece[:rows], (at, 0)),
                lax.dynamic_update_slice(earlier[1], total(piece[rows:]), (0, at)),
            )
        return earlier

    def kernel(rep_ref, sum_ref, *refs):
        refs[-2][...] = sum_ref[:rows, :].astype(f32)
        refs[-1][...] = total(sum_ref[rows:, :].astype(f32))

    return pl.pallas_call(
        kernel,
        grid_spec=pltpu.PrefetchScalarGridSpec(
            num_scalar_prefetch=1,
            grid=(pieces,),
            in_specs=[pl.BlockSpec((rows + 16, features), lambda i, rep_ref: (i, 0))] + [ANY_ARG] * len(earlier),
            out_specs=[
                pl.BlockSpec((rows, features), lambda i, rep_ref: (place(i, rep_ref), 0)),
                pl.BlockSpec((1, rows), lambda i, rep_ref: (0, place(i, rep_ref))),
            ],
        ),
        out_shape=[jax.ShapeDtypeStruct((shard, features), f32), jax.ShapeDtypeStruct((1, shard), f32)],
        input_output_aliases={2: 0, 3: 1} if earlier else {},
        compiler_params=params(8),
        cost_estimate=cost(sums.size, 6 * sums.size),
        name="finished_half",
    )(rep, sums, *earlier)


def local(layer_input, value_grad, value_weight, norm_gain, top_grad):
    groups = lax.axis_size("fsdp")
    reps = lax.axis_size("rep")
    bits = reps.bit_length() - 1
    me = lax.axis_index("fsdp").astype(jnp.int32)[None]
    rep = lax.axis_index("rep").astype(jnp.int32)[None]
    _, micro, rows, width = layer_input.shape
    tokens = micro * rows
    norm_scale = float(tokens * reps * groups) ** (-0.5)
    chunks = 2
    orders = [tuple(range(bits)), tuple(reversed(range(bits)))]

    weight = value_weight[0]
    is_upper = lax.axis_index("section").astype(jnp.int32)[None]
    inputs = after(layer_input[0].reshape(tokens, width), me, rep, is_upper)

    hats = scaled_blocks(inputs, me, rep, groups, reps, 1)[0]
    plane = list(hats)
    for e in range(1, reps):
        plane[e] = flipped(hats[e], "rep", e)
    grads = after(value_grad[0].reshape(tokens, -1), hats[0])
    slots = [grads] + [cyclic(after(grads, plane[1]) if j == groups - 1 else grads, "fsdp", j) for j in range(1, groups)]

    plane[0] = after(plane[0], *slots[1:-1])
    sent = regrouped(plane, groups)
    far = groups // 2
    near = [j for j in range(1, groups) if j != far]
    back = returned_blocks(slots, weight, norm_gain, micro, far)
    columns = list(sent)
    columns[far] = cyclic(sent[far], "fsdp", far)
    columns[near[0]] = cyclic(sent[near[0]], "fsdp", near[0])
    for j in near[1:]:
        columns[j] = cyclic(after(sent[j], back[0][0], columns[near[0]]), "fsdp", j)
    held = after(joined(slots), sent[0])
    values = [held if e == 0 else flipped(held, "rep", e) for e in range(reps)]

    lines = [list(arrays) for arrays in back]

    def send_back(j, m, *ties):
        lines[j][m] = cyclic(after(lines[j][m], *ties), "fsdp", -j)

    send_back(far, 0, columns[far])
    send_back(near[-1], 0, columns[far])
    for j in near[:-1]:
        send_back(j, 0, lines[far][0])
    for m in range(1, micro):
        send_back(far, m, lines[far][m - 1])
    sums = weight_product(columns, values, weight, norm_gain, rep, groups, chunks, norm_scale)
    gathered = [doubled(sums[c], orders[c]) for c in range(chunks)]
    finished = ()
    for half in (0, 1):
        for c in range(chunks):
            finished = finished_half(gathered[c][half], rep, orders[c], half, c, chunks, finished)
        if half == 0:
            early = finished
    weight_grad, gain_grad = finished

    uppers = []
    for m in range(micro):
        line = [arrays[m if j == far else 0] for j, arrays in enumerate(lines)]
        line[0] = after(line[0], *([*early] if m else [*early]))
        line[0] = after(line[0], *[u for u, _ in uppers])
        uppers.append(row_gradient(layer_input, top_grad, line, me, m))
    result = ()
    for m, (upper, piece) in enumerate(uppers):
        passed = lax.ppermute(upper, "section", [(1, 0)])
        piece = after(piece, *finished)
        result = (input_gradient(upper, piece, passed, is_upper, layer_input.shape, m, result),)
    return (result[0], weight_grad[None], gain_grad)


def solution(mesh):
    return jax.shard_map(
        local,
        mesh=mesh,
        in_specs=(
            P("section", None, ("rep", "fsdp"), None),
            P("section", None, ("rep", "fsdp"), None),
            P("section", "fsdp", None),
            P("section", "fsdp"),
            P(None, ("rep", "fsdp"), None),
        ),
        out_specs=(
            P("section", None, ("rep", "fsdp"), None),
            P("section", "fsdp", None),
            P("section", "fsdp"),
        ),
        check_vma=False,
    )
```

```python
import jax
import jax.numpy as jnp
from jax import lax
from jax.experimental import pallas as pl
from jax.experimental.pallas import tpu as pltpu
from jax.sharding import PartitionSpec as P

norm_eps = 1e-05
bf16 = jnp.bfloat16
f32 = jnp.float32
MIB = 1 << 20
SMEM_ARG = pl.BlockSpec(memory_space=pltpu.SMEM)
ANY_ARG = pl.BlockSpec(memory_space=pl.ANY)


def cyclic(value, axis, steps):
    count = lax.axis_size(axis)
    return lax.ppermute(value, axis, [(i, (i + steps) % count) for i in range(count)])


def flipped(value, axis, mask):
    count = lax.axis_size(axis)
    return lax.ppermute(value, axis, [(i, i ^ mask) for i in range(count)])


def after(value, *others):
    return lax.optimization_barrier((value, *others))[0]


def params(mib):
    return pltpu.CompilerParams(vmem_limit_bytes=mib * MIB)


def cost(flops, bytes_accessed):
    return pl.CostEstimate(flops=int(flops), bytes_accessed=int(bytes_accessed), transcendentals=0)


def scaled_blocks(x, me, rep, groups, reps, chunks):
    tokens, width = x.shape
    shard = width // groups
    piece = shard // reps
    chunk = piece // chunks
    if chunk % 128:
        x = x.astype(f32)
        hat = (x * lax.rsqrt(jnp.mean(x * x, axis=1, keepdims=True) + norm_eps)).astype(bf16)
        hat = jnp.roll(hat.reshape(tokens, groups, reps, chunks, chunk), -me[0], axis=1)
        take = lambda e, c: lax.dynamic_index_in_dim(hat, rep[0] ^ e, 2, False)[:, :, c].reshape(tokens, groups * chunk)
        return [[take(e, c) for e in range(reps)] for c in range(chunks)]
    step = 16
    block = min(tokens, 32)

    def kernel(me_ref, rep_ref, x_ref, *out_refs):
        span = min(shard, 512)
        for row in range(0, block, step):
            rows = slice(row, row + step)
            total = jnp.zeros((step, 128), f32)
            for c in range(0, width, span):
                v = x_ref[rows, c : c + span].astype(f32)
                v = v * v
                for k in range(0, span, 128):
                    total = total + v[:, k : k + 128]
            scale = lax.rsqrt(jnp.sum(total, axis=1, keepdims=True) / width + norm_eps)
            for c in range(chunks):
                for e in range(reps):
                    for j in range(groups):
                        at = lax.rem(me_ref[0] + j, groups) * shard + (rep_ref[0] ^ e) * piece + c * chunk
                        v = x_ref[rows, pl.ds(pl.multiple_of(at, chunk), chunk)].astype(f32)
                        out_refs[c * reps + e][rows, j * chunk : (j + 1) * chunk] = (v * scale).astype(bf16)

    outs = pl.pallas_call(
        kernel,
        grid=(tokens // block,),
        out_shape=[jax.ShapeDtypeStruct((tokens, groups * chunk), bf16)] * (chunks * reps),
        in_specs=[SMEM_ARG, SMEM_ARG, pl.BlockSpec((block, width), lambda i: (i, 0))],
        out_specs=[pl.BlockSpec((block, groups * chunk), lambda i: (i, 0))] * (chunks * reps),
        compiler_params=params(8),
        cost_estimate=cost(6 * x.size, 4 * x.size),
        name="scaled_blocks",
    )(me, rep, x)
    return [list(outs[c * reps : (c + 1) * reps]) for c in range(chunks)]


def joined(arrays):
    rows, width = arrays[0].shape
    if rows % 16 or width % 128:
        return jnp.concatenate(arrays, axis=0)

    def kernel(*refs):
        copies = []
        for k in range(len(arrays)):
            target = refs[-2].at[k * rows : (k + 1) * rows, :]
            copies.append(pltpu.make_async_copy(refs[k], target, refs[-1].at[k]))
            copies[-1].start()
        for copy in copies:
            copy.wait()

    return pl.pallas_call(
        kernel,
        out_shape=jax.ShapeDtypeStruct((len(arrays) * rows, width), bf16),
        in_specs=[ANY_ARG] * len(arrays),
        out_specs=ANY_ARG,
        scratch_shapes=[pltpu.SemaphoreType.DMA((len(arrays),))],
        compiler_params=params(4),
        cost_estimate=cost(0, 4 * len(arrays) * rows * width),
        name="joined",
    )(*arrays)


def doubled(value, order):
    for bit in order[:-1]:
        value = joined([value, flipped(value, "rep", 1 << bit)])
    return value, flipped(value, "rep", 1 << order[-1])


def mask_of(pos, order):
    return sum(((pos >> i) & 1) << bit for i, bit in enumerate(order))


def regrouped(blocks, groups):
    tokens, width = blocks[0].shape
    chunk = width // groups
    reps = len(blocks)
    if chunk % 128:
        return [jnp.concatenate([b[:, j * chunk : (j + 1) * chunk] for b in blocks], axis=0) for j in range(groups)]

    def kernel(*refs):
        copies = []
        for e in range(reps):
            for j in range(groups):
                source = refs[e].at[:, j * chunk : (j + 1) * chunk]
                target = refs[reps + j].at[e * tokens : (e + 1) * tokens, :]
                copies.append(pltpu.make_async_copy(source, target, refs[-1].at[e * groups + j]))
                copies[-1].start()
        for copy in copies:
            copy.wait()

    return list(
        pl.pallas_call(
            kernel,
            out_shape=[jax.ShapeDtypeStruct((reps * tokens, chunk), bf16)] * groups,
            in_specs=[ANY_ARG] * reps,
            out_specs=[ANY_ARG] * groups,
            scratch_shapes=[pltpu.SemaphoreType.DMA((reps * groups,))],
            compiler_params=params(8),
            cost_estimate=cost(0, 4 * reps * tokens * width),
            name="regrouped",
        )(*blocks)
    )


def weight_product(columns, values, weight, gain, rep, groups, count, norm_scale):
    rows, width = columns[0].shape
    reps = len(values)
    tokens = rows // reps
    features = values[0].shape[1]
    chunk = width // count
    contract = (((0,), (0,)), ((), ()))

    def thirds(row):
        first = row.astype(bf16)
        rest = row - first.astype(f32)
        second = rest.astype(bf16)
        return first, second, (rest - second.astype(f32)).astype(bf16)

    if chunk % 128:
        order = jnp.stack([v.reshape(groups, tokens, features) for v in values], axis=1)
        raw = lax.dot_general(
            jnp.concatenate(columns, axis=0), order.reshape(-1, features), contract, preferred_element_type=f32
        )
        own = lax.dynamic_slice_in_dim(weight, rep[0] * width, width, 0).astype(f32)
        dots = jnp.sum(raw * own, axis=1) * norm_scale
        factor = lax.dynamic_slice_in_dim(gain[0], rep[0] * width, width, 0).astype(f32) * norm_scale
        raw = (raw * factor[:, None]).astype(bf16)
        outs = []
        for c in range(count):
            at = slice(c * chunk, (c + 1) * chunk)
            under = jnp.stack(thirds(dots[at]) + (jnp.zeros((chunk,), bf16),) * 13)
            outs.append(jnp.concatenate([raw[at], jnp.pad(under, ((0, 0), (0, features - chunk)))], axis=0))
        return outs

    def kernel(rep_ref, *refs):
        column_refs, value_refs = refs[:groups], refs[groups : groups + reps]
        weight_ref, gain_ref = refs[groups + reps], refs[groups + reps + 1]
        out_refs, total = refs[groups + reps + 2 : -1], refs[-1]
        start = pl.multiple_of(rep_ref[0] * width, width)
        for j in range(groups):
            right = jnp.concatenate([v[j * tokens : (j + 1) * tokens, :] for v in value_refs], axis=0)
            for c in range(count):
                block = column_refs[j][:, c * chunk : (c + 1) * chunk]
                product = lax.dot_general(block, right, contract, preferred_element_type=f32)
                if j == 0:
                    total[c] = product
                else:
                    total[c] += product
        for c in range(count):
            at = pl.ds(pl.multiple_of(start + c * chunk, chunk), chunk)
            raw = total[c]
            factor = gain_ref[:, at].astype(f32) * norm_scale
            factor = jnp.transpose(jnp.broadcast_to(factor, (128, chunk)))[:, 0:1]
            out_refs[c][:chunk, :] = (raw * factor).astype(bf16)
            terms = raw * weight_ref[at, :].astype(f32)
            terms = sum(terms[:, k : k + 128] for k in range(0, features, 128))
            dots = lax.dot_general(
                jnp.full((8, 128), norm_scale, f32),
                terms,
                (((1,), (1,)), ((), ())),
                precision=lax.Precision.HIGHEST,
                preferred_element_type=f32,
            )
            under = jnp.concatenate([row[0:1, :].astype(f32) for row in thirds(dots)] + [jnp.zeros((13, chunk), f32)], axis=0)
            out_refs[c][chunk:, :chunk] = under.astype(bf16)
            out_refs[c][chunk:, chunk:] = jnp.zeros((16, features - chunk), bf16)

    vmem = pl.BlockSpec(memory_space=pltpu.VMEM)
    return pl.pallas_call(
        kernel,
        out_shape=[jax.ShapeDtypeStruct((chunk + 16, features), bf16)] * count,
        in_specs=[SMEM_ARG] + [vmem] * (groups + reps + 2),
        out_specs=[vmem] * count,
        scratch_shapes=[pltpu.VMEM((count, chunk, features), f32)],
        compiler_params=params(24),
        cost_estimate=cost(2 * groups * rows * width * features, 2 * groups * rows * (width + features) + 4 * width * features),
        name="weight_product",
    )(rep, *columns, *values, weight, gain)


def returned_blocks(slots, weight, gain, micro, far):
    groups = len(slots)
    tokens, features = slots[0].shape
    counts = [micro if j == far else 1 for j in range(groups)]
    starts = [sum(counts[:j]) for j in range(groups)]
    parts = [tokens // n for n in counts for _ in range(n)]
    shard = weight.shape[0]
    tile = min(shard, 512)

    def kernel(*refs):
        slot_refs, weight_ref, gain_ref = refs[:groups], refs[groups], refs[groups + 1]
        out_refs = refs[groups + 2 :]
        factor = gain_ref[...].astype(f32)
        pair = 2 if groups % 2 == 0 else 1
        out_refs = [out_refs[at : at + n] for at, n in zip(starts, counts)]
        for j in range(0, groups, pair):
            values = jnp.concatenate([slot_refs[j + i][...] for i in range(pair)], axis=0)
            back = lax.dot_general(values, weight_ref[...], (((1,), (1,)), ((), ())), preferred_element_type=f32)
            back = (back * factor).astype(bf16)
            for i in range(pair):
                part = tokens // counts[j + i]
                for m in range(counts[j + i]):
                    at = i * tokens + m * part
                    out_refs[j + i][m][...] = back[at : at + part, :]

    outs = pl.pallas_call(
        kernel,
        grid=(shard // tile,),
        out_shape=[jax.ShapeDtypeStruct((part, shard), bf16) for part in parts],
        in_specs=[pl.BlockSpec((tokens, features), lambda i: (0, 0))] * groups
        + [pl.BlockSpec((tile, features), lambda i: (i, 0)), pl.BlockSpec((1, tile), lambda i: (0, i))],
        out_specs=[pl.BlockSpec((part, tile), lambda i: (0, i)) for part in parts],
        compiler_params=params(8),
        cost_estimate=cost(2 * groups * tokens * shard * features, 2 * groups * tokens * (shard + features) + 2 * shard * features),
        name="returned_blocks",
    )(*slots, weight, gain)
    return [list(outs[at : at + n]) for at, n in zip(starts, counts)]


def row_gradient(x, top, blocks, me, m):
    groups = len(blocks)
    shard = blocks[0].shape[1]
    rows = x.shape[2]
    width = shard * groups
    step = min(rows, 32)

    def block_spec(block):
        base = m * rows // step if block.shape[0] > rows else 0
        return pl.BlockSpec((step, shard), lambda i: (base + i, 0))

    def kernel(me_ref, x_ref, top_ref, *refs):
        block_refs, upper_ref, piece_ref = refs[:groups], refs[groups], refs[groups + 1]
        squares = jnp.zeros((step, 128), f32)
        dots = jnp.zeros((step, 128), f32)
        starts = [pl.multiple_of(lax.rem(me_ref[0] + j, groups) * shard, shard) for j in range(groups)]
        span = min(shard, 512)
        for j in range(groups):
            for c in range(0, shard, span):
                v = x_ref[0, 0, :, pl.ds(pl.multiple_of(starts[j] + c, span), span)].astype(f32)
                d = block_refs[j][:, c : c + span].astype(f32) * v
                v = v * v
                for k in range(0, span, 128):
                    squares = squares + v[:, k : k + 128]
                    dots = dots + d[:, k : k + 128]
        scale = lax.rsqrt(jnp.sum(squares, axis=1, keepdims=True) / width + norm_eps)
        mean = jnp.sum(dots, axis=1, keepdims=True) * scale / width
        slope = scale * mean
        for j in range(groups):
            for c in range(0, shard, span):
                at = pl.ds(pl.multiple_of(starts[j] + c, span), span)
                v = x_ref[0, 0, :, at].astype(f32)
                piece = (scale * (block_refs[j][:, c : c + span].astype(f32) - v * slope)).astype(bf16)
                piece_ref[:, at] = piece
                upper_ref[:, at] = (top_ref[0, :, at].astype(f32) + piece.astype(f32)).astype(bf16)

    return pl.pallas_call(
        kernel,
        grid=(rows // step,),
        out_shape=[jax.ShapeDtypeStruct((rows, width), bf16)] * 2,
        in_specs=[
            SMEM_ARG,
            pl.BlockSpec((1, 1, step, width), lambda i: (0, m, i, 0)),
            pl.BlockSpec((1, step, width), lambda i: (m, i, 0)),
        ]
        + [block_spec(block) for block in blocks],
        out_specs=[pl.BlockSpec((step, width), lambda i: (i, 0))] * 2,
        compiler_params=params(8),
        cost_estimate=cost(12 * rows * width, 10 * rows * width),
        name="row_gradient",
    )(me, x, top, *blocks)


def input_gradient(upper, piece, passed, is_upper, shape, m, earlier):
    rows, width = upper.shape
    step = min(rows, 64)

    def kernel(is_upper_ref, upper_ref, piece_ref, passed_ref, *refs):
        lower = (passed_ref[...].astype(f32) + piece_ref[...].astype(f32)).astype(bf16)
        refs[-1][0, 0] = jnp.where(is_upper_ref[0] == 1, upper_ref[...], lower)

    spec = pl.BlockSpec((step, width), lambda i: (i, 0))
    return pl.pallas_call(
        kernel,
        grid=(rows // step,),
        out_shape=jax.ShapeDtypeStruct(shape, bf16),
        in_specs=[SMEM_ARG, spec, spec, spec] + [ANY_ARG] * len(earlier),
        out_specs=pl.BlockSpec((1, 1, step, width), lambda i: (0, m, i, 0)),
        input_output_aliases={4: 0} if earlier else {},
        compiler_params=params(12),
        cost_estimate=cost(4 * rows * width, 8 * rows * width),
        name="input_gradient",
    )(is_upper, upper, piece, passed, *earlier)


def finished_half(sums, rep, order, half, c, chunks, earlier):
    pieces = (1 << len(order)) // 2
    rows = sums.shape[0] // pieces - 16
    features = sums.shape[1]
    shard = rows * chunks * pieces * 2

    def place(i, rep_ref):
        return (rep_ref[0] ^ mask_of(i + half * pieces, order)) * chunks + c

    def total(under):
        return under[0:1, :rows] + under[1:2, :rows] + under[2:3, :rows]

    if rows % 128:
        earlier = earlier or (jnp.zeros((shard, features), f32), jnp.zeros((1, shard), f32))
        for i in range(pieces):
            piece = sums[i * (rows + 16) : (i + 1) * (rows + 16)].astype(f32)
            at = place(i, rep) * rows
            earlier = (
                lax.dynamic_update_slice(earlier[0], piece[:rows], (at, 0)),
                lax.dynamic_update_slice(earlier[1], total(piece[rows:]), (0, at)),
            )
        return earlier

    def kernel(rep_ref, sum_ref, *refs):
        refs[-2][...] = sum_ref[:rows, :].astype(f32)
        refs[-1][...] = total(sum_ref[rows:, :].astype(f32))

    return pl.pallas_call(
        kernel,
        grid_spec=pltpu.PrefetchScalarGridSpec(
            num_scalar_prefetch=1,
            grid=(pieces,),
            in_specs=[pl.BlockSpec((rows + 16, features), lambda i, rep_ref: (i, 0))] + [ANY_ARG] * len(earlier),
            out_specs=[
                pl.BlockSpec((rows, features), lambda i, rep_ref: (place(i, rep_ref), 0)),
                pl.BlockSpec((1, rows), lambda i, rep_ref: (0, place(i, rep_ref))),
            ],
        ),
        out_shape=[jax.ShapeDtypeStruct((shard, features), f32), jax.ShapeDtypeStruct((1, shard), f32)],
        input_output_aliases={2: 0, 3: 1} if earlier else {},
        compiler_params=params(8),
        cost_estimate=cost(sums.size, 6 * sums.size),
        name="finished_half",
    )(rep, sums, *earlier)


def local(layer_input, value_grad, value_weight, norm_gain, top_grad):
    groups = lax.axis_size("fsdp")
    reps = lax.axis_size("rep")
    bits = reps.bit_length() - 1
    me = lax.axis_index("fsdp").astype(jnp.int32)[None]
    rep = lax.axis_index("rep").astype(jnp.int32)[None]
    _, micro, rows, width = layer_input.shape
    tokens = micro * rows
    norm_scale = float(tokens * reps * groups) ** (-0.5)
    chunks = 2
    orders = [tuple(range(bits)), tuple(reversed(range(bits)))]

    weight = value_weight[0]
    is_upper = lax.axis_index("section").astype(jnp.int32)[None]
    inputs = after(layer_input[0].reshape(tokens, width), me, rep, is_upper)

    hats = scaled_blocks(inputs, me, rep, groups, reps, 1)[0]
    plane = list(hats)
    for e in range(1, reps):
        plane[e] = flipped(hats[e], "rep", e)
    grads = after(value_grad[0].reshape(tokens, -1), hats[0])
    slots = [grads] + [cyclic(after(grads, plane[1]) if j == groups - 1 else grads, "fsdp", j) for j in range(1, groups)]

    plane[0] = after(plane[0], *slots[1:-1])
    sent = regrouped(plane, groups)
    far = groups // 2
    near = [j for j in range(1, groups) if j != far]
    back = returned_blocks(slots, weight, norm_gain, micro, far)
    columns = list(sent)
    columns[far] = cyclic(sent[far], "fsdp", far)
    columns[near[0]] = cyclic(sent[near[0]], "fsdp", near[0])
    for j in near[1:]:
        columns[j] = cyclic(after(sent[j], back[0][0], columns[near[0]]), "fsdp", j)
    held = after(joined(slots), sent[0])
    values = [held if e == 0 else flipped(held, "rep", e) for e in range(reps)]

    lines = [list(arrays) for arrays in back]

    def send_back(j, m, *ties):
        lines[j][m] = cyclic(after(lines[j][m], *ties), "fsdp", -j)

    send_back(far, 0, columns[far])
    send_back(near[-1], 0, columns[far])
    for j in near[:-1]:
        send_back(j, 0, lines[far][0])
    for m in range(1, micro):
        send_back(far, m, lines[far][m - 1])
    sums = weight_product(columns, values, weight, norm_gain, rep, groups, chunks, norm_scale)
    gathered = [doubled(sums[c], orders[c]) for c in range(chunks)]
    finished = ()
    for half in (0, 1):
        for c in range(chunks):
            finished = finished_half(gathered[c][half], rep, orders[c], half, c, chunks, finished)
        if half == 0:
            early = finished
    weight_grad, gain_grad = finished

    uppers = []
    for m in range(micro):
        line = [arrays[m if j == far else 0] for j, arrays in enumerate(lines)]
        line[0] = after(line[0], *([*early] if m else [*early]))
        line[0] = after(line[0], *[u for u, _ in uppers])
        uppers.append(row_gradient(layer_input, top_grad, line, me, m))
    result = ()
    for m, (upper, piece) in enumerate(uppers):
        passed = lax.ppermute(upper, "section", [(1, 0)])
        piece = after(piece, *finished)
        result = (input_gradient(upper, piece, passed, is_upper, layer_input.shape, m, result),)
    return (result[0], weight_grad[None], gain_grad)


def solution(mesh):
    return jax.shard_map(
        local,
        mesh=mesh,
        in_specs=(
            P("section", None, ("rep", "fsdp"), None),
            P("section", None, ("rep", "fsdp"), None),
            P("section", "fsdp", None),
            P("section", "fsdp"),
            P(None, ("rep", "fsdp"), None),
        ),
        out_specs=(
            P("section", None, ("rep", "fsdp"), None),
            P("section", "fsdp", None),
            P("section", "fsdp"),
        ),
        check_vma=False,
    )
```
